32 devices in a mesh: dp: 8 (over y, x, core), fsdp: 4 (over z).
Axes of the slice: x: 2, y: 2, z: 4, core: 2. Of those that a mesh axis runs over, the one named last changes fastest.
Arguments:
- frames: bfloat16 [64, 768, 512], P(('dp', 'fsdp')), may hold values from -6 to 6
- lengths: int32 [64], P(('dp', 'fsdp')), may hold values from 25 to 750, as said below
- ffn1_in: bfloat16 [512, 2048], P('dp', 'fsdp'), may hold values from -0.25 to 0.25
- ffn1_out: bfloat16 [2048, 512], P('dp', 'fsdp'), may hold values from -0.125 to 0.125
- ffn1_vec: bfloat16 [7, 512], P(None, 'fsdp')
- ssm_in: bfloat16 [512, 1024], P('dp', 'fsdp'), may hold values from -0.25 to 0.25
- ssm_out: bfloat16 [512, 512], P('dp', 'fsdp'), may hold values from -0.25 to 0.25
- ssm_vec: bfloat16 [3, 512], P(None, 'fsdp')
- decay: float32 [8, 32], replicated, may hold values from 0.05 to 2
- freq: float32 [8, 32], replicated, may hold values from 0 to 3
- coef_re: float32 [8, 32], replicated, may hold values from -6 to 6
- coef_im: float32 [8, 32], replicated, may hold values from -6 to 6
- conv_in: bfloat16 [512, 1024], P('dp', 'fsdp'), may hold values from -0.25 to 0.25
- conv_out: bfloat16 [512, 512], P('dp', 'fsdp'), may hold values from -0.25 to 0.25
- conv_vec: bfloat16 [17, 512], P(None, 'fsdp')
- ffn2_in: bfloat16 [512, 2048], P('dp', 'fsdp'), may hold values from -0.25 to 0.25
- ffn2_out: bfloat16 [2048, 512], P('dp', 'fsdp'), may hold values from -0.125 to 0.125
- ffn2_vec: bfloat16 [9, 512], P(None, 'fsdp')
- cotangent: bfloat16 [64, 768, 512], P(('dp', 'fsdp')), may hold values from -6 to 6
Outputs:
- output: bfloat16 [64, 768, 512], P(('dp', 'fsdp'))
- frames_grad: bfloat16 [64, 768, 512], P(('dp', 'fsdp'))
- ffn1_in_grad: float32 [512, 2048], P('dp', 'fsdp')
- ffn1_out_grad: float32 [2048, 512], P('dp', 'fsdp')
- ffn1_vec_grad: float32 [7, 512], P(None, 'fsdp')
- ssm_in_grad: float32 [512, 1024], P('dp', 'fsdp')
- ssm_out_grad: float32 [512, 512], P('dp', 'fsdp')
- ssm_vec_grad: float32 [3, 512], P(None, 'fsdp')
- decay_grad: float32 [8, 32], replicated
- freq_grad: float32 [8, 32], replicated
- coef_re_grad: float32 [8, 32], replicated
- coef_im_grad: float32 [8, 32], replicated
- conv_in_grad: float32 [512, 1024], P('dp', 'fsdp')
- conv_out_grad: float32 [512, 512], P('dp', 'fsdp')
- conv_vec_grad: float32 [17, 512], P(None, 'fsdp')
- ffn2_in_grad: float32 [512, 2048], P('dp', 'fsdp')
- ffn2_out_grad: float32 [2048, 512], P('dp', 'fsdp')
- ffn2_vec_grad: float32 [9, 512], P(None, 'fsdp')
The draws below stay inside these ranges and needn't reach their ends.
Inputs may be any that keep to these rules, and one draw needn't show every extreme that they name: `lengths`: real frames of each utterance; later frames are padding. Some utterance has exactly 750 and some exactly 25.
All inputs are finite; a program needn't handle non-finite values.
Results may differ from the reference program's by a relative error of at most 0.019.
Values may be sent and summed in bfloat16 or wider, within the bound.
A program may use at most 320 MiB of HBM per device.

```python
import math
import jax
import jax.numpy as jnp
from jax import lax

D = 512
FF = 2048
HEADS = 8
STATE = 32
CONV = 15
L = 768
LMIN = 25
LMAX = 750
UTTS = 64


def rows_block(key, layout):
    pieces = []
    for number, (count, center, spread) in enumerate(layout):
        noise = jax.random.normal(jax.random.fold_in(key, number), (count, D), jnp.float32)
        pieces.append(center + spread * noise)
    return jnp.concatenate(pieces, 0)


def draw_ffn1_vec(key, part):
    key = jax.random.fold_in(key, 11)
    layout = [(1, 1.0, 0.1), (1, 0.0, 0.2), (FF // D, 0.0, 0.3), (1, 0.0, 0.2)]
    return rows_block(key, layout).astype(jnp.bfloat16)


def draw_ssm_vec(key, part):
    key = jax.random.fold_in(key, 12)
    layout = [(1, 1.0, 0.1), (1, 0.0, 0.2), (1, 0.0, 0.5)]
    return rows_block(key, layout).astype(jnp.bfloat16)


def draw_conv_vec(key, part):
    key = jax.random.fold_in(key, 13)
    layout = [(1, 1.0, 0.1), (1, 0.0, 0.2), (CONV, 0.0, CONV ** (-0.5))]
    return rows_block(key, layout).astype(jnp.bfloat16)


def draw_ffn2_vec(key, part):
    key = jax.random.fold_in(key, 14)
    layout = [(1, 1.0, 0.1), (1, 0.0, 0.2), (FF // D, 0.0, 0.3), (1, 0.0, 0.2), (1, 1.0, 0.1), (1, 0.0, 0.3)]
    return rows_block(key, layout).astype(jnp.bfloat16)


def draw_lengths(key, part):
    key = jax.random.fold_in(key, 15)
    values = jax.random.randint(jax.random.fold_in(key, 1), (UTTS,), LMIN, LMAX + 1, dtype=jnp.int32)
    order = jax.random.permutation(jax.random.fold_in(key, 2), UTTS)
    values = values.at[order[0]].set(LMAX)
    return values.at[order[1]].set(LMIN)


def strengthened(drawn, own_key, source, target, shards_of, factor):
    def block_of(position):
        return (jnp.arange(drawn.shape[position]) // (drawn.shape[position] // shards_of)).reshape((-1,) + (1,) * (drawn.ndim - 1 - position))

    one_side = jax.random.permutation(own_key, shards_of)[block_of(target)]
    other_side = (block_of(target) + shards_of // 2) % shards_of
    return jnp.where((block_of(source) == one_side) | (block_of(source) == other_side), factor * drawn, drawn)


def steps_of(key, dims, cuts, low, top_value):
    loudness, own = 1.0, jax.random.fold_in(key, 6)
    for dim, blocks in cuts:
        draws = jnp.exp(jax.random.uniform(jax.random.fold_in(own, dim), (blocks,), jnp.float32, low / len(cuts), top_value / len(cuts)))
        loudness = loudness * jnp.repeat(draws, dims[dim] // blocks).reshape([-1 if axis == dim else 1 for axis in range(len(dims))])
    return loudness


def bell_draw(key, shape, scale, most, cuts=(), kind=jnp.bfloat16):
    values = scale * jax.random.normal(key, shape, jnp.float32)
    if cuts:
        values = values * steps_of(key, shape, cuts, -0.22, 0.18)
    return jnp.clip(values, -most, most).astype(kind)


def gaussian_with(stream_key, shape, width, reach, cuts, heavy, held_as=jnp.bfloat16):
    values = width * jax.random.normal(stream_key, shape, jnp.float32)
    if cuts:
        values = values * steps_of(stream_key, shape, cuts, -0.22, 0.18)
    return jnp.clip(strengthened(values, jax.random.fold_in(stream_key, 3), *heavy), -reach, reach).astype(held_as)


def setup_inputs(seed: int = 0) -> dict:
    seeds = jax.random.split(jax.random.key(seed), 20)
    frames = bell_draw(seeds[0], (UTTS, L, D), 1.0, 6.0, ((0, 32),))
    lengths = draw_lengths(jax.random.fold_in(seeds[19], 71), 0)
    ffn1_in = bell_draw(seeds[2], (D, FF), D ** -0.5, 0.25, ((0, 8), (1, 4)))
    ffn1_out = bell_draw(seeds[3], (FF, D), FF ** -0.5, 0.125, ((0, 8), (1, 4)))
    ffn1_vec = draw_ffn1_vec(jax.random.fold_in(seeds[19], 71), 0)
    ssm_in = bell_draw(seeds[5], (D, 2 * D), D ** -0.5, 0.25, ((0, 8), (1, 4)))
    ssm_out = bell_draw(seeds[6], (D, D), D ** -0.5, 0.25, ((0, 8), (1, 4)))
    ssm_vec = draw_ssm_vec(jax.random.fold_in(seeds[19], 71), 0)
    decay = jnp.clip(jnp.exp(jax.random.uniform(seeds[8], (HEADS, STATE), jnp.float32, math.log(0.05), math.log(2.0))), 0.05, 2.0)
    freq = jnp.clip(jax.random.uniform(seeds[9], (HEADS, STATE), jnp.float32, 0.0, 3.0), 0.0, 3.0)
    coef_re = bell_draw(seeds[10], (HEADS, STATE), 1.0, 6.0, (), jnp.float32)
    coef_im = bell_draw(seeds[11], (HEADS, STATE), 1.0, 6.0, (), jnp.float32)
    conv_in = bell_draw(seeds[12], (D, 2 * D), D ** -0.5, 0.25, ((0, 8), (1, 4)))
    conv_out = bell_draw(seeds[13], (D, D), D ** -0.5, 0.25, ((0, 8), (1, 4)))
    conv_vec = draw_conv_vec(jax.random.fold_in(seeds[19], 71), 0)
    ffn2_in = bell_draw(seeds[15], (D, FF), D ** -0.5, 0.25, ((0, 8), (1, 4)))
    ffn2_out = bell_draw(seeds[16], (FF, D), FF ** -0.5, 0.125, ((0, 8), (1, 4)))
    ffn2_vec = draw_ffn2_vec(jax.random.fold_in(seeds[19], 71), 0)
    cotangent = gaussian_with(seeds[18], (UTTS, L, D), 1.0, 6.0, ((0, 32),), (0, 2, 32, 2.75))
    return {"frames": frames, "lengths": lengths, "ffn1_in": ffn1_in, "ffn1_out": ffn1_out, "ffn1_vec": ffn1_vec, "ssm_in": ssm_in, "ssm_out": ssm_out, "ssm_vec": ssm_vec, "decay": decay, "freq": freq, "coef_re": coef_re, "coef_im": coef_im, "conv_in": conv_in, "conv_out": conv_out, "conv_vec": conv_vec, "ffn2_in": ffn2_in, "ffn2_out": ffn2_out, "ffn2_vec": ffn2_vec, "cotangent": cotangent}


EPSILON = 1e-05

@jax.custom_vjp
def low(v):
    return lax.optimization_barrier(v.astype(jnp.bfloat16)).astype(jnp.float32)

@jax.custom_vjp
def low_back(v):
    return v

def low_keep(v):
    return (low(v), None)

def low_pass(kept, grad):
    return (grad,)

def back_keep(v):
    return (v, None)

def back_low(kept, grad):
    return (low(grad),)
low.defvjp(low_keep, low_pass)
low_back.defvjp(back_keep, back_low)

def layer_norm(hidden, gain, shift):
    center = hidden - lax.optimization_barrier(jnp.mean(hidden, -1, keepdims=True))
    scale = lax.rsqrt(lax.optimization_barrier(jnp.mean(center * center, -1, keepdims=True)) + EPSILON)
    return center * scale * gain + shift

def dense(values, weight):
    return jnp.dot(values, weight, precision=lax.Precision.HIGHEST)

def ssm_kernel(decay, freq, coef_re, coef_im, length):
    heads = decay.shape[0]
    log_steps = -6.9 + 4.6 * jnp.arange(heads, dtype=jnp.float32) / (heads - 1)
    step = jnp.exp(log_steps)[:, None, None]
    places = jnp.arange(length, dtype=jnp.float32)
    damping = jnp.exp(-(step * decay[:, :, None]) * places)
    phase = step * freq[:, :, None] * places
    terms = damping * (coef_re[:, :, None] * jnp.cos(phase) - coef_im[:, :, None] * jnp.sin(phase))
    return lax.optimization_barrier(jnp.sum(terms, 1)) * jnp.sqrt(step[:, :, 0] / decay.shape[1])

def causal_mix(values, kernel):
    batch = values.shape[0]
    heads = kernel.shape[0]
    split = values.reshape(batch, L, heads, D // heads)
    spectrum = jnp.fft.rfft(split, n=2 * L, axis=1)
    response = jnp.fft.rfft(kernel, n=2 * L, axis=1).T[None, :, :, None]
    mixed = jnp.fft.irfft(spectrum * response, n=2 * L, axis=1)[:, :L]
    return mixed.reshape(batch, L, D)

def depthwise(values, taps):
    half = (CONV - 1) // 2
    padded = jnp.pad(values, ((0, 0), (half, half), (0, 0)))
    total = jnp.zeros_like(values)
    for offset in range(CONV):
        total = total + taps[offset] * padded[:, offset:offset + L]
    return total

def feed_forward(hidden, weight_in, weight_out, vectors):
    blocks = FF // D
    normal = low(layer_norm(hidden, vectors[0], vectors[1]))
    before = low_back(dense(normal, weight_in) + vectors[2:2 + blocks].reshape(FF))
    active = low(jax.nn.silu(before))
    return hidden + 0.5 * low_back(dense(active, weight_out) + vectors[2 + blocks])

def state_mixer(hidden, weight_in, weight_out, vectors, kernel):
    normal = low(layer_norm(hidden, vectors[0], vectors[1]))
    mixed = low_back(dense(normal, weight_in))
    value = low(mixed[..., :D])
    gate = mixed[..., D:]
    state = low_back(causal_mix(value, kernel)) + vectors[2] * value
    gated = low(state * jax.nn.silu(gate))
    return hidden + low_back(dense(gated, weight_out))

def conv_module(hidden, weight_in, weight_out, vectors, mask):
    normal = low(layer_norm(hidden, vectors[0], vectors[1]))
    mixed = low_back(dense(normal, weight_in))
    glu = mixed[..., :D] * jax.nn.sigmoid(mixed[..., D:]) * mask
    active = low(jax.nn.silu(depthwise(glu, vectors[2:])))
    return hidden + low_back(dense(active, weight_out))

def layer(values, weights, mask):
    ffn1_in, ffn1_out, ffn1_vec, ssm_in, ssm_out, ssm_vec, decay, freq, coef_re, coef_im, conv_in, conv_out, conv_vec, ffn2_in, ffn2_out, ffn2_vec = weights
    blocks = FF // D
    kernel = low(ssm_kernel(decay, freq, coef_re, coef_im, L))
    hidden = feed_forward(values, ffn1_in, ffn1_out, ffn1_vec)
    hidden = state_mixer(hidden, ssm_in, ssm_out, ssm_vec, kernel)
    hidden = conv_module(hidden, conv_in, conv_out, conv_vec, mask)
    hidden = feed_forward(hidden, ffn2_in, ffn2_out, ffn2_vec)
    return mask * layer_norm(hidden, ffn2_vec[3 + blocks], ffn2_vec[4 + blocks])

def reference(frames, lengths, ffn1_in, ffn1_out, ffn1_vec, ssm_in, ssm_out, ssm_vec, decay, freq, coef_re, coef_im, conv_in, conv_out, conv_vec, ffn2_in, ffn2_out, ffn2_vec, cotangent):
    weights = (ffn1_in, ffn1_out, ffn1_vec, ssm_in, ssm_out, ssm_vec, decay, freq, coef_re, coef_im, conv_in, conv_out, conv_vec, ffn2_in, ffn2_out, ffn2_vec)
    weights = tuple((weight.astype(jnp.float32) for weight in weights))
    groups = UTTS // 4
    inputs = (frames.reshape(groups, 4, L, D), lengths.reshape(groups, 4), cotangent.reshape(groups, 4, L, D))

    def one_group(totals, block):
        block_frames, block_lengths, block_cot = block
        places = jnp.arange(L, dtype=jnp.int32)
        mask = (places[None, :] < block_lengths[:, None]).astype(jnp.float32)[:, :, None]

        def forward(values, params):
            return layer(values, params, mask)
        result, pull = jax.vjp(forward, block_frames.astype(jnp.float32), weights)
        grad_frames, grad_weights = pull(block_cot.astype(jnp.float32))
        totals = jax.tree.map(jnp.add, totals, grad_weights)
        return (totals, (result.astype(jnp.bfloat16), grad_frames.astype(jnp.bfloat16)))
    zeros = jax.tree.map(jnp.zeros_like, weights)
    totals, (results, grads) = lax.scan(one_group, zeros, inputs)
    return (results.reshape(UTTS, L, D), grads.reshape(UTTS, L, D), totals[0], totals[1], totals[2], totals[3], totals[4], totals[5], totals[6], totals[7], totals[8], totals[9], totals[10], totals[11], totals[12], totals[13], totals[14], totals[15])
```

```python
from functools import partial

import jax
import jax.numpy as jnp
from jax import lax
from jax.experimental import pallas as pl
from jax.experimental.pallas import tpu as pltpu
from jax.sharding import PartitionSpec as P

EPSILON = 1e-05
VMEM_BYTES = 60 * 2**20
LANES = 128
TILE = 256
EDGE = 8
F1, SS, CV, F2 = (0, 8, 16, 40)
TABLE = 56
f32 = jnp.float32
bf16 = jnp.bfloat16


def dot(left, right):
    return jnp.dot(left, right, preferred_element_type=f32)


def dot_nt(left, right):
    return lax.dot_general(left, right, (((1,), (1,)), ((), ())), preferred_element_type=f32)


def dot_tn(left, right):
    return lax.dot_general(left, right, (((0,), (0,)), ((), ())), preferred_element_type=f32)


def loop(number, step):
    def turn(index, carry):
        step(index)
        return carry

    lax.fori_loop(0, number, turn, 0)


def at(index, size):
    return pl.ds(pl.multiple_of(index * size, size), size)


def norm(hidden):
    center = hidden - jnp.mean(hidden, -1, keepdims=True)
    scale = lax.rsqrt(jnp.mean(center * center, -1, keepdims=True) + EPSILON)
    return (center * scale, scale)


def norm_back(grad, normed, scale, gain):
    scaled = grad * gain
    centered = (
        scaled
        - jnp.mean(scaled, -1, keepdims=True)
        - normed * jnp.mean(scaled * normed, -1, keepdims=True)
    )
    return (
        scale * centered,
        jnp.sum(grad * normed, 0, keepdims=True),
        jnp.sum(grad, 0, keepdims=True),
    )


def frame_mask(length, valid):
    return (lax.broadcasted_iota(jnp.int32, (length, 1), 0) < valid).astype(f32)


def identity(size):
    return lax.broadcasted_iota(jnp.int32, (size, size), 0) == lax.broadcasted_iota(
        jnp.int32, (size, size), 1
    )


def state_column(values):
    heads, states = values.shape
    eye = identity(states)
    columns = [
        jnp.sum(
            jnp.where(eye, jnp.broadcast_to(values[h : h + 1, :], (states, states)), 0.0),
            1,
            keepdims=True,
        )
        for h in range(heads)
    ]
    return jnp.concatenate(columns, 0)


def state_rows(column, heads):
    states = column.shape[0] // heads
    eye = identity(states)
    rows = [
        jnp.sum(
            jnp.where(
                eye,
                jnp.broadcast_to(column[h * states : (h + 1) * states, :], (states, states)),
                0.0,
            ),
            0,
            keepdims=True,
        )
        for h in range(heads)
    ]
    return jnp.concatenate(rows, 0)


def head_steps(heads, states):
    row = lax.broadcasted_iota(jnp.int32, (heads * states, 1), 0)
    log_steps = jnp.full((heads * states, 1), -6.9, f32)
    for h in range(1, heads):
        log_steps = jnp.where(row >= h * states, -6.9 + 4.6 * h / (heads - 1), log_steps)
    return jnp.exp(log_steps)


def state_powers(decay, freq, step, stride):
    places = lax.broadcasted_iota(jnp.int32, (1, LANES), 1).astype(f32) * float(stride)
    damping = jnp.exp(-(step * decay) * places)
    phase = (step * freq) * places
    return (damping * jnp.cos(phase), damping * jnp.sin(phase))


def build_bands(decay_ref, freq_ref, re_ref, im_ref, powers, wide, wide_t, length):
    heads, states = decay_ref.shape
    step = head_steps(heads, states)
    decay, freq = (state_column(decay_ref[...]), state_column(freq_ref[...]))
    real, imag = (state_column(re_ref[...]), state_column(im_ref[...]))
    near_re, near_im = state_powers(decay, freq, step, 1)
    far_re, far_im = state_powers(decay, freq, step, LANES)
    powers[0], powers[1], powers[2], powers[3] = (near_re, near_im, far_re, far_im)
    lead_re = real * far_re - imag * far_im
    lead_im = real * far_im + imag * far_re
    blocks = length // LANES
    pieces = []
    for a in range(blocks):
        term = lead_re[:, a : a + 1] * near_re - lead_im[:, a : a + 1] * near_im
        pieces.append(jnp.sum(term.reshape(heads, states, LANES), 1))
    root = jnp.sqrt(step / states)
    factor = jnp.concatenate([root[h * states : h * states + 1, :] for h in range(heads)], 0)
    low = [(piece * factor).astype(bf16) for piece in pieces]
    turn = (
        lax.broadcasted_iota(jnp.int32, (LANES, LANES), 0)
        + lax.broadcasted_iota(jnp.int32, (LANES, LANES), 1)
        == LANES - 1
    ).astype(bf16)
    ring = length + TILE
    zeros = jnp.zeros((heads, TILE), f32)
    forward = jnp.concatenate([piece.astype(f32) for piece in low] + [zeros], 1)
    backward = jnp.concatenate([dot(piece, turn) for piece in low[::-1]] + [zeros], 1)
    backward = pltpu.roll(backward, ring - (TILE - 1), 1)
    for source, band in ((backward, wide), (forward, wide_t)):
        for h in range(heads):
            row = jnp.broadcast_to(source[h : h + 1, :], (8, ring))
            base = pltpu.roll(row, 0, 1, stride=1, stride_axis=0)
            for g in range(0, LANES // 8, 2):
                pair = jnp.concatenate(
                    [pltpu.roll(base, 8 * g, 1), pltpu.roll(base, 8 * g + 8, 1)], 0
                )
                for q in range(TILE // LANES):
                    if q == 0:
                        cut = pair[:, :length]
                    else:
                        cut = jnp.concatenate(
                            [pair[:, ring - q * LANES :], pair[:, : length - q * LANES]], 1
                        )
                    place = (h % 2) * TILE + q * LANES + 8 * g
                    band[h // 2, place : place + 16, :] = cut.astype(bf16)


def state_grads(kernel_grad, powers, decay_ref, re_ref, im_ref, out):
    heads, states = decay_ref.shape
    step = head_steps(heads, states)
    real, imag = (state_column(re_ref[...]), state_column(im_ref[...]))
    near_re, near_im, far_re, far_im = (powers[0], powers[1], powers[2], powers[3])
    length = kernel_grad.shape[1]
    zero_re = zero_im = one_re = one_im = None
    for a in range(length // LANES):
        block = kernel_grad[:, a * LANES : (a + 1) * LANES]
        spread = jnp.concatenate(
            [jnp.broadcast_to(block[h : h + 1, :], (states, LANES)) for h in range(heads)], 0
        )
        term_re, term_im = (far_re[:, a : a + 1] * spread, far_im[:, a : a + 1] * spread)
        if a == 0:
            zero_re, zero_im = (term_re, term_im)
            one_re, one_im = (jnp.zeros_like(term_re), jnp.zeros_like(term_im))
        else:
            zero_re, zero_im = (zero_re + term_re, zero_im + term_im)
            one_re, one_im = (one_re + a * LANES * term_re, one_im + a * LANES * term_im)
    places = lax.broadcasted_iota(jnp.int32, (1, LANES), 1).astype(f32)
    one_re, one_im = (one_re + places * zero_re, one_im + places * zero_im)

    def close(left_re, left_im):
        return (
            jnp.sum(near_re * left_re - near_im * left_im, 1, keepdims=True),
            jnp.sum(near_re * left_im + near_im * left_re, 1, keepdims=True),
        )

    plain_re, plain_im = close(zero_re, zero_im)
    place_re, place_im = close(one_re, one_im)
    scale = jnp.sqrt(step / states)
    columns = (
        -step * scale * (real * place_re - imag * place_im),
        -step * scale * (real * place_im + imag * place_re),
        scale * plain_re,
        -scale * plain_im,
    )
    out[...] = jnp.zeros_like(out)
    for number, column in enumerate(columns):
        out[number * heads : (number + 1) * heads, :states] = state_rows(column, heads)


def feed_forward(normal, weight_in, weight_out, table, base, before, rows):
    width = normal.shape[1]
    total = None
    for c in range(weight_in.shape[1] // width):
        part = slice(c * width, (c + 1) * width)
        value = dot(normal, weight_in[:, part]) + table[base + 2 + c : base + 3 + c, :]
        before[rows, part] = value.astype(bf16)
        active = (value * jax.nn.sigmoid(value)).astype(bf16)
        term = dot(active, weight_out[part, :])
        total = term if total is None else total + term
    return total


def ffn1_forward(count, frames, table, weight_in, weight_out, hidden, before):
    length = frames.shape[0] // count
    blocks = weight_in.shape[1] // weight_in.shape[0]

    def step(u):
        rows = at(u, length)
        value = frames[rows, :].astype(f32)
        normed, _ = norm(value)
        normal = (normed * table[F1 : F1 + 1, :] + table[F1 + 1 : F1 + 2, :]).astype(bf16)
        total = feed_forward(normal, weight_in, weight_out, table, F1, before, rows)
        bias = table[F1 + 2 + blocks : F1 + 3 + blocks, :]
        hidden[rows, :] = value + 0.5 * (total + bias)

    loop(count, step)


def head_lanes():
    return lax.broadcasted_iota(jnp.int32, (1, 2 * LANES), 1) % LANES < LANES // 2


def ssm_forward(
    count, hidden, table, weight_in, weight_out, wide, normed_ref, scale_ref, value_ref, gate_ref,
    state_ref, gated,
):
    total_rows, width = hidden.shape
    length = total_rows // count
    tiles = width // LANES

    def enter(u):
        rows = at(u, length)
        lanes = at(u, LANES)
        normed, scale = norm(hidden[rows, :])
        normed_ref[rows, :] = normed.astype(bf16)
        scale_ref[rows, :] = scale
        normal = (normed * table[SS : SS + 1, :] + table[SS + 1 : SS + 2, :]).astype(bf16)
        value = dot(normal, weight_in[:, :width]).astype(bf16)
        gate = dot(normal, weight_in[:, width:]).astype(bf16)
        for j in range(tiles):
            part = slice(j * LANES, (j + 1) * LANES)
            value_ref[j, :, lanes] = value[:, part]
            gate_ref[j, :, lanes] = gate[:, part]

    loop(count, enter)
    first = head_lanes()
    steps = length // TILE
    for j in range(tiles):
        part = slice(j * LANES, (j + 1) * LANES)
        skip = table[SS + 2 : SS + 3, part]
        skip = jnp.concatenate([skip, skip], 1)
        for i in range(steps):
            rows = slice(i * TILE, (i + 1) * TILE)
            both = dot(wide[j, :, (steps - 1 - i) * TILE :], value_ref[j, : (i + 1) * TILE, :])
            mixed = jnp.where(first, both[:TILE], both[TILE:])
            gate = gate_ref[j, rows, :].astype(f32)
            state = mixed + skip * value_ref[j, rows, :].astype(f32)
            state_ref[j, rows, :] = state.astype(bf16)
            out = (state * (gate * jax.nn.sigmoid(gate))).astype(bf16)
            for u in range(count):
                gated[u * length + i * TILE : u * length + (i + 1) * TILE, part] = out[
                    :, u * LANES : (u + 1) * LANES
                ]

    def leave(u):
        rows = at(u, length)
        hidden[rows, :] += dot(gated[rows, :], weight_out[...])

    loop(count, leave)


def clear_edges(padded, length):
    number, _, lanes = padded.shape
    zeros = jnp.zeros((number, EDGE, lanes), f32)
    padded[:, :EDGE, :] = zeros
    padded[:, EDGE + length :, :] = zeros


ROWS = 96


def conv_forward(
    count, hidden, lengths, table, weight_in, weight_out, normed_ref, scale_ref, linear_ref,
    gate_ref, depth_ref, glu, active,
):
    total_rows, width = hidden.shape
    length = total_rows // count
    tiles = width // LANES
    clear_edges(glu, length)

    def enter(u):
        rows = at(u, length)
        normed, scale = norm(hidden[rows, :])
        normed_ref[rows, :] = normed.astype(bf16)
        scale_ref[rows, :] = scale
        normal = (normed * table[CV : CV + 1, :] + table[CV + 1 : CV + 2, :]).astype(bf16)
        linear = dot(normal, weight_in[:, :width])
        gate = jax.nn.sigmoid(dot(normal, weight_in[:, width:]))
        linear_ref[rows, :] = linear.astype(bf16)
        gate_ref[rows, :] = gate.astype(bf16)
        value = linear * gate * frame_mask(length, lengths[u])
        for j in range(tiles):
            glu[u * tiles + j, EDGE : EDGE + length, :] = value[:, j * LANES : (j + 1) * LANES]

    loop(count, enter)
    number = CONV_TAPS

    def convolve(index):
        u, j = (index // tiles, index % tiles)
        lanes = at(j, LANES)
        taps = [table[CV + 2 + t : CV + 3 + t, lanes] for t in range(number)]
        for begin in range(0, length, ROWS):
            total = None
            for t in range(number):
                shifted = EDGE + begin + t - number // 2
                term = taps[t] * glu[index, shifted : shifted + ROWS, :]
                total = term if total is None else total + term
            rows = pl.ds(pl.multiple_of(u * length + begin, 32), ROWS)
            depth_ref[rows, lanes] = total.astype(bf16)
            active[rows, lanes] = (total * jax.nn.sigmoid(total)).astype(bf16)

    loop(count * tiles, convolve)

    def leave(u):
        rows = at(u, length)
        hidden[rows, :] += dot(active[rows, :], weight_out[...])

    loop(count, leave)


CONV_TAPS = 15


def ffn_backward(
    count, weight_in, weight_out, before, branch, normal, back, grad_in, grad_out, vec_grad,
    before_grad, active,
):
    total_rows, width = branch.shape
    length = total_rows // count
    back[...] = jnp.zeros_like(back)

    def chunk(c):
        part = at(c, width)

        def step(u):
            rows = at(u, length)
            grad = dot_nt(branch[rows, :], weight_out[part, :])
            value = before[rows, part].astype(f32)
            sig = jax.nn.sigmoid(value)
            active[rows, :] = (value * sig).astype(bf16)
            low = (grad * (sig * (1.0 + value * (1.0 - sig)))).astype(bf16)
            before_grad[rows, :] = low
            vec_grad[pl.ds(2 + c, 1), :] += jnp.sum(low.astype(f32), 0, keepdims=True)
            back[rows, :] += dot_nt(low, weight_in[:, part])

        loop(count, step)
        grad_in[:, part] = dot_tn(normal[...], before_grad[...]).astype(bf16)
        grad_out[part, :] = dot_tn(active[...], branch[...]).astype(bf16)

    loop(weight_in.shape[1] // width, chunk)


def ffn2_both(
    count, hidden, cotangent, lengths, table, weight_in, weight_out, output, grad, grad_in,
    grad_out, vec_grad, normed_ref, scale_ref, before, normal_ref, branch, before_grad, active,
    back,
):
    total_rows, width = hidden.shape
    length = total_rows // count
    blocks = weight_in.shape[1] // width
    vec_grad[...] = jnp.zeros_like(vec_grad)
    last = 3 + blocks

    def forward(u):
        rows = at(u, length)
        value = hidden[rows, :]
        normed, scale = norm(value)
        normed_ref[rows, :] = normed.astype(bf16)
        scale_ref[rows, :] = scale
        normal = (normed * table[F2 : F2 + 1, :] + table[F2 + 1 : F2 + 2, :]).astype(bf16)
        normal_ref[rows, :] = normal
        total = feed_forward(normal, weight_in, weight_out, table, F2, before, rows)
        value = value + 0.5 * (total + table[F2 + 2 + blocks : F2 + 3 + blocks, :])
        normed, scale = norm(value)
        gain = table[F2 + last : F2 + last + 1, :]
        mask = frame_mask(length, lengths[u])
        shift = table[F2 + last + 1 : F2 + last + 2, :]
        output[rows, :] = ((normed * gain + shift) * mask).astype(bf16)
        grad_in, gain_grad, shift_grad = norm_back(
            cotangent[rows, :].astype(f32) * mask, normed, scale, gain
        )
        vec_grad[last : last + 1, :] += gain_grad
        vec_grad[last + 1 : last + 2, :] += shift_grad
        grad[rows, :] = grad_in
        low = (0.5 * grad_in).astype(bf16)
        branch[rows, :] = low
        vec_grad[last - 1 : last, :] += jnp.sum(low.astype(f32), 0, keepdims=True)

    loop(count, forward)
    ffn_backward(
        count, weight_in, weight_out, before, branch, normal_ref, back, grad_in, grad_out,
        vec_grad, before_grad, active,
    )

    def leave(u):
        rows = at(u, length)
        grad_in, gain_grad, shift_grad = norm_back(
            back[rows, :], normed_ref[rows, :].astype(f32), scale_ref[rows, :],
            table[F2 : F2 + 1, :],
        )
        grad[rows, :] += grad_in
        vec_grad[0:1, :] += gain_grad
        vec_grad[1:2, :] += shift_grad

    loop(count, leave)


def conv_backward(
    count, lengths, table, weight_in, weight_out, normed_ref, scale_ref, linear_ref, gate_ref,
    depth_ref, grad, grad_in, grad_out, vec_grad, normal_ref, branch, active, depth_grad, glu,
    mixed_grad,
):
    total_rows, width = grad.shape
    length = total_rows // count
    tiles = width // LANES
    number = CONV_TAPS
    vec_grad[...] = jnp.zeros_like(vec_grad)
    clear_edges(glu, length)
    clear_edges(depth_grad, length)

    def enter(u):
        rows = at(u, length)
        low = grad[rows, :].astype(bf16)
        branch[rows, :] = low
        normed = normed_ref[rows, :].astype(f32)
        normal = (normed * table[CV : CV + 1, :] + table[CV + 1 : CV + 2, :]).astype(bf16)
        normal_ref[rows, :] = normal
        active_grad = dot_nt(low, weight_out[...])
        depth = depth_ref[rows, :].astype(f32)
        sig = jax.nn.sigmoid(depth)
        active[rows, :] = (depth * sig).astype(bf16)
        slope = active_grad * (sig * (1.0 + depth * (1.0 - sig)))
        value = (
            linear_ref[rows, :].astype(f32)
            * gate_ref[rows, :].astype(f32)
            * frame_mask(length, lengths[u])
        )
        for j in range(tiles):
            part = slice(j * LANES, (j + 1) * LANES)
            depth_grad[u * tiles + j, EDGE : EDGE + length, :] = slope[:, part]
            glu[u * tiles + j, EDGE : EDGE + length, :] = value[:, part]

    loop(count, enter)

    def convolve(index):
        u, j = (index // tiles, index % tiles)
        lanes = at(j, LANES)
        second = pl.ds(pl.multiple_of(width + j * LANES, LANES), LANES)
        taps = [table[CV + 2 + t : CV + 3 + t, lanes] for t in range(number)]
        sums = [None] * number
        for begin in range(0, length, ROWS):
            total = None
            here = depth_grad[index, EDGE + begin : EDGE + begin + ROWS, :]
            for t in range(number):
                shifted = EDGE + begin + number // 2 - t
                term = taps[t] * depth_grad[index, shifted : shifted + ROWS, :]
                total = term if total is None else total + term
                shifted = EDGE + begin + t - number // 2
                pairs = here * glu[index, shifted : shifted + ROWS, :]
                pairs = jnp.sum(pairs.reshape(ROWS // 8, 8, LANES), 0)
                sums[t] = pairs if sums[t] is None else sums[t] + pairs
            rows = pl.ds(pl.multiple_of(u * length + begin, 32), ROWS)
            places = begin + lax.broadcasted_iota(jnp.int32, (ROWS, 1), 0)
            total = total * (places < lengths[u]).astype(f32)
            linear = linear_ref[rows, lanes].astype(f32)
            gate = gate_ref[rows, lanes].astype(f32)
            gated = total * gate
            mixed_grad[rows, lanes] = gated.astype(bf16)
            mixed_grad[rows, second] = (gated * linear * (1.0 - gate)).astype(bf16)
        for t in range(number):
            vec_grad[2 + t : 3 + t, lanes] += jnp.sum(sums[t], 0, keepdims=True)

    loop(count * tiles, convolve)
    grad_in[...] = dot_tn(normal_ref[...], mixed_grad[...]).astype(bf16)
    grad_out[...] = dot_tn(active[...], branch[...]).astype(bf16)
    mixer_leave(count, table, CV, weight_in, normed_ref, scale_ref, grad, vec_grad, mixed_grad)


def mixer_leave(count, table, base, weight_in, normed_ref, scale_ref, grad, vec_grad, mixed_grad):
    length = grad.shape[0] // count

    def leave(u):
        rows = at(u, length)
        back = dot_nt(mixed_grad[rows, :], weight_in[...])
        grad_in, gain_grad, shift_grad = norm_back(
            back, normed_ref[rows, :].astype(f32), scale_ref[rows, :], table[base : base + 1, :]
        )
        grad[rows, :] += grad_in
        vec_grad[0:1, :] += gain_grad
        vec_grad[1:2, :] += shift_grad

    loop(count, leave)


def diagonal_sums(block):
    size = block.shape[0]
    zeros = jnp.zeros((8, size), f32)
    total = None
    for g in range(size // 8):
        rows = jnp.concatenate([block[8 * g : 8 * g + 8, :], zeros], 1)
        if g:
            rows = pltpu.roll(rows, 2 * size - 8 * g, 1)
        total = rows if total is None else total + rows
    out = total[0:1, :]
    for i in range(1, 8):
        out = out + pltpu.roll(total, 2 * size - i, 1)[i : i + 1, :]
    return out


def ssm_backward(
    count, table, weight_in, weight_out, wide_t, powers, decay_ref, re_ref, im_ref, normed_ref,
    scale_ref, value_ref, gate_ref, state_ref, grad, grad_in, grad_out, vec_grad, state_out,
    normal_ref, branch, time_grad, gated, mixed_grad,
):
    total_rows, width = grad.shape
    length = total_rows // count
    tiles = width // LANES
    steps = length // TILE
    vec_grad[...] = jnp.zeros_like(vec_grad)

    def enter(u):
        rows = at(u, length)
        lanes = at(u, LANES)
        low = grad[rows, :].astype(bf16)
        branch[rows, :] = low
        normed = normed_ref[rows, :].astype(f32)
        normal = (normed * table[SS : SS + 1, :] + table[SS + 1 : SS + 2, :]).astype(bf16)
        normal_ref[rows, :] = normal
        gated_grad = dot_nt(low, weight_out[...])
        for j in range(tiles):
            part = slice(j * LANES, (j + 1) * LANES)
            second = slice(width + j * LANES, width + (j + 1) * LANES)
            gate = gate_ref[j, :, lanes].astype(f32)
            state = state_ref[j, :, lanes].astype(f32)
            sig = jax.nn.sigmoid(gate)
            swish = gate * sig
            here = gated_grad[:, part]
            state_grad = here * swish
            time_grad[j, :, lanes] = state_grad.astype(bf16)
            gated[rows, part] = (state * swish).astype(bf16)
            mixed_grad[rows, second] = (
                here * state * (sig * (1.0 + gate * (1.0 - sig)))
            ).astype(bf16)
            vec_grad[2:3, part] += jnp.sum(
                state_grad * value_ref[j, :, lanes].astype(f32), 0, keepdims=True
            )

    loop(count, enter)
    first = head_lanes()
    kernel_rows = []
    for j in range(tiles):
        part = slice(j * LANES, (j + 1) * LANES)
        skip = table[SS + 2 : SS + 3, part]
        skip = jnp.concatenate([skip, skip], 1)
        sums = [[None] * steps for _ in range(2)]
        for i in range(steps):
            rows = slice(i * TILE, (i + 1) * TILE)
            both = dot(wide_t[j, :, : length - i * TILE], time_grad[j, i * TILE :, :])
            back = jnp.where(first, both[:TILE], both[TILE:])
            back = (back + skip * time_grad[j, rows, :].astype(f32)).astype(bf16)
            for u in range(count):
                mixed_grad[u * length + i * TILE : u * length + (i + 1) * TILE, part] = back[
                    :, u * LANES : (u + 1) * LANES
                ]
        for d in range(steps):
            total = None
            for i in range(steps - d):
                value = value_ref[j, i * TILE : (i + 1) * TILE, :]
                split = jnp.concatenate(
                    [jnp.where(first, value, 0), jnp.where(first, 0, value)], 0
                ).astype(bf16)
                term = dot_nt(split, time_grad[j, (i + d) * TILE : (i + d + 1) * TILE, :])
                total = term if total is None else total + term
            for e in range(2):
                sums[e][d] = diagonal_sums(total[e * TILE : (e + 1) * TILE, :])
        for e in range(2):
            pieces = []
            for d in range(steps):
                piece = sums[e][d][:, :TILE]
                if d + 1 < steps:
                    piece = piece + sums[e][d + 1][:, TILE:]
                pieces.append(piece)
            kernel_rows.append(jnp.concatenate(pieces, 1))
    state_grads(jnp.concatenate(kernel_rows, 0), powers, decay_ref, re_ref, im_ref, state_out)
    grad_in[...] = dot_tn(normal_ref[...], mixed_grad[...]).astype(bf16)
    grad_out[...] = dot_tn(gated[...], branch[...]).astype(bf16)
    mixer_leave(count, table, SS, weight_in, normed_ref, scale_ref, grad, vec_grad, mixed_grad)


def ffn1_backward(
    count, frames, grad, table, weight_in, weight_out, before, frames_grad, grad_in, grad_out,
    vec_grad, normal_ref, branch, before_grad, active, back,
):
    total_rows, width = frames.shape
    length = total_rows // count
    blocks = weight_in.shape[1] // width
    vec_grad[...] = jnp.zeros_like(vec_grad)

    def enter(u):
        rows = at(u, length)
        normed, _ = norm(frames[rows, :].astype(f32))
        normal = (normed * table[F1 : F1 + 1, :] + table[F1 + 1 : F1 + 2, :]).astype(bf16)
        normal_ref[rows, :] = normal
        low = (0.5 * grad[rows, :]).astype(bf16)
        branch[rows, :] = low
        vec_grad[2 + blocks : 3 + blocks, :] += jnp.sum(low.astype(f32), 0, keepdims=True)

    loop(count, enter)
    ffn_backward(
        count, weight_in, weight_out, before, branch, normal_ref, back, grad_in, grad_out,
        vec_grad, before_grad, active,
    )

    def leave(u):
        rows = at(u, length)
        normed, scale = norm(frames[rows, :].astype(f32))
        grad_in, gain_grad, shift_grad = norm_back(
            back[rows, :], normed, scale, table[F1 : F1 + 1, :]
        )
        frames_grad[rows, :] = (grad[rows, :] + grad_in).astype(bf16)
        vec_grad[0:1, :] += gain_grad
        vec_grad[1:2, :] += shift_grad

    loop(count, leave)


def shape(dims, kind):
    return jax.ShapeDtypeStruct(dims, kind)


def call(kernel, outs, scratch, smem, *operands):
    whole = pl.BlockSpec(memory_space=pltpu.VMEM)
    scalars = pl.BlockSpec(memory_space=pltpu.SMEM)
    return pl.pallas_call(
        kernel,
        out_shape=outs,
        in_specs=[scalars if n in smem else whole for n in range(len(operands))],
        out_specs=[whole] * len(outs),
        scratch_shapes=[pltpu.VMEM(s.shape, s.dtype) for s in scratch],
        compiler_params=pltpu.CompilerParams(vmem_limit_bytes=VMEM_BYTES),
    )(*operands)


def bring(weight_in, weight_out):
    first, second = (
        lax.all_gather(weight_in, "fsdp", axis=1, tiled=True),
        lax.all_gather(weight_out, "fsdp", axis=1, tiled=True),
    )
    return (
        lax.all_gather(first, "dp", axis=0, tiled=True),
        lax.all_gather(second, "dp", axis=0, tiled=True),
    )


def send(grad):
    part = lax.psum_scatter(grad, "fsdp", scatter_dimension=1, tiled=True)
    return lax.psum_scatter(part, "dp", scatter_dimension=0, tiled=True).astype(f32)


class Place:
    def __init__(self):
        me, z = (lax.axis_index("dp"), lax.axis_index("fsdp"))
        y, x, core = (me // 4, me // 2 % 2, me % 2)
        self.me, self.z, self.depth, self.layers = (me, z, 8, 4)
        self.across = me + 2 - 4 * x
        self.along = me + 4 - 8 * y
        self.corner = me + 6 - 4 * x - 8 * y
        self.twin = me + 1 - 2 * core
        self.mates = (me, self.across, self.along, self.corner)
        turn = 1 - 2 * core
        self.twin_mates = tuple(mate + turn for mate in self.mates)

    def above(self, offset):
        return (self.z + offset) % self.layers

    def greet(self, everyone):
        barrier = pltpu.get_barrier_semaphore()
        others = [(self.me, self.above(o)) for o in range(1, self.layers)]
        if everyone:
            others += [((self.me + o) % self.depth, self.z) for o in range(1, self.depth)]
        else:
            others += [(mate, self.z) for mate in (self.across, self.along, self.twin)]
        for other in others:
            pl.semaphore_signal(
                barrier, inc=1, device_id=other, device_id_type=pl.DeviceIdType.MESH
            )
        pl.semaphore_wait(barrier, len(others))


def copy_to(source, target, sems, slot, device):
    copy = pltpu.make_async_remote_copy(
        src_ref=source,
        dst_ref=target,
        send_sem=sems.at[0, slot],
        recv_sem=sems.at[1, slot],
        device_id=device,
        device_id_type=pl.DeviceIdType.MESH,
    )
    copy.start()
    return copy


GATHER_SLOTS = 12


def gather_steps(spot, shard, whole, sems):
    rows, columns = shard.shape
    copies = {}

    def line(owner, begin=0, number=rows):
        return whole.at[pl.ds(pl.multiple_of(owner * rows + begin, 16), number), :]

    def start(name, source, target, device):
        copies[name] = copy_to(source, target, sems, len(copies), device)

    def send_up():
        spot_rows, spot_columns = (at(spot.me, rows), at(spot.z, columns))
        own = whole.at[spot_rows, spot_columns]
        for o in range(1, spot.layers):
            start(("z", o), shard, own, (spot.me, spot.above(o)))
        whole[spot_rows, spot_columns] = shard[...]

    def send_line():
        for o in range(1, spot.layers):
            copies["z", o].wait_recv()
        mine = line(spot.me)
        start("across", mine, mine, (spot.across, spot.z))
        start("along", mine, mine, (spot.along, spot.z))
        start(("twin", 0), mine, mine, (spot.twin, spot.z))

    def send_on():
        copies["across"].wait_recv()
        part = line(spot.across, 0, rows // 2)
        start("corner along", part, part, (spot.along, spot.z))
        mine = line(spot.across)
        start(("twin", 1), mine, mine, (spot.twin, spot.z))
        copies["along"].wait_recv()
        part = line(spot.along, rows // 2, rows // 2)
        start("corner across", part, part, (spot.across, spot.z))
        mine = line(spot.along)
        start(("twin", 2), mine, mine, (spot.twin, spot.z))

    def send_corner():
        copies["corner along"].wait_recv()
        copies["corner across"].wait_recv()
        mine = line(spot.corner)
        start(("twin", 3), mine, mine, (spot.twin, spot.z))

    def finish():
        for n in range(4):
            copies["twin", n].wait_recv()

    def close():
        for copy in copies.values():
            copy.wait_send()

    return [send_up, send_line, send_on, send_corner, finish, close]


def table_steps(spot, shard, whole, sems):
    columns = shard.shape[1]
    copies = []

    def send_up():
        own = whole.at[:, at(spot.z, columns)]
        for o in range(1, spot.layers):
            copies.append(copy_to(shard, own, sems, o - 1, (spot.me, spot.above(o))))
        whole[:, at(spot.z, columns)] = shard[...]

    def finish():
        for copy in copies:
            copy.wait()

    return [send_up, finish]


def gather_all(table, weights):
    number = len(weights)

    def kernel(*refs):
        table, shards = (refs[0], refs[1 : 1 + number])
        whole_table, wholes = (refs[1 + number], refs[2 + number : 2 + 2 * number])
        table_sems, sems = refs[2 + 2 * number :]
        spot = Place()
        spot.greet(False)
        vectors = table_steps(spot, table, whole_table, table_sems)
        steps = [
            gather_steps(spot, shards[n], wholes[n], sems.at[n]) for n in range(number)
        ]
        for n in range(number):
            steps[n][0]()
            if n == 0:
                vectors[0]()
        for turn in range(1, number + 5):
            for n in range(number):
                if 1 <= turn - n <= 4:
                    steps[n][turn - n]()
        vectors[1]()
        for n in range(number):
            steps[n][5]()

    whole = pl.BlockSpec(memory_space=pltpu.VMEM)
    return pl.pallas_call(
        kernel,
        out_shape=[shape((table.shape[0], 4 * table.shape[1]), f32)]
        + [shape((8 * w.shape[0], 4 * w.shape[1]), w.dtype) for w in weights],
        in_specs=[whole] * (number + 1),
        out_specs=[whole] * (number + 1),
        scratch_shapes=[
            pltpu.SemaphoreType.DMA((2, 3)),
            pltpu.SemaphoreType.DMA((number, 2, GATHER_SLOTS)),
        ],
        compiler_params=pltpu.CompilerParams(
            vmem_limit_bytes=VMEM_BYTES, collective_id=0, has_side_effects=True
        ),
    )(table, *weights)


SCATTER_SLOTS = 11


def scatter_buffers(rows, columns):
    return [
        shape((4, rows, columns), bf16),
        shape((2, rows // 2, columns), bf16),
        shape((2, rows, columns), bf16),
        shape((3, rows, columns // 4), bf16),
    ]


def scatter_steps(spot, grad, out, sums, corner, layer, lines, sems):
    _, rows, columns = sums.shape
    part = columns // spot.layers
    half = rows // 2
    copies = {}

    def start(name, source, target, device):
        copies[name] = copy_to(source, target, sems, len(copies), device)

    def send_twin():
        for n in (3, 1, 2, 0):
            theirs = grad.at[at(spot.twin_mates[n], rows), :]
            start(("twin", n), theirs, sums.at[n], (spot.twin, spot.z))

    def add(target, begin, size, *terms):
        total = terms[0].astype(f32)
        for term in terms[1:]:
            total = total + term.astype(f32)
        sums[target, begin : begin + size, :] = total.astype(bf16)

    def send_corner():
        for n in (3, 1, 2, 0):
            copies["twin", n].wait_recv()
            add(n, 0, rows, grad[at(spot.mates[n], rows), :], sums[n])
            if n == 3:
                start("along", sums.at[3, :half], corner.at[0], (spot.along, spot.z))
                start("across", sums.at[3, half:], corner.at[1], (spot.across, spot.z))

    def send_layer():
        copies["along"].wait_recv()
        add(1, 0, half, sums[1, :half, :], corner[0])
        start("own across", sums.at[1], layer.at[0], (spot.across, spot.z))
        copies["across"].wait_recv()
        add(2, half, half, sums[2, half:, :], corner[1])
        start("own along", sums.at[2], layer.at[1], (spot.along, spot.z))

    def send_up():
        copies["own across"].wait_recv()
        copies["own along"].wait_recv()
        add(0, 0, rows, sums[0], layer[0], layer[1])
        for o in range(1, spot.layers):
            theirs = sums.at[0, :, at(spot.above(o), part)]
            start(("z", o), theirs, lines.at[o - 1], (spot.me, spot.above(o)))

    def finish():
        total = sums[0, :, at(spot.z, part)].astype(f32)
        for o in range(1, spot.layers):
            copies["z", o].wait_recv()
            total = total + lines[o - 1].astype(f32)
        out[...] = total

    def close():
        for copy in copies.values():
            copy.wait_send()

    return [send_twin, send_corner, send_layer, send_up, finish, close]


def small_steps(spot, vectors, states, out, lines, layers, sems):
    high, low = (vectors.shape[0], states.shape[0])
    columns = vectors.shape[1] // spot.layers
    copies = []

    def send_up():
        for o in range(1, spot.layers):
            above = spot.above(o)
            copies.append(
                copy_to(
                    vectors.at[:, at(above, columns)],
                    lines.at[spot.z, :high],
                    sems,
                    2 * o - 2,
                    (spot.me, above),
                )
            )
            copies.append(
                copy_to(states, lines.at[spot.z, high:], sems, 2 * o - 1, (spot.me, above))
            )
        lines[spot.z, :high, :] = vectors[:, at(spot.z, columns)]
        lines[spot.z, high:, :] = states[...]

    def send_layer():
        for copy in copies:
            copy.wait()
        del copies[:]
        total = lines[0]
        for n in range(1, spot.layers):
            total = total + lines[n]
        layers[spot.me] = total
        own = layers.at[spot.me]
        for o in range(1, spot.depth):
            other = ((spot.me + o) % spot.depth, spot.z)
            copies.append(copy_to(own, own, sems, 5 + o, other))

    def finish():
        for copy in copies:
            copy.wait()
        total = layers[0]
        for n in range(1, spot.depth):
            total = total + layers[n]
        out[...] = total

    return [send_up, send_layer, finish]


def scatter_all(vectors, states, grads):
    number = len(grads)
    blocks = [(g.shape[0] // 8, g.shape[1]) for g in grads]
    small = shape((vectors.shape[0] + states.shape[0], vectors.shape[1] // 4), f32)

    def kernel(*refs):
        vectors, states, grads = (refs[0], refs[1], refs[2 : 2 + number])
        refs = refs[2 + number :]
        small_out, outs = (refs[0], refs[1 : 1 + number])
        refs = refs[1 + number :]
        lines, layers, small_sems, sems = refs[:4]
        refs = refs[4:]
        spot = Place()
        spot.greet(True)
        little = small_steps(spot, vectors, states, small_out, lines, layers, small_sems)
        steps = [
            scatter_steps(spot, grads[n], outs[n], *refs[4 * n : 4 * n + 4], sems.at[n])
            for n in range(number)
        ]
        order = list(range(number))[::-1]
        little[0]()
        for turn in range(number + 5):
            for n, which in enumerate(order):
                if 0 <= turn - n <= 4:
                    steps[which][turn - n]()
            if turn in (1, 3):
                little[(turn + 1) // 2]()
        for step in steps:
            step[5]()

    whole = pl.BlockSpec(memory_space=pltpu.VMEM)
    scratch = [
        pltpu.VMEM((4,) + small.shape, f32),
        pltpu.VMEM((8,) + small.shape, f32),
        pltpu.SemaphoreType.DMA((2, 13)),
        pltpu.SemaphoreType.DMA((number, 2, SCATTER_SLOTS)),
    ]
    for rows, columns in blocks:
        scratch += [pltpu.VMEM(s.shape, s.dtype) for s in scatter_buffers(rows, columns)]
    out, *outs = pl.pallas_call(
        kernel,
        out_shape=[small] + [shape((rows, columns // 4), f32) for rows, columns in blocks],
        in_specs=[whole] * (number + 2),
        out_specs=[whole] * (number + 1),
        scratch_shapes=scratch,
        compiler_params=pltpu.CompilerParams(
            vmem_limit_bytes=VMEM_BYTES, collective_id=1, has_side_effects=True
        ),
    )(vectors, states, *grads)
    return [out[: vectors.shape[0]], out[vectors.shape[0] :], *outs]


def body(
    frames,
    lengths,
    ffn1_in,
    ffn1_out,
    ffn1_vec,
    ssm_in,
    ssm_out,
    ssm_vec,
    decay,
    freq,
    coef_re,
    coef_im,
    conv_in,
    conv_out,
    conv_vec,
    ffn2_in,
    ffn2_out,
    ffn2_vec,
    cotangent,
):
    count, length, width = frames.shape
    rows = count * length
    tiles = width // LANES
    hidden_width = width * (ffn1_vec.shape[0] - 3)
    heads, states = decay.shape
    flat = frames.reshape(rows, width)

    def pad(vec, to):
        return jnp.pad(vec.astype(f32), ((0, to - vec.shape[0]), (0, 0)))

    table = jnp.concatenate(
        [pad(ffn1_vec, SS - F1), pad(ssm_vec, CV - SS), pad(conv_vec, F2 - CV), pad(ffn2_vec, TABLE - F2)], 0
    )
    weights = (ffn1_in, ffn1_out, ssm_in, ssm_out, conv_in, conv_out, ffn2_in, ffn2_out)
    fast = (lax.axis_size("dp"), lax.axis_size("fsdp")) == (8, 4)
    if fast:
        table, *weights = gather_all(table, weights)
    else:
        table = lax.all_gather(table, "fsdp", axis=1, tiled=True)
        weights = [whole for n in range(0, 8, 2) for whole in bring(weights[n], weights[n + 1])]
    first_in, first_out, mixer_in, mixer_out = weights[:4]
    module_in, module_out, second_in, second_out = weights[4:]

    row = shape((rows, width), bf16)
    row_f = shape((rows, width), f32)
    wide_row = shape((rows, hidden_width), bf16)
    scales = shape((rows, 1), f32)
    mixes = shape((tiles, length, count * LANES), bf16)
    band = shape((tiles, 2 * TILE, length), bf16)
    padded = shape((count * tiles, length + 2 * EDGE, LANES), f32)
    square = shape((width, width), bf16)
    double = shape((width, 2 * width), bf16)
    wide_grad = shape((width, hidden_width), bf16)
    tall_grad = shape((hidden_width, width), bf16)
    power = shape((4, heads * states, LANES), f32)

    hidden, before = call(
        partial(ffn1_forward, count), [row_f, wide_row], [], (), flat, table, first_in, first_out
    )

    def mixer_kernel(
        hidden_in, table, weight_in, weight_out, decay, freq, re, im, hidden, normed, scale, value,
        gate, state, powers, wide_t, wide, gated,
    ):
        hidden[...] = hidden_in[...]
        build_bands(decay, freq, re, im, powers, wide, wide_t, length)
        ssm_forward(
            count, hidden, table, weight_in, weight_out, wide, normed, scale, value, gate, state,
            gated,
        )

    hidden, mixer_normed, mixer_scale, value, gate, state, powers, wide_t = call(
        mixer_kernel, [row_f, row, scales, mixes, mixes, mixes, power, band], [band, row], (),
        hidden, table, mixer_in, mixer_out, decay, freq, coef_re, coef_im,
    )

    def module_kernel(hidden_in, lengths, table, weight_in, weight_out, hidden, *rest):
        hidden[...] = hidden_in[...]
        conv_forward(count, hidden, lengths, table, weight_in, weight_out, *rest)

    hidden, module_normed, module_scale, linear, module_gate, depth = call(
        module_kernel, [row_f, row, scales, row, row, row], [padded, row], (1,),
        hidden, lengths, table, module_in, module_out,
    )
    output, grad, second_in_grad, second_out_grad, second_vec = call(
        partial(ffn2_both, count),
        [row, row_f, wide_grad, tall_grad, shape((TABLE - F2, width), f32)],
        [row, scales, wide_row, row, row, row, row, row_f],
        (2,), hidden, cotangent.reshape(rows, width), lengths, table, second_in, second_out,
    )

    def module_back(grad_in, lengths, table, w_in, w_out, normed, scale, linear, gate, depth, grad, *rest):
        grad[...] = grad_in[...]
        conv_backward(
            count, lengths, table, w_in, w_out, normed, scale, linear, gate, depth, grad, *rest
        )

    grad, module_in_grad, module_out_grad, module_vec = call(
        module_back,
        [row_f, double, square, shape((F2 - CV, width), f32)],
        [row, row, row, padded, padded, shape((rows, 2 * width), bf16)],
        (1,), grad, lengths, table, module_in, module_out, module_normed, module_scale, linear,
        module_gate, depth,
    )

    def mixer_back(
        grad_in, table, w_in, w_out, wide_t, powers, decay, re, im, normed, scale, value, gate,
        state, grad, *rest,
    ):
        grad[...] = grad_in[...]
        ssm_backward(
            count, table, w_in, w_out, wide_t, powers, decay, re, im, normed, scale, value, gate,
            state, grad, *rest,
        )

    grad, mixer_in_grad, mixer_out_grad, mixer_vec, state_grad = call(
        mixer_back,
        [row_f, double, square, shape((CV - SS, width), f32), shape((4 * heads, LANES), f32)],
        [row, row, mixes, row, shape((rows, 2 * width), bf16)],
        (), grad, table, mixer_in, mixer_out, wide_t, powers, decay, coef_re, coef_im,
        mixer_normed, mixer_scale, value, gate, state,
    )
    frames_grad, first_in_grad, first_out_grad, first_vec = call(
        partial(ffn1_backward, count),
        [row, wide_grad, tall_grad, shape((SS - F1, width), f32)],
        [row, row, row, row, row_f],
        (), flat, grad, table, first_in, first_out, before,
    )
    vec_grads = jnp.concatenate([first_vec, mixer_vec, module_vec, second_vec], 0)
    grads = (
        first_in_grad, first_out_grad, mixer_in_grad, mixer_out_grad, module_in_grad,
        module_out_grad, second_in_grad, second_out_grad,
    )
    if fast:
        vec_grads, state_grad, *grads = scatter_all(vec_grads, state_grad, grads)
    else:
        vec_grads = lax.psum(
            lax.psum_scatter(vec_grads, "fsdp", scatter_dimension=1, tiled=True), "dp"
        )
        state_grad = lax.psum(state_grad, ("dp", "fsdp"))
        grads = [send(grad) for grad in grads]
    state_grad = state_grad[:, :states].reshape(4, heads, states)

    def layer(number, base, like):
        return (grads[number], grads[number + 1], vec_grads[base : base + like.shape[0]])

    return (
        (output.reshape(count, length, width), frames_grad.reshape(count, length, width))
        + layer(0, F1, ffn1_vec)
        + layer(2, SS, ssm_vec)
        + tuple(state_grad[n] for n in range(4))
        + layer(4, CV, conv_vec)
        + layer(6, F2, ffn2_vec)
    )


def solution(mesh):
    split = P(("dp", "fsdp"), None, None)
    weight = P("dp", "fsdp")
    vector = P(None, "fsdp")
    layer = (weight, weight, vector)
    whole = (P(), P(), P(), P())
    in_specs = (split, P(("dp", "fsdp"))) + layer + layer + whole + layer + layer + (split,)
    out_specs = (split, split) + layer + layer + whole + layer + layer
    return jax.shard_map(body, mesh=mesh, in_specs=in_specs, out_specs=out_specs, check_vma=False)
```

```python
from functools import partial

import jax
import jax.numpy as jnp
from jax import lax
from jax.experimental import pallas as pl
from jax.experimental.pallas import tpu as pltpu
from jax.sharding import PartitionSpec as P

EPSILON = 1e-05
VMEM_BYTES = 62 * 2**20
LANES = 128
TILE = 256
EDGE = 8
F1, SS, CV, F2 = (0, 8, 16, 40)
TABLE = 56
f32 = jnp.float32
bf16 = jnp.bfloat16


def dot(left, right):
    return jnp.dot(left, right, preferred_element_type=f32)


def dot_nt(left, right):
    return lax.dot_general(left, right, (((1,), (1,)), ((), ())), preferred_element_type=f32)


def dot_tn(left, right):
    return lax.dot_general(left, right, (((0,), (0,)), ((), ())), preferred_element_type=f32)


def loop(number, step):
    def turn(index, carry):
        step(index)
        return carry

    lax.fori_loop(0, number, turn, 0)


def at(index, size):
    if isinstance(index, int):
        return slice(index * size, (index + 1) * size)
    return pl.ds(pl.multiple_of(index * size, size), size)


def idle(micros=0.0):
    pass


def steps_of(number, step, tick, micros):
    if tick is idle:
        loop(number, step)
    else:
        for index in range(number):
            step(index)
            tick(micros)


def norm(hidden):
    center = hidden - jnp.mean(hidden, -1, keepdims=True)
    scale = lax.rsqrt(jnp.mean(center * center, -1, keepdims=True) + EPSILON)
    return (center * scale, scale)


def norm_back(grad, normed, scale, gain):
    scaled = grad * gain
    centered = (
        scaled
        - jnp.mean(scaled, -1, keepdims=True)
        - normed * jnp.mean(scaled * normed, -1, keepdims=True)
    )
    return (
        scale * centered,
        jnp.sum(grad * normed, 0, keepdims=True),
        jnp.sum(grad, 0, keepdims=True),
    )


def frame_mask(length, valid):
    return (lax.broadcasted_iota(jnp.int32, (length, 1), 0) < valid).astype(f32)


def identity(size):
    return lax.broadcasted_iota(jnp.int32, (size, size), 0) == lax.broadcasted_iota(
        jnp.int32, (size, size), 1
    )


def state_column(values):
    heads, states = values.shape
    eye = identity(states)
    columns = [
        jnp.sum(
            jnp.where(eye, jnp.broadcast_to(values[h : h + 1, :], (states, states)), 0.0),
            1,
            keepdims=True,
        )
        for h in range(heads)
    ]
    return jnp.concatenate(columns, 0)


def state_rows(column, heads):
    states = column.shape[0] // heads
    eye = identity(states)
    rows = [
        jnp.sum(
            jnp.where(
                eye,
                jnp.broadcast_to(column[h * states : (h + 1) * states, :], (states, states)),
                0.0,
            ),
            0,
            keepdims=True,
        )
        for h in range(heads)
    ]
    return jnp.concatenate(rows, 0)


def head_steps(heads, states):
    row = lax.broadcasted_iota(jnp.int32, (heads * states, 1), 0)
    log_steps = jnp.full((heads * states, 1), -6.9, f32)
    for h in range(1, heads):
        log_steps = jnp.where(row >= h * states, -6.9 + 4.6 * h / (heads - 1), log_steps)
    return jnp.exp(log_steps)


def state_powers(decay, freq, step, stride):
    places = lax.broadcasted_iota(jnp.int32, (1, LANES), 1).astype(f32) * float(stride)
    damping = jnp.exp(-(step * decay) * places)
    phase = (step * freq) * places
    return (damping * jnp.cos(phase), damping * jnp.sin(phase))


def build_bands(decay_ref, freq_ref, re_ref, im_ref, powers, wide, wide_t, length, tick=idle):
    heads, states = decay_ref.shape
    step = head_steps(heads, states)
    decay, freq = (state_column(decay_ref[...]), state_column(freq_ref[...]))
    real, imag = (state_column(re_ref[...]), state_column(im_ref[...]))
    near_re, near_im = state_powers(decay, freq, step, 1)
    far_re, far_im = state_powers(decay, freq, step, LANES)
    powers[0], powers[1], powers[2], powers[3] = (near_re, near_im, far_re, far_im)
    lead_re = real * far_re - imag * far_im
    lead_im = real * far_im + imag * far_re
    blocks = length // LANES
    pieces = []
    for a in range(blocks):
        term = lead_re[:, a : a + 1] * near_re - lead_im[:, a : a + 1] * near_im
        pieces.append(jnp.sum(term.reshape(heads, states, LANES), 1))
    root = jnp.sqrt(step / states)
    factor = jnp.concatenate([root[h * states : h * states + 1, :] for h in range(heads)], 0)
    low = [(piece * factor).astype(bf16) for piece in pieces]
    turn = (
        lax.broadcasted_iota(jnp.int32, (LANES, LANES), 0)
        + lax.broadcasted_iota(jnp.int32, (LANES, LANES), 1)
        == LANES - 1
    ).astype(bf16)
    ring = length + TILE
    zeros = jnp.zeros((heads, TILE), f32)
    forward = jnp.concatenate([piece.astype(f32) for piece in low] + [zeros], 1)
    backward = jnp.concatenate([dot(piece, turn) for piece in low[::-1]] + [zeros], 1)
    backward = pltpu.roll(backward, ring - (TILE - 1), 1)
    tick(9.0)
    for source, band in ((backward, wide), (forward, wide_t)):
        for h in range(heads):
            if h == heads // 2:
                tick(9.0)
            row = jnp.broadcast_to(source[h : h + 1, :], (8, ring))
            base = pltpu.roll(row, 0, 1, stride=1, stride_axis=0)
            for g in range(0, LANES // 8, 2):
                pair = jnp.concatenate(
                    [pltpu.roll(base, 8 * g, 1), pltpu.roll(base, 8 * g + 8, 1)], 0
                )
                for q in range(TILE // LANES):
                    if q == 0:
                        cut = pair[:, :length]
                    else:
                        cut = jnp.concatenate(
                            [pair[:, ring - q * LANES :], pair[:, : length - q * LANES]], 1
                        )
                    place = (h % 2) * TILE + q * LANES + 8 * g
                    band[h // 2, place : place + 16, :] = cut.astype(bf16)
        tick(9.0)


def state_grads(kernel_grad, powers, decay_ref, re_ref, im_ref, out):
    heads, states = decay_ref.shape
    step = head_steps(heads, states)
    real, imag = (state_column(re_ref[...]), state_column(im_ref[...]))
    near_re, near_im, far_re, far_im = (powers[0], powers[1], powers[2], powers[3])
    length = kernel_grad.shape[1]
    zero_re = zero_im = one_re = one_im = None
    for a in range(length // LANES):
        block = kernel_grad[:, a * LANES : (a + 1) * LANES]
        spread = jnp.concatenate(
            [jnp.broadcast_to(block[h : h + 1, :], (states, LANES)) for h in range(heads)], 0
        )
        term_re, term_im = (far_re[:, a : a + 1] * spread, far_im[:, a : a + 1] * spread)
        if a == 0:
            zero_re, zero_im = (term_re, term_im)
            one_re, one_im = (jnp.zeros_like(term_re), jnp.zeros_like(term_im))
        else:
            zero_re, zero_im = (zero_re + term_re, zero_im + term_im)
            one_re, one_im = (one_re + a * LANES * term_re, one_im + a * LANES * term_im)
    places = lax.broadcasted_iota(jnp.int32, (1, LANES), 1).astype(f32)
    one_re, one_im = (one_re + places * zero_re, one_im + places * zero_im)

    def close(left_re, left_im):
        return (
            jnp.sum(near_re * left_re - near_im * left_im, 1, keepdims=True),
            jnp.sum(near_re * left_im + near_im * left_re, 1, keepdims=True),
        )

    plain_re, plain_im = close(zero_re, zero_im)
    place_re, place_im = close(one_re, one_im)
    scale = jnp.sqrt(step / states)
    columns = (
        -step * scale * (real * place_re - imag * place_im),
        -step * scale * (real * place_im + imag * place_re),
        scale * plain_re,
        -scale * plain_im,
    )
    out[...] = jnp.zeros_like(out)
    for number, column in enumerate(columns):
        out[number * heads : (number + 1) * heads, :states] = state_rows(column, heads)


def feed_forward(normal, weight_in, weight_out, table, base, before, rows):
    width = normal.shape[1]
    total = None
    for c in range(weight_in.shape[1] // width):
        part = slice(c * width, (c + 1) * width)
        value = dot(normal, weight_in[:, part]) + table[base + 2 + c : base + 3 + c, :]
        before[rows, part] = value.astype(bf16)
        active = (value * jax.nn.sigmoid(value)).astype(bf16)
        term = dot(active, weight_out[part, :])
        total = term if total is None else total + term
    return total


def ffn1_forward(count, frames, table, weight_in, weight_out, hidden, before, tick=idle):
    length = frames.shape[0] // count
    blocks = weight_in.shape[1] // weight_in.shape[0]

    def step(u):
        rows = at(u, length)
        value = frames[rows, :].astype(f32)
        normed, _ = norm(value)
        normal = (normed * table[F1 : F1 + 1, :] + table[F1 + 1 : F1 + 2, :]).astype(bf16)
        total = feed_forward(normal, weight_in, weight_out, table, F1, before, rows)
        bias = table[F1 + 2 + blocks : F1 + 3 + blocks, :]
        hidden[rows, :] = value + 0.5 * (total + bias)

    steps_of(count, step, tick, 4.0)


def head_lanes():
    return lax.broadcasted_iota(jnp.int32, (1, 2 * LANES), 1) % LANES < LANES // 2


def ssm_forward(
    count, hidden, table, weight_in, weight_out, wide, normed_ref, scale_ref, value_ref, gate_ref,
    state_ref, gated, tick=idle,
):
    total_rows, width = hidden.shape
    length = total_rows // count
    tiles = width // LANES

    def enter(u):
        rows = at(u, length)
        lanes = at(u, LANES)
        normed, scale = norm(hidden[rows, :])
        normed_ref[rows, :] = normed.astype(bf16)
        scale_ref[rows, :] = scale
        normal = (normed * table[SS : SS + 1, :] + table[SS + 1 : SS + 2, :]).astype(bf16)
        value = dot(normal, weight_in[:, :width]).astype(bf16)
        gate = dot(normal, weight_in[:, width:]).astype(bf16)
        for j in range(tiles):
            part = slice(j * LANES, (j + 1) * LANES)
            value_ref[j, :, lanes] = value[:, part]
            gate_ref[j, :, lanes] = gate[:, part]

    steps_of(count, enter, tick, 1.5)
    first = head_lanes()
    steps = length // TILE
    for j in range(tiles):
        part = slice(j * LANES, (j + 1) * LANES)
        skip = table[SS + 2 : SS + 3, part]
        skip = jnp.concatenate([skip, skip], 1)
        for i in range(steps):
            rows = slice(i * TILE, (i + 1) * TILE)
            both = dot(wide[j, :, (steps - 1 - i) * TILE :], value_ref[j, : (i + 1) * TILE, :])
            mixed = jnp.where(first, both[:TILE], both[TILE:])
            gate = gate_ref[j, rows, :].astype(f32)
            state = mixed + skip * value_ref[j, rows, :].astype(f32)
            state_ref[j, rows, :] = state.astype(bf16)
            out = (state * (gate * jax.nn.sigmoid(gate))).astype(bf16)
            for u in range(count):
                gated[u * length + i * TILE : u * length + (i + 1) * TILE, part] = out[
                    :, u * LANES : (u + 1) * LANES
                ]
        if j % 2:
            tick(1.2)

    def leave(u):
        rows = at(u, length)
        hidden[rows, :] += dot(gated[rows, :], weight_out[...])

    loop(count, leave)
    tick(1.0)


def clear_edges(padded, length):
    number, _, lanes = padded.shape
    zeros = jnp.zeros((number, EDGE, lanes), f32)
    padded[:, :EDGE, :] = zeros
    padded[:, EDGE + length :, :] = zeros


ROWS, GROUP = (64, 4)


def conv_rows(n, base):
    first = pl.multiple_of(n * (ROWS * GROUP), ROWS * GROUP)
    for g in range(GROUP):
        begin = first + g * ROWS
        yield begin, pl.ds(pl.multiple_of(base + begin, 32), ROWS)


def shifted(padded, index, begin):
    for b in range(8):
        near = padded[index, pl.ds(begin + b + EDGE - 8, ROWS + 8), :]
        yield b - 8, near[:ROWS]
        yield b, near[8:]


def conv_forward(
    count, hidden, lengths, table, weight_in, weight_out, normed_ref, scale_ref, linear_ref,
    gate_ref, depth_ref, glu, active, tick=idle,
):
    total_rows, width = hidden.shape
    length = total_rows // count
    tiles = width // LANES
    clear_edges(glu, length)

    def enter(u):
        rows = at(u, length)
        normed, scale = norm(hidden[rows, :])
        normed_ref[rows, :] = normed.astype(bf16)
        scale_ref[rows, :] = scale
        normal = (normed * table[CV : CV + 1, :] + table[CV + 1 : CV + 2, :]).astype(bf16)
        linear = dot(normal, weight_in[:, :width])
        gate = jax.nn.sigmoid(dot(normal, weight_in[:, width:]))
        linear_ref[rows, :] = linear.astype(bf16)
        gate_ref[rows, :] = gate.astype(bf16)
        value = linear * gate * frame_mask(length, lengths[u])
        for j in range(tiles):
            glu[u * tiles + j, EDGE : EDGE + length, :] = value[:, j * LANES : (j + 1) * LANES]

    steps_of(count, enter, tick, 1.7)
    number = CONV_TAPS

    def convolve(index):
        u, j = (index // tiles, index % tiles)
        lanes = at(j, LANES)
        taps = [table[CV + 2 + t : CV + 3 + t, lanes] for t in range(number)]

        def block(n):
            for begin, rows in conv_rows(n, u * length):
                total = None
                for shift, moved in shifted(glu, index, begin):
                    t = number // 2 + shift
                    if 0 <= t < number:
                        term = taps[t] * moved
                        total = term if total is None else total + term
                depth_ref[rows, lanes] = total.astype(bf16)
                active[rows, lanes] = (total * jax.nn.sigmoid(total)).astype(bf16)

        loop(length // (ROWS * GROUP), block)

    steps_of(count, lambda u: loop(tiles, lambda j: convolve(u * tiles + j)), tick, 1.6)

    def leave(u):
        rows = at(u, length)
        hidden[rows, :] += dot(active[rows, :], weight_out[...])

    loop(count, leave)
    tick(1.0)


CONV_TAPS = 15


def half_of(size, q):
    return [slice(b + q * LANES, b + (q + 1) * LANES) for b in range(0, size, 2 * LANES)]


IN_PIECES = ((0, 0, 1), (1, 0, 2), (1, 1, 2))


def ffn_backward(
    count, weight_in, weight_out, before, branch, normal, grad_in, grad_out, vec_grad, active,
    leave, tick=idle, ready=None,
):
    total_rows, width = branch.shape
    length = total_rows // count
    done = 0
    for q in range(2):
        parts = half_of(weight_in.shape[1], q)

        def step(u):
            rows = at(u, length)
            out = jnp.concatenate([weight_out[part, :] for part in parts], 0)
            grad = dot_nt(branch[rows, :], out)
            value = jnp.concatenate([before[rows, part] for part in parts], 1).astype(f32)
            sig = jax.nn.sigmoid(value)
            active[rows, :] = (value * sig).astype(bf16)
            low = (grad * (sig * (1.0 + value * (1.0 - sig)))).astype(bf16)
            sums = jnp.sum(low.astype(f32), 0, keepdims=True)
            for n, part in enumerate(parts):
                lanes = slice(n * LANES, (n + 1) * LANES)
                before[rows, part] = low[:, lanes]
                row, begin = (2 + part.start // width, part.start % width)
                vec_grad[row : row + 1, begin : begin + LANES] += sums[:, lanes]

        steps_of(count, step, tick, 2.9)
        grad_out[q][...] = dot_tn(active[...], branch[...]).astype(bf16)
        if ready:
            ready(done)
        done += 1
        tick(2.1)
        for target, (half, first, every) in zip(grad_in, IN_PIECES):
            if half == q:
                mine = [before[:, part] for part in parts[first::every]]
                target[...] = dot_tn(normal[...], jnp.concatenate(mine, 1)).astype(bf16)
                if ready:
                    ready(done)
                done += 1
                tick(2.1 / every)
    if ready:
        ready(done)

    def finish(u):
        rows = at(u, length)
        leave(rows, dot_nt(before[rows, :], weight_in[...]))

    steps_of(count, finish, tick, 4.6)


def ffn2_both(
    count, hidden, cotangent, lengths, table, weight_in, weight_out, output, grad, grad_in,
    grad_out, vec_grad, normed_ref, scale_ref, before, normal_ref, branch, active, tick=idle,
    ready=None, greeted=None,
):
    total_rows, width = hidden.shape
    length = total_rows // count
    blocks = weight_in.shape[1] // width
    vec_grad[...] = jnp.zeros_like(vec_grad)
    last = 3 + blocks

    def forward(u):
        rows = at(u, length)
        value = hidden[rows, :]
        normed, scale = norm(value)
        normed_ref[rows, :] = normed.astype(bf16)
        scale_ref[rows, :] = scale
        normal = (normed * table[F2 : F2 + 1, :] + table[F2 + 1 : F2 + 2, :]).astype(bf16)
        normal_ref[rows, :] = normal
        total = feed_forward(normal, weight_in, weight_out, table, F2, before, rows)
        value = value + 0.5 * (total + table[F2 + 2 + blocks : F2 + 3 + blocks, :])
        normed, scale = norm(value)
        gain = table[F2 + last : F2 + last + 1, :]
        mask = frame_mask(length, lengths[u])
        shift = table[F2 + last + 1 : F2 + last + 2, :]
        grad_in, gain_grad, shift_grad = norm_back(
            cotangent[rows, :].astype(f32) * mask, normed, scale, gain
        )
        output[rows, :] = ((normed * gain + shift) * mask).astype(bf16)
        vec_grad[last : last + 1, :] += gain_grad
        vec_grad[last + 1 : last + 2, :] += shift_grad
        grad[rows, :] = grad_in
        low = (0.5 * grad_in).astype(bf16)
        branch[rows, :] = low
        vec_grad[last - 1 : last, :] += jnp.sum(low.astype(f32), 0, keepdims=True)

    if tick is idle:
        loop(count, forward)
    else:
        forward(0)
        greeted()
        for u in range(1, count):
            forward(u)

    def leave(rows, value):
        grad_in, gain_grad, shift_grad = norm_back(
            value, normed_ref[rows, :].astype(f32), scale_ref[rows, :], table[F2 : F2 + 1, :]
        )
        grad[rows, :] += grad_in
        vec_grad[0:1, :] += gain_grad
        vec_grad[1:2, :] += shift_grad

    ffn_backward(
        count, weight_in, weight_out, before, branch, normal_ref, grad_in, grad_out, vec_grad,
        active, leave, tick, ready,
    )


def conv_backward(
    count, lengths, table, weight_in, weight_out, normed_ref, scale_ref, linear_ref, gate_ref,
    depth_ref, grad, grad_in, grad_out, vec_grad, normal_ref, branch, active, depth_grad,
    tap_grads, mixed_grad, tick=idle,
):
    total_rows, width = grad.shape
    length = total_rows // count
    tiles = width // LANES
    number = CONV_TAPS
    vec_grad[...] = jnp.zeros_like(vec_grad)
    clear_edges(depth_grad, length)

    def enter(u):
        rows = at(u, length)
        low = grad[rows, :].astype(bf16)
        branch[rows, :] = low
        normed = normed_ref[rows, :].astype(f32)
        normal = (normed * table[CV : CV + 1, :] + table[CV + 1 : CV + 2, :]).astype(bf16)
        normal_ref[rows, :] = normal
        active_grad = dot_nt(low, weight_out[...])
        depth = depth_ref[rows, :].astype(f32)
        sig = jax.nn.sigmoid(depth)
        active[rows, :] = (depth * sig).astype(bf16)
        slope = active_grad * (sig * (1.0 + depth * (1.0 - sig)))
        for j in range(tiles):
            part = slice(j * LANES, (j + 1) * LANES)
            depth_grad[u * tiles + j, EDGE : EDGE + length, :] = slope[:, part]

    steps_of(count, enter, tick, 1.8)

    def convolve(index):
        u, j = (index // tiles, index % tiles)
        lanes = at(j, LANES)
        second = pl.ds(pl.multiple_of(width + j * LANES, LANES), LANES)
        taps = [table[CV + 2 + t : CV + 3 + t, lanes] for t in range(number)]
        tap_grads[...] = jnp.zeros_like(tap_grads)

        def block(n):
            sums = [None] * number
            for begin, rows in conv_rows(n, u * length):
                places = begin + lax.broadcasted_iota(jnp.int32, (ROWS, 1), 0)
                mask = (places < lengths[u]).astype(f32)
                linear = linear_ref[rows, lanes].astype(f32)
                gate = gate_ref[rows, lanes].astype(f32)
                glu = linear * gate * mask
                total = None
                for shift, moved in shifted(depth_grad, index, begin):
                    t = number // 2 - shift
                    if not 0 <= t < number:
                        continue
                    term = taps[t] * moved
                    total = term if total is None else total + term
                    pairs = jnp.sum((glu * moved).reshape(ROWS // 8, 8, LANES), 0)
                    sums[t] = pairs if sums[t] is None else sums[t] + pairs
                gated = total * mask * gate
                mixed_grad[rows, lanes] = gated.astype(bf16)
                mixed_grad[rows, second] = (gated * linear * (1.0 - gate)).astype(bf16)
            for t in range(number):
                tap_grads[t] += sums[t]

        loop(length // (ROWS * GROUP), block)
        for t in range(number):
            vec_grad[2 + t : 3 + t, lanes] += jnp.sum(tap_grads[t], 0, keepdims=True)

    steps_of(count, lambda u: loop(tiles, lambda j: convolve(u * tiles + j)), tick, 2.7)
    grad_in[...] = dot_tn(normal_ref[...], mixed_grad[...]).astype(bf16)
    tick(2.1)
    grad_out[...] = dot_tn(active[...], branch[...]).astype(bf16)
    tick(1.3)
    mixer_leave(
        count, table, CV, weight_in, normed_ref, scale_ref, grad, vec_grad, mixed_grad, tick
    )


def mixer_leave(
    count, table, base, weight_in, normed_ref, scale_ref, grad, vec_grad, mixed_grad, tick
):
    length = grad.shape[0] // count

    def leave(u):
        rows = at(u, length)
        back = dot_nt(mixed_grad[rows, :], weight_in[...])
        grad_in, gain_grad, shift_grad = norm_back(
            back, normed_ref[rows, :].astype(f32), scale_ref[rows, :], table[base : base + 1, :]
        )
        grad[rows, :] += grad_in
        vec_grad[0:1, :] += gain_grad
        vec_grad[1:2, :] += shift_grad

    steps_of(count, leave, tick, 1.5)


def diagonal_sums(block):
    size = block.shape[0]
    zeros = jnp.zeros((8, size), f32)
    total = None
    for g in range(size // 8):
        rows = jnp.concatenate([block[8 * g : 8 * g + 8, :], zeros], 1)
        if g:
            rows = pltpu.roll(rows, 2 * size - 8 * g, 1)
        total = rows if total is None else total + rows
    out = total[0:1, :]
    for i in range(1, 8):
        out = out + pltpu.roll(total, 2 * size - i, 1)[i : i + 1, :]
    return out


def ssm_backward(
    count, table, weight_in, weight_out, wide_t, normed_ref, scale_ref, value_ref, gate_ref,
    state_ref, grad, grad_in, grad_out, vec_grad, kernel_grad, normal_ref, branch, time_grad,
    gated, mixed_grad, tick=idle, start=None,
):
    total_rows, width = grad.shape
    length = total_rows // count
    tiles = width // LANES
    steps = length // TILE
    vec_grad[...] = jnp.zeros_like(vec_grad)

    def enter(u):
        rows = at(u, length)
        lanes = at(u, LANES)
        low = grad[rows, :].astype(bf16)
        branch[rows, :] = low
        normed = normed_ref[rows, :].astype(f32)
        normal = (normed * table[SS : SS + 1, :] + table[SS + 1 : SS + 2, :]).astype(bf16)
        normal_ref[rows, :] = normal
        gated_grad = dot_nt(low, weight_out[...])
        for j in range(tiles):
            part = slice(j * LANES, (j + 1) * LANES)
            second = slice(width + j * LANES, width + (j + 1) * LANES)
            gate = gate_ref[j, :, lanes].astype(f32)
            state = state_ref[j, :, lanes].astype(f32)
            sig = jax.nn.sigmoid(gate)
            swish = gate * sig
            here = gated_grad[:, part]
            state_grad = here * swish
            time_grad[j, :, lanes] = state_grad.astype(bf16)
            gated[rows, part] = (state * swish).astype(bf16)
            mixed_grad[rows, second] = (
                here * state * (sig * (1.0 + gate * (1.0 - sig)))
            ).astype(bf16)
            vec_grad[2:3, part] += jnp.sum(
                state_grad * value_ref[j, :, lanes].astype(f32), 0, keepdims=True
            )

    if tick is idle:
        loop(count, enter)
    else:
        enter(0)
        start()
        for u in range(1, count):
            enter(u)
            tick(1.7)
    first = head_lanes()
    kernel_rows = []
    for j in range(tiles):
        part = slice(j * LANES, (j + 1) * LANES)
        skip = table[SS + 2 : SS + 3, part]
        skip = jnp.concatenate([skip, skip], 1)
        sums = [[None] * steps for _ in range(2)]
        for i in range(steps):
            rows = slice(i * TILE, (i + 1) * TILE)
            both = dot(wide_t[j, :, : length - i * TILE], time_grad[j, i * TILE :, :])
            back = jnp.where(first, both[:TILE], both[TILE:])
            back = (back + skip * time_grad[j, rows, :].astype(f32)).astype(bf16)
            for u in range(count):
                mixed_grad[u * length + i * TILE : u * length + (i + 1) * TILE, part] = back[
                    :, u * LANES : (u + 1) * LANES
                ]
        for d in range(steps):
            total = None
            for i in range(steps - d):
                value = value_ref[j, i * TILE : (i + 1) * TILE, :]
                split = jnp.concatenate(
                    [jnp.where(first, value, 0), jnp.where(first, 0, value)], 0
                ).astype(bf16)
                term = dot_nt(split, time_grad[j, (i + d) * TILE : (i + d + 1) * TILE, :])
                total = term if total is None else total + term
            for e in range(2):
                sums[e][d] = diagonal_sums(total[e * TILE : (e + 1) * TILE, :])
        for e in range(2):
            pieces = []
            for d in range(steps):
                piece = sums[e][d][:, :TILE]
                if d + 1 < steps:
                    piece = piece + sums[e][d + 1][:, TILE:]
                pieces.append(piece)
            kernel_rows.append(jnp.concatenate(pieces, 1))
        tick(1.3)
    kernel_grad[...] = jnp.concatenate(kernel_rows, 0)
    grad_in[...] = dot_tn(normal_ref[...], mixed_grad[...]).astype(bf16)
    grad_out[...] = dot_tn(gated[...], branch[...]).astype(bf16)
    tick(2.9)
    mixer_leave(
        count, table, SS, weight_in, normed_ref, scale_ref, grad, vec_grad, mixed_grad, tick
    )


def ffn1_backward(
    count, frames, grad, table, weight_in, weight_out, before, frames_grad, grad_in, grad_out,
    vec_grad, normal_ref, branch, active, tick=idle, ready=None,
):
    total_rows, width = frames.shape
    length = total_rows // count
    blocks = weight_in.shape[1] // width
    vec_grad[...] = jnp.zeros_like(vec_grad)

    def enter(u):
        rows = at(u, length)
        normed, _ = norm(frames[rows, :].astype(f32))
        normal = (normed * table[F1 : F1 + 1, :] + table[F1 + 1 : F1 + 2, :]).astype(bf16)
        normal_ref[rows, :] = normal
        low = (0.5 * grad[rows, :]).astype(bf16)
        branch[rows, :] = low
        vec_grad[2 + blocks : 3 + blocks, :] += jnp.sum(low.astype(f32), 0, keepdims=True)

    steps_of(count, enter, tick, 1.0)

    def leave(rows, value):
        normed, scale = norm(frames[rows, :].astype(f32))
        grad_in, gain_grad, shift_grad = norm_back(value, normed, scale, table[F1 : F1 + 1, :])
        frames_grad[rows, :] = (grad[rows, :] + grad_in).astype(bf16)
        vec_grad[0:1, :] += gain_grad
        vec_grad[1:2, :] += shift_grad

    ffn_backward(
        count, weight_in, weight_out, before, branch, normal_ref, grad_in, grad_out, vec_grad,
        active, leave, tick, ready,
    )


def shape(dims, kind):
    return jax.ShapeDtypeStruct(dims, kind)


def call(kernel, outs, scratch, smem, *operands):
    whole = pl.BlockSpec(memory_space=pltpu.VMEM)
    scalars = pl.BlockSpec(memory_space=pltpu.SMEM)
    return pl.pallas_call(
        kernel,
        out_shape=outs,
        in_specs=[scalars if n in smem else whole for n in range(len(operands))],
        out_specs=[whole] * len(outs),
        scratch_shapes=[pltpu.VMEM(s.shape, s.dtype) for s in scratch],
        compiler_params=pltpu.CompilerParams(vmem_limit_bytes=VMEM_BYTES),
    )(*operands)


def bring(weight_in, weight_out):
    first, second = (
        lax.all_gather(weight_in, "fsdp", axis=1, tiled=True),
        lax.all_gather(weight_out, "fsdp", axis=1, tiled=True),
    )
    return (
        lax.all_gather(first, "dp", axis=0, tiled=True),
        lax.all_gather(second, "dp", axis=0, tiled=True),
    )


def send(grad):
    part = lax.psum_scatter(grad, "fsdp", scatter_dimension=1, tiled=True)
    return lax.psum_scatter(part, "dp", scatter_dimension=0, tiled=True).astype(f32)


class Place:
    def __init__(self):
        me, z = (lax.axis_index("dp"), lax.axis_index("fsdp"))
        y, x, core = (me // 4, me // 2 % 2, me % 2)
        self.me, self.z, self.depth, self.layers = (me, z, 8, 4)
        self.chip, self.core = (me // 2, core)
        self.across = me + 2 - 4 * x
        self.along = me + 4 - 8 * y
        self.corner = me + 6 - 4 * x - 8 * y
        self.twin = me + 1 - 2 * core
        self.mates = (me, self.across, self.along, self.corner)
        turn = 1 - 2 * core
        self.twin_mates = tuple(mate + turn for mate in self.mates)

    def above(self, offset):
        return (self.z + offset) % self.layers

    def greet(self, everyone):
        barrier = pltpu.get_barrier_semaphore()
        others = [(self.me, self.above(o)) for o in range(1, self.layers)]
        if everyone:
            others += [((self.me + o) % self.depth, self.z) for o in range(1, self.depth)]
        else:
            others += [(mate, self.z) for mate in (self.across, self.along, self.twin)]
        for other in others:
            pl.semaphore_signal(
                barrier, inc=1, device_id=other, device_id_type=pl.DeviceIdType.MESH
            )
        return lambda: pl.semaphore_wait(barrier, len(others))


def copy_to(source, target, sems, slot, device):
    copy = pltpu.make_async_remote_copy(
        src_ref=source,
        dst_ref=target,
        send_sem=sems.at[0, slot],
        recv_sem=sems.at[1, slot],
        device_id=device,
        device_id_type=pl.DeviceIdType.MESH,
    )
    copy.start()
    return copy


TWIN, LAYER, LINE = range(3)
LATENCY = (1.4, 2.7, 2.7)


class Turns:
    def __init__(self):
        self.pieces, self.begun, self.due = ([], [], [])
        self.now, self.free, self.open = (0.0, [0.0, 0.0, 0.0], [0.0, 0.0, 0.0])

    def add(self, piece):
        link, micros = piece[0][0][1:]
        self.pieces.append(piece)
        self.begun.append(0)
        self.due.append(max(self.now, self.open[link] - micros))
        self.open[link] = max(self.now, self.open[link]) + micros
        self.settle()
        return len(self.pieces) - 1

    def step(self, n):
        action, link, micros = self.pieces[n][0][self.begun[n]]
        action()
        self.begun[n] += 1
        self.free[link] = max(self.now, self.free[link]) + micros
        self.due[n] = self.free[link] + LATENCY[link]

    def live(self):
        return [n for n in range(len(self.pieces)) if not self.finished(n)]

    def settle(self):
        while True:
            due = [n for n in self.live() if self.due[n] <= self.now]
            if not due:
                return
            self.step(min(due, key=lambda n: (self.due[n], n)))

    def tick(self, micros):
        self.now += micros
        self.settle()

    def finished(self, n):
        return self.begun[n] == len(self.pieces[n][0])

    def run_until(self, *names):
        while not all(self.finished(n) for n in names):
            n = min(self.live(), key=lambda n: (self.due[n], n))
            self.now = max(self.now, self.due[n])
            self.step(n)

    def close(self):
        self.run_until(*range(len(self.pieces)))
        for _, copies in self.pieces:
            for copy in copies.values():
                copy.wait_send()


GATHER_SLOTS = 8
GATHER_RATES = (0.15, 0.09, 0.045, 0.03)


def gather_piece(spot, shard, whole, sems, begin, number):
    columns = shard.shape[1]
    half = number // 2
    copies = {}
    chip, core = (spot.chip, spot.core)
    lanes = at(spot.z, columns)

    def start(name, source, target, device):
        copies[name] = copy_to(source, target, sems, len(copies), device)

    def send_up():
        own = whole.at[chip, core, begin : begin + number, lanes]
        for o in range(1, spot.layers):
            start(("z", o), shard.at[begin : begin + number, :], own, (spot.me, spot.above(o)))
        whole[chip, core, begin : begin + number, lanes] = shard[begin : begin + number, :]

    def send_line():
        for o in range(1, spot.layers):
            copies["z", o].wait_recv()
        mine = whole.at[chip, core, begin : begin + number]
        start("across", mine, mine, (spot.across, spot.z))
        start("along", mine, mine, (spot.along, spot.z))

    def send_on():
        copies["across"].wait_recv()
        part = whole.at[spot.across // 2, core, begin : begin + half]
        start("corner along", part, part, (spot.along, spot.z))
        copies["along"].wait_recv()
        part = whole.at[spot.along // 2, core, begin + half : begin + number]
        start("corner across", part, part, (spot.across, spot.z))

    def send_twin():
        copies["corner along"].wait_recv()
        copies["corner across"].wait_recv()
        mine = whole.at[:, core, begin : begin + number]
        start("twin", mine, mine, (spot.twin, spot.z))

    def finish():
        copies["twin"].wait_recv()

    size = 1e-3 * number * columns * 2
    steps = [
        (send_up, LINE, GATHER_RATES[0] * size),
        (send_line, LAYER, GATHER_RATES[1] * size),
        (send_on, LAYER, GATHER_RATES[2] * size),
        (send_twin, TWIN, GATHER_RATES[3] * size),
        (finish, TWIN, 0.0),
    ]
    return (steps, copies)


def table_piece(spot, shard, whole, sems):
    columns = shard.shape[1]
    copies = {}

    def send_up():
        own = whole.at[:, at(spot.z, columns)]
        for o in range(1, spot.layers):
            copies[o] = copy_to(shard, own, sems, o - 1, (spot.me, spot.above(o)))
        whole[:, at(spot.z, columns)] = shard[...]

    def finish():
        for copy in copies.values():
            copy.wait_recv()

    return ([send_up, finish], copies)


def scatter_buffers(number, columns):
    return [
        shape((4, number, columns), bf16),
        shape((2, number // 2, columns), bf16),
        shape((2, number, columns), bf16),
        shape((3, number, columns // 4), bf16),
    ]


SCATTER_SLOTS = 11
SCATTER_RATES = (0.0008, 0.0013, 0.0026, 0.003)


def scatter_piece(spot, grad, keep, sums, corner, layer, lines, sems):
    number, columns = (grad.shape[0] // spot.depth, grad.shape[1])
    part = columns // spot.layers
    half = number // 2
    copies = {}

    def start(name, source, target, device):
        copies[name] = copy_to(source, target, sems, len(copies), device)

    def block(owner):
        return at(owner, number)

    def send_twin():
        for n in (3, 1, 2, 0):
            theirs = grad.at[block(spot.twin_mates[n]), :]
            start(("twin", n), theirs, sums.at[n], (spot.twin, spot.z))

    def add(target, first, size, *terms):
        total = terms[0].astype(f32)
        for term in terms[1:]:
            total = total + term.astype(f32)
        sums[target, first : first + size, :] = total.astype(bf16)

    def send_corner():
        for n in (3, 1, 2, 0):
            copies["twin", n].wait_recv()
            add(n, 0, number, grad[block(spot.mates[n]), :], sums[n])
            if n == 3:
                start("along", sums.at[3, :half], corner.at[0], (spot.along, spot.z))
                start("across", sums.at[3, half:], corner.at[1], (spot.across, spot.z))

    def send_layer():
        copies["along"].wait_recv()
        add(1, 0, half, sums[1, :half, :], corner[0])
        start("own across", sums.at[1], layer.at[0], (spot.across, spot.z))
        copies["across"].wait_recv()
        add(2, half, half, sums[2, half:, :], corner[1])
        start("own along", sums.at[2], layer.at[1], (spot.along, spot.z))

    def send_up():
        copies["own across"].wait_recv()
        copies["own along"].wait_recv()
        add(0, 0, number, sums[0], layer[0], layer[1])
        for o in range(1, spot.layers):
            theirs = sums.at[0, :, at(spot.above(o), part)]
            start(("z", o), theirs, lines.at[o - 1], (spot.me, spot.above(o)))

    def finish():
        total = sums[0, :, at(spot.z, part)].astype(f32)
        for o in range(1, spot.layers):
            copies["z", o].wait_recv()
            total = total + lines[o - 1].astype(f32)
        keep(total)

    size = 1e-3 * 8 * number * columns * 2
    steps = [
        (send_twin, TWIN, SCATTER_RATES[0] * size),
        (send_corner, LAYER, SCATTER_RATES[1] * size),
        (send_layer, LAYER, SCATTER_RATES[2] * size),
        (send_up, LINE, SCATTER_RATES[3] * size),
        (finish, TWIN, 0.0),
    ]
    return (steps, copies)


SMALL_SLOTS = 13


def small_piece(spot, vectors, states, keep, lines, layers, sems):
    high = vectors.shape[0]
    columns = vectors.shape[1] // spot.layers
    copies = {}

    def start(source, target, device):
        copies[len(copies)] = copy_to(source, target, sems, len(copies), device)

    def send_up():
        for o in range(1, spot.layers):
            above = spot.above(o)
            start(vectors.at[:, at(above, columns)], lines.at[spot.z, :high], (spot.me, above))
            start(states, lines.at[spot.z, high:], (spot.me, above))
        lines[spot.z, :high, :] = vectors[:, at(spot.z, columns)]
        lines[spot.z, high:, :] = states[...]

    def send_layer():
        for n in range(2 * spot.layers - 2):
            copies[n].wait_recv()
        total = lines[0]
        for n in range(1, spot.layers):
            total = total + lines[n]
        layers[spot.me] = total
        own = layers.at[spot.me]
        for o in range(1, spot.depth):
            start(own, own, ((spot.me + o) % spot.depth, spot.z))

    def finish():
        for n in range(2 * spot.layers - 2, len(copies)):
            copies[n].wait_recv()
        total = layers[0]
        for n in range(1, spot.depth):
            total = total + layers[n]
        keep(total)

    steps = [(send_up, LINE, 0.5), (send_layer, LAYER, 1.5), (finish, TWIN, 0.0)]
    return (steps, copies)


class Whole:
    def __init__(self, ref):
        chips, cores, rows, columns = ref.shape
        self.ref, self.block = (ref, cores * rows)
        self.shape = (chips * cores * rows, columns)

    def __getitem__(self, key):
        rows, columns = key if isinstance(key, tuple) else (slice(None), slice(None))
        if rows != slice(None):
            rows = slice(rows.start // self.block, rows.stop // self.block)
        value = self.ref[rows, :, :, columns]
        return value.reshape(-1, value.shape[-1])


class Refs:
    def __init__(self):
        self.copies, self.spilled = ({}, [])

    def later(self, *refs):
        return [Late(self, ref) for ref in refs]

    def fetch(self, *refs):
        return [late.start() for late in self.later(*refs)]

    def ready(self, *refs):
        for ref in refs:
            self.copies[id(ref)].wait()

    def spill(self, *refs):
        for ref in refs:
            self.copies[id(ref)].start()
            self.spilled.append(ref)


class Late:
    def __init__(self, r, ref):
        self.r, self.ref, self.here = (r, ref, False)
        self.shape, self.dtype = (ref.shape, ref.dtype)

    def start(self):
        self.r.copies[id(self.ref)].start()
        return self

    def land(self):
        if not self.here:
            self.r.ready(self.ref)
            self.here = True
        return self.ref

    def __getitem__(self, key):
        return self.land()[key]

    def __setitem__(self, key, value):
        self.land()[key] = value


NEAR, SCALAR, ANY, FAR = (pltpu.VMEM, pltpu.SMEM, pl.ANY, None)


def launch(body, inputs, outputs, scratch, collective=None, semaphores=None):
    operands = {**inputs, **outputs}
    names = list(operands)
    far = [name for name in names if operands[name][1] is FAR]
    semaphores = semaphores or {}

    def kernel(*refs):
        r = Refs()
        near = dict(zip(names, refs))
        rest = refs[len(names) :]
        buffers = dict(zip(far, rest))
        sems = rest[len(far)]
        rest = rest[len(far) + 1 :]
        for slot, name in enumerate(far):
            pair = (near[name], buffers[name])
            if name in outputs:
                pair = pair[::-1]
            r.copies[id(buffers[name])] = pltpu.make_async_copy(*pair, sems.at[slot])
        near.update(buffers)
        near.update(zip(list(scratch) + list(semaphores), rest))
        r.__dict__.update(near)
        body(r)
        r.ready(*r.spilled)

    def like(value):
        return pltpu.VMEM(value.shape, value.dtype)

    def specs(values):
        return [pl.BlockSpec(memory_space=ANY if p is FAR else p) for _, p in values.values()]

    results = pl.pallas_call(
        kernel,
        out_shape=[value for value, _ in outputs.values()],
        in_specs=specs(inputs),
        out_specs=specs(outputs),
        scratch_shapes=[like(operands[name][0]) for name in far]
        + [pltpu.SemaphoreType.DMA((max(1, len(far)),))]
        + [like(value) for value in scratch.values()]
        + [pltpu.SemaphoreType.DMA(dims) for dims in semaphores.values()],
        compiler_params=pltpu.CompilerParams(
            vmem_limit_bytes=VMEM_BYTES,
            collective_id=collective,
            has_side_effects=collective is not None,
        ),
    )(*[value for value, _ in inputs.values()])
    return dict(zip(outputs, results))


WEIGHTS = ("w1", "w2", "s1", "s2", "c1", "c2", "f1", "f2")


def under(prefix, values):
    return {prefix + str(n): value for n, value in enumerate(values)}


def held(r, prefix, number):
    return [r.__dict__[prefix + str(n)] for n in range(number)]


def scatter(r, spot, slot, name, keep):
    return scatter_piece(
        spot, r.__dict__[name], keep, *held(r, name + "_", 4), r.scatter_sems.at[slot]
    )


def piece_names(first):
    names = []
    for q in range(2):
        names.append(first + "2" + str(q))
        names += [
            first + "1" + str(half) + str(start) for half, start, _ in IN_PIECES if half == q
        ]
    return names


def scatter_halves(r, spot, slot, first, turns, after=idle):
    ins, outs = (r.__dict__[first + "1_out"], r.__dict__[first + "2_out"])
    names = piece_names(first)
    plans = {first + "1" + str(half) + str(start): (half, start) for half, start, _ in IN_PIECES}

    def ready(n):
        if n == len(names):
            return after()
        name = names[n]

        def keep_out(total):
            q = int(name[-1])
            outs[q * LANES : (q + 1) * LANES, :] = total

        def keep_in(total):
            half, start = plans[name]
            for part in range(total.shape[1] // LANES):
                begin = (2 * (start + part) + half) * LANES
                ins[:, begin : begin + LANES] = total[:, part * LANES : (part + 1) * LANES]

        turns.add(scatter(r, spot, slot + n, name, keep_in if name in plans else keep_out))

    return ready


def half_pieces(width, hidden_width):
    half = hidden_width // 2
    ins = [shape((width, half // every), bf16) for _, _, every in IN_PIECES]
    return (ins, [shape((half, width), bf16)] * 2)


def half_scratch(first, width, hidden_width):
    ins, outs = half_pieces(width, hidden_width)
    scratch = {}
    for name in piece_names(first):
        grad = ins.pop(0) if name[1] == "1" else outs.pop(0)
        scratch[name] = grad
        scratch.update(under(name + "_", scatter_buffers(grad.shape[0] // 8, grad.shape[1])))
    return scratch


def half_refs(r, first):
    names = piece_names(first)
    ins = [r.__dict__[name] for name in names if name[1] == "1"]
    return (ins, [r.__dict__[name] for name in names if name[1] == "2"])


def fast_layer(frames, lengths, vectors, states_in, weights, cotangent):
    count, length, width = frames.shape
    rows = count * length
    tiles = width // LANES
    hidden_width = weights[0].shape[1] * 4
    heads, states = states_in[0].shape
    flat = frames.reshape(rows, width)
    row = shape((rows, width), bf16)
    row_f = shape((rows, width), f32)
    wide_row = shape((rows, hidden_width), bf16)
    scales = shape((rows, 1), f32)
    mixes = shape((tiles, length, count * LANES), bf16)
    band = shape((tiles, 2 * TILE, length), bf16)
    padded = shape((count * tiles, length + 2 * EDGE, LANES), f32)
    power = shape((4, heads * states, LANES), f32)
    whole_table = shape((TABLE, width), f32)
    bases = (F1, SS, CV, F2)
    decay, freq, real, imag = states_in

    def gathered(w):
        return shape((4, 2, w.shape[0], 4 * w.shape[1]), bf16)

    cuts = (2, 2, 1, 1, 1, 1, 2, 2)

    def forward(r):
        r.fetch(r.frames)
        spot = Place()
        greeted = spot.greet(False)
        r.shard[...] = jnp.zeros_like(r.shard)
        for ref, base in zip(held(r, "vec", 4), bases):
            r.shard[base : base + ref.shape[0], :] = ref[...].astype(f32)
        greeted()
        turns = Turns()
        place = {}
        for name, cut, shard in zip(WEIGHTS, cuts, held(r, "shard", 8)):
            size = shard.shape[0] // cut
            place[name] = []
            for q in range(cut):
                sems = r.gather_sems.at[len(turns.pieces)]
                piece = gather_piece(spot, shard, r.__dict__[name], sems, q * size, size)
                place[name].append(turns.add(piece))
        vector_steps, vector_copies = table_piece(spot, r.shard, r.table, r.table_sems)
        tick = turns.tick
        vector_steps[0]()
        build_bands(r.decay, r.freq, r.real, r.imag, r.powers, r.wide, r.wide_t, length, tick)
        r.spill(r.powers, r.wide_t)
        vector_steps[1]()

        def need(*wanted):
            for name in wanted:
                turns.run_until(*place[name])
                r.spill(r.__dict__[name])
            return [Whole(r.__dict__[name]) for name in wanted]

        first = need(*WEIGHTS[:2])
        r.ready(r.frames)
        ffn1_forward(count, r.frames, r.table, *first, r.hidden, r.before, tick)
        r.spill(r.before)
        mixer = need(*WEIGHTS[2:4])
        ssm_forward(
            count, r.hidden, r.table, *mixer, r.wide, r.s_normed, r.s_scale, r.s_value, r.s_gate,
            r.s_state, r.gated, tick,
        )
        r.spill(r.s_normed, r.s_scale, r.s_value, r.s_gate, r.s_state)
        module = need(*WEIGHTS[4:6])
        conv_forward(
            count, r.hidden, r.lengths, r.table, *module, r.c_normed, r.c_scale, r.c_linear,
            r.c_gate, r.c_depth, r.glu, r.gated, tick,
        )
        r.spill(r.hidden, r.c_normed, r.c_scale, r.c_linear, r.c_gate, r.c_depth)
        need(*WEIGHTS[6:])
        turns.close()
        for copy in vector_copies.values():
            copy.wait_send()

    saved = launch(
        forward,
        dict(
            frames=(flat, FAR), lengths=(lengths, SCALAR), decay=(decay, NEAR), freq=(freq, NEAR),
            real=(real, NEAR), imag=(imag, NEAR), **under("vec", [(v, NEAR) for v in vectors]),
            **under("shard", [(w, NEAR) for w in weights]),
        ),
        dict(
            table=(whole_table, NEAR), hidden=(row_f, FAR), before=(wide_row, FAR),
            powers=(power, FAR), wide_t=(band, FAR), s_normed=(row, FAR), s_scale=(scales, FAR),
            s_value=(mixes, FAR), s_gate=(mixes, FAR), s_state=(mixes, FAR), c_normed=(row, FAR),
            c_scale=(scales, FAR), c_linear=(row, FAR), c_gate=(row, FAR), c_depth=(row, FAR),
            **{name: (gathered(w), FAR) for name, w in zip(WEIGHTS, weights)},
        ),
        dict(shard=shape((TABLE, LANES), f32), wide=band, gated=row, glu=padded),
        0,
        dict(gather_sems=(sum(cuts), 2, GATHER_SLOTS), table_sems=(2, 3)),
    )
    shards = {}
    for name, w in zip(WEIGHTS, weights):
        saved[name] = saved[name].reshape(8 * w.shape[0], 4 * w.shape[1])
        shards[name + "_out"] = (shape(w.shape, f32), NEAR)
    kept = {name: (value, FAR) for name, value in saved.items()}
    table = (saved["table"], NEAR)

    def some(values, *prefixes):
        return {name: value for name, value in values.items() if name.startswith(prefixes)}

    half_width = hidden_width // 2
    square, double = (shape((width, width), bf16), shape((width, 2 * width), bf16))
    half_row = shape((rows, half_width), bf16)

    def later(r):
        spot = Place()
        greeted = spot.greet(False)
        hidden, f1, f2, cot = r.fetch(r.hidden, r.f1, r.f2, r.cot)
        conv_in = r.later(r.c2, r.c_normed, r.c_scale, r.c_linear, r.c_gate, r.c_depth, r.c1)

        def start():
            greeted()
            for late in conv_in:
                late.start()

        turns = Turns()
        tick = turns.tick
        ffn2_both(
            count, hidden, cot, r.lengths, r.table, f1, f2, cot, hidden, *half_refs(r, "f"),
            r.f_vec, r.normed, r.scale, r.before, r.normal, r.branch, r.active, tick,
            scatter_halves(r, spot, 0, "f", turns), start,
        )
        save_output = pltpu.make_async_copy(r.cot, r.output, r.save_sems.at[1])
        save_output.start()
        c2, *kept_in, c1 = [late.land() for late in conv_in]
        conv_backward(
            count, r.lengths, r.table, c1, c2, *kept_in, r.hidden, r.c1_grad, r.c2_grad,
            r.c_vec, r.normal, r.branch, r.active.at[:, :width], r.depth_grad, r.tap_grads,
            r.mixed, tick,
        )
        r.spill(r.c1_grad, r.c2_grad)
        save = pltpu.make_async_copy(r.hidden, r.grad, r.save_sems.at[0])
        save.start()
        turns.close()
        save.wait()
        save_output.wait()

    two = launch(
        later,
        dict(
            cot=(cotangent.reshape(rows, width), FAR), lengths=(lengths, SCALAR), table=table,
            **some(kept, "hidden", "f", "c"),
        ),
        dict(
            output=(row, ANY), grad=(row_f, ANY), c1_grad=(double, FAR), c2_grad=(square, FAR),
            f_vec=(shape((TABLE - F2, width), f32), NEAR),
            c_vec=(shape((F2 - CV, width), f32), NEAR), **some(shards, "f"),
        ),
        dict(
            normed=row, scale=scales, before=wide_row, normal=row, branch=row, mixed=half_row,
            active=half_row, depth_grad=padded, tap_grads=shape((CONV_TAPS, 8, LANES), f32),
            **half_scratch("f", width, hidden_width),
        ),
        1,
        dict(scatter_sems=(5, 2, SCATTER_SLOTS), save_sems=(2,)),
    )

    def last(r):
        spot = Place()
        greeted = spot.greet(True)
        grad, s2, *kept_in = r.fetch(
            r.grad, r.s2, r.s_normed, r.s_scale, r.s_value, r.s_gate, r.s_state, r.c1g, r.c2g
        )
        wide_t, s1, frames, w2, before, w1, powers = r.later(
            r.wide_t, r.s1, r.frames, r.w2, r.before, r.w1, r.powers
        )
        r.vectors[...] = jnp.zeros_like(r.vectors)
        r.vectors[CV:F2, :] = r.c_vec[...]
        r.vectors[F2:, :] = r.f_vec[...]
        turns = Turns()
        tick = turns.tick

        def send(name, slot, out):
            def keep(total):
                out[...] = total

            turns.add(scatter(r, spot, slot, name, keep))

        def start():
            for late in (wide_t, s1, frames, w2, before, w1, powers):
                late.start()
            for late in kept_in[-2:]:
                late.land()
            greeted()
            send("c1g", 0, r.c1_out)
            send("c2g", 1, r.c2_out)

        ssm_backward(
            count, r.table, s1, s2, wide_t, *kept_in[:-2], grad, r.s1g, r.s2g,
            r.vectors.at[SS:CV], r.kernel_grad, r.normal, r.branch, r.time_grad,
            r.active.at[:, :width], r.mixed, tick, start,
        )
        send("s1g", 2, r.s1_out)
        send("s2g", 3, r.s2_out)

        def after():
            state_grads(r.kernel_grad[...], powers, r.decay, r.real, r.imag, r.states)
            tick(2.0)

        ffn1_backward(
            count, frames, r.grad, r.table, w1, w2, before, r.normal, *half_refs(r, "w"),
            r.vectors.at[F1:SS], r.normal, r.branch, r.active, tick,
            scatter_halves(r, spot, 4, "w", turns, after),
        )
        save = pltpu.make_async_copy(r.normal, r.frames_grad, r.save_sems.at[0])
        save.start()

        def keep(total):
            r.small[...] = total

        turns.add(
            small_piece(spot, r.vectors, r.states, keep, r.lines, r.layers, r.small_sems)
        )
        turns.close()
        save.wait()

    small = shape((TABLE + 4 * heads, LANES), f32)
    sent = dict(c1g=double, c2g=square, s1g=double, s2g=square)
    arriving = {}
    for name, grad in sent.items():
        arriving.update(under(name + "_", scatter_buffers(grad.shape[0] // 8, grad.shape[1])))
    three = launch(
        last,
        dict(
            frames=(flat, FAR), grad=(two["grad"], FAR), c1g=(two["c1_grad"], FAR),
            c2g=(two["c2_grad"], FAR), table=table, c_vec=(two["c_vec"], NEAR),
            f_vec=(two["f_vec"], NEAR), decay=(decay, NEAR), real=(real, NEAR), imag=(imag, NEAR),
            **some(kept, "s", "w", "powers", "before"),
        ),
        dict(frames_grad=(row, ANY), small=(small, NEAR), **some(shards, "w", "s", "c")),
        dict(
            s1g=double, s2g=square, states=shape((4 * heads, LANES), f32), normal=row, branch=row,
            mixed=half_row, active=half_row, time_grad=mixes, vectors=whole_table,
            kernel_grad=shape((heads, length), f32), lines=shape((4,) + small.shape, f32),
            layers=shape((8,) + small.shape, f32), **half_scratch("w", width, hidden_width),
            **arriving,
        ),
        2,
        dict(
            scatter_sems=(9, 2, SCATTER_SLOTS), small_sems=(2, SMALL_SLOTS), save_sems=(1,)
        ),
    )

    done = [(two if name[0] == "f" else three)[name + "_out"] for name in WEIGHTS]

    def finish(r):
        for target, value in zip(held(r, "out", 8), held(r, "in", 8)):
            target[...] = value[...]
        for base, target in zip(bases, held(r, "vec", 4)):
            target[...] = r.small[base : base + target.shape[0], :]
        for n, target in enumerate(held(r, "st", 4)):
            begin = TABLE + n * heads
            target[...] = r.small[begin : begin + heads, :states]
        r.frames_end[...] = r.frames_grad[...]

    end = launch(
        finish,
        dict(
            small=(three["small"], NEAR), frames_grad=(three["frames_grad"], NEAR),
            **under("in", [(value, NEAR) for value in done]),
        ),
        dict(
            frames_end=(row, NEAR),
            **under("out", [(shape(value.shape, f32), NEAR) for value in done]),
            **under("vec", [(shape(v.shape, f32), NEAR) for v in vectors]),
            **under("st", [(shape((heads, states), f32), NEAR)] * 4),
        ),
        {},
    )
    frames_end, *outs = end.values()
    vec, state_grads_out = (outs[8:12], outs[12:])
    return (
        (two["output"].reshape(frames.shape), frames_end.reshape(frames.shape))
        + (outs[0], outs[1], vec[0], outs[2], outs[3], vec[1])
        + tuple(state_grads_out)
        + (outs[4], outs[5], vec[2], outs[6], outs[7], vec[3])
    )


def body(
    frames,
    lengths,
    ffn1_in,
    ffn1_out,
    ffn1_vec,
    ssm_in,
    ssm_out,
    ssm_vec,
    decay,
    freq,
    coef_re,
    coef_im,
    conv_in,
    conv_out,
    conv_vec,
    ffn2_in,
    ffn2_out,
    ffn2_vec,
    cotangent,
):
    count, length, width = frames.shape
    rows = count * length
    tiles = width // LANES
    hidden_width = width * (ffn1_vec.shape[0] - 3)
    heads, states = decay.shape
    flat = frames.reshape(rows, width)

    vectors = (ffn1_vec, ssm_vec, conv_vec, ffn2_vec)
    states_in = (decay, freq, coef_re, coef_im)
    weights = (ffn1_in, ffn1_out, ssm_in, ssm_out, conv_in, conv_out, ffn2_in, ffn2_out)
    if (lax.axis_size("dp"), lax.axis_size("fsdp")) == (8, 4):
        return fast_layer(frames, lengths, vectors, states_in, weights, cotangent)

    def pad(vec, to):
        return jnp.pad(vec.astype(f32), ((0, to - vec.shape[0]), (0, 0)))

    table = jnp.concatenate(
        [pad(ffn1_vec, SS - F1), pad(ssm_vec, CV - SS), pad(conv_vec, F2 - CV), pad(ffn2_vec, TABLE - F2)], 0
    )
    table = lax.all_gather(table, "fsdp", axis=1, tiled=True)
    weights = [whole for n in range(0, 8, 2) for whole in bring(weights[n], weights[n + 1])]
    first_in, first_out, mixer_in, mixer_out = weights[:4]
    module_in, module_out, second_in, second_out = weights[4:]

    row = shape((rows, width), bf16)
    row_f = shape((rows, width), f32)
    wide_row = shape((rows, hidden_width), bf16)
    scales = shape((rows, 1), f32)
    mixes = shape((tiles, length, count * LANES), bf16)
    band = shape((tiles, 2 * TILE, length), bf16)
    padded = shape((count * tiles, length + 2 * EDGE, LANES), f32)
    square = shape((width, width), bf16)
    double = shape((width, 2 * width), bf16)
    half_row = shape((rows, hidden_width // 2), bf16)
    power = shape((4, heads * states, LANES), f32)

    hidden, before = call(
        partial(ffn1_forward, count), [row_f, wide_row], [], (), flat, table, first_in, first_out
    )

    def mixer_kernel(
        hidden_in, table, weight_in, weight_out, decay, freq, re, im, hidden, normed, scale, value,
        gate, state, powers, wide_t, wide, gated,
    ):
        hidden[...] = hidden_in[...]
        build_bands(decay, freq, re, im, powers, wide, wide_t, length)
        ssm_forward(
            count, hidden, table, weight_in, weight_out, wide, normed, scale, value, gate, state,
            gated,
        )

    hidden, mixer_normed, mixer_scale, value, gate, state, powers, wide_t = call(
        mixer_kernel, [row_f, row, scales, mixes, mixes, mixes, power, band], [band, row], (),
        hidden, table, mixer_in, mixer_out, decay, freq, coef_re, coef_im,
    )

    def module_kernel(hidden_in, lengths, table, weight_in, weight_out, hidden, *rest):
        hidden[...] = hidden_in[...]
        conv_forward(count, hidden, lengths, table, weight_in, weight_out, *rest)

    hidden, module_normed, module_scale, linear, module_gate, depth = call(
        module_kernel, [row_f, row, scales, row, row, row], [padded, row], (1,),
        hidden, lengths, table, module_in, module_out,
    )

    ins, outs = half_pieces(width, hidden_width)
    number = len(ins)

    def second_kernel(hidden, cot, lengths, table, w_in, w_out, output, grad, *rest):
        ffn2_both(
            count, hidden, cot, lengths, table, w_in, w_out, output, grad, rest[:number],
            rest[number : number + 2], *rest[number + 2 :],
        )

    output, grad, *second_grads, second_vec = call(
        second_kernel,
        [row, row_f, *ins, *outs, shape((TABLE - F2, width), f32)],
        [row, scales, wide_row, row, row, half_row],
        (2,), hidden, cotangent.reshape(rows, width), lengths, table, second_in, second_out,
    )

    def module_back(grad_in, lengths, table, w_in, w_out, normed, scale, linear, gate, depth, grad, *rest):
        grad[...] = grad_in[...]
        conv_backward(
            count, lengths, table, w_in, w_out, normed, scale, linear, gate, depth, grad, *rest
        )

    grad, module_in_grad, module_out_grad, module_vec = call(
        module_back,
        [row_f, double, square, shape((F2 - CV, width), f32)],
        [
            row, row, row, padded, shape((CONV_TAPS, 8, LANES), f32),
            shape((rows, 2 * width), bf16),
        ],
        (1,), grad, lengths, table, module_in, module_out, module_normed, module_scale, linear,
        module_gate, depth,
    )

    def mixer_back(
        grad_in, table, w_in, w_out, wide_t, powers, decay, re, im, normed, scale, value, gate,
        state, grad, in_grad, out_grad, vec_grad, states, *rest,
    ):
        grad[...] = grad_in[...]
        ssm_backward(
            count, table, w_in, w_out, wide_t, normed, scale, value, gate, state, grad, in_grad,
            out_grad, vec_grad, *rest,
        )
        state_grads(rest[0][...], powers, decay, re, im, states)

    grad, mixer_in_grad, mixer_out_grad, mixer_vec, state_grad = call(
        mixer_back,
        [row_f, double, square, shape((CV - SS, width), f32), shape((4 * heads, LANES), f32)],
        [
            shape((heads, length), f32), row, row, mixes, row, shape((rows, 2 * width), bf16),
        ],
        (), grad, table, mixer_in, mixer_out, wide_t, powers, decay, coef_re, coef_im,
        mixer_normed, mixer_scale, value, gate, state,
    )

    def first_back(frames, grad, table, w_in, w_out, kept, out, *rest):
        *rest, before = rest
        before[...] = kept[...]
        ffn1_backward(
            count, frames, grad, table, w_in, w_out, before, out, rest[:number],
            rest[number : number + 2], *rest[number + 2 :],
        )

    frames_grad, *first_grads, first_vec = call(
        first_back,
        [row, *ins, *outs, shape((SS - F1, width), f32)],
        [row, row, half_row, wide_row],
        (), flat, grad, table, first_in, first_out, before,
    )
    vec_grads = jnp.concatenate([first_vec, mixer_vec, module_vec, second_vec], 0)

    def join(in_a, *parts):
        wide = [part.reshape(width, -1, LANES) for part in (in_a,) + parts[:2]]
        wide = [wide[0], jnp.stack(wide[1:], 2).reshape(width, -1, LANES)]
        tall = [part.reshape(-1, LANES, width) for part in parts[2:]]
        return (
            jnp.stack(wide, 2).reshape(width, hidden_width),
            jnp.stack(tall, 1).reshape(hidden_width, width),
        )

    grads = (
        *join(*first_grads), mixer_in_grad, mixer_out_grad, module_in_grad, module_out_grad,
        *join(*second_grads),
    )
    vec_grads = lax.psum(
        lax.psum_scatter(vec_grads, "fsdp", scatter_dimension=1, tiled=True), "dp"
    )
    state_grad = lax.psum(state_grad, ("dp", "fsdp"))
    grads = [send(grad) for grad in grads]
    state_grad = state_grad[:, :states].reshape(4, heads, states)

    def layer(number, base, like):
        return (grads[number], grads[number + 1], vec_grads[base : base + like.shape[0]])

    return (
        (output.reshape(count, length, width), frames_grad.reshape(count, length, width))
        + layer(0, F1, ffn1_vec)
        + layer(2, SS, ssm_vec)
        + tuple(state_grad[n] for n in range(4))
        + layer(4, CV, conv_vec)
        + layer(6, F2, ffn2_vec)
    )


def solution(mesh):
    split = P(("dp", "fsdp"), None, None)
    weight = P("dp", "fsdp")
    vector = P(None, "fsdp")
    layer = (weight, weight, vector)
    whole = (P(), P(), P(), P())
    in_specs = (split, P(("dp", "fsdp"))) + layer + layer + whole + layer + layer + (split,)
    out_specs = (split, split) + layer + layer + whole + layer + layer
    return jax.shard_map(body, mesh=mesh, in_specs=in_specs, out_specs=out_specs, check_vma=False)
```

```python
from functools import partial

import jax
import jax.numpy as jnp
from jax import lax
from jax.experimental import pallas as pl
from jax.experimental.pallas import tpu as pltpu
from jax.sharding import PartitionSpec as P

EPSILON = 1e-05
VMEM_BYTES = 62 * 2**20
LANES = 128
TILE = 256
EDGE = 8
F1, SS, CV, F2 = (0, 8, 16, 40)
TABLE = 56
f32 = jnp.float32
bf16 = jnp.bfloat16


def dot(left, right):
    return jnp.dot(left, right, preferred_element_type=f32)


def dot_nt(left, right):
    return lax.dot_general(left, right, (((1,), (1,)), ((), ())), preferred_element_type=f32)


def dot_tn(left, right):
    return lax.dot_general(left, right, (((0,), (0,)), ((), ())), preferred_element_type=f32)


def loop(number, step):
    def turn(index, carry):
        step(index)
        return carry

    lax.fori_loop(0, number, turn, 0)


def at(index, size):
    if isinstance(index, int):
        return slice(index * size, (index + 1) * size)
    return pl.ds(pl.multiple_of(index * size, size), size)


def idle(micros=0.0):
    pass


def steps_of(number, step, tick, micros):
    if tick is idle:
        loop(number, step)
    else:
        for index in range(number):
            step(index)
            tick(micros)


def norm(hidden):
    center = hidden - jnp.mean(hidden, -1, keepdims=True)
    scale = lax.rsqrt(jnp.mean(center * center, -1, keepdims=True) + EPSILON)
    return (center * scale, scale)


def norm_back(grad, normed, scale, gain):
    scaled = grad * gain
    centered = (
        scaled
        - jnp.mean(scaled, -1, keepdims=True)
        - normed * jnp.mean(scaled * normed, -1, keepdims=True)
    )
    return (
        scale * centered,
        jnp.sum(grad * normed, 0, keepdims=True),
        jnp.sum(grad, 0, keepdims=True),
    )


def frame_mask(length, valid):
    return (lax.broadcasted_iota(jnp.int32, (length, 1), 0) < valid).astype(f32)


def identity(size):
    return lax.broadcasted_iota(jnp.int32, (size, size), 0) == lax.broadcasted_iota(
        jnp.int32, (size, size), 1
    )


def state_column(values):
    heads, states = values.shape
    eye = identity(states)
    columns = [
        jnp.sum(
            jnp.where(eye, jnp.broadcast_to(values[h : h + 1, :], (states, states)), 0.0),
            1,
            keepdims=True,
        )
        for h in range(heads)
    ]
    return jnp.concatenate(columns, 0)


def state_rows(column, heads):
    states = column.shape[0] // heads
    eye = identity(states)
    rows = [
        jnp.sum(
            jnp.where(
                eye,
                jnp.broadcast_to(column[h * states : (h + 1) * states, :], (states, states)),
                0.0,
            ),
            0,
            keepdims=True,
        )
        for h in range(heads)
    ]
    return jnp.concatenate(rows, 0)


def head_steps(heads, states):
    row = lax.broadcasted_iota(jnp.int32, (heads * states, 1), 0)
    log_steps = jnp.full((heads * states, 1), -6.9, f32)
    for h in range(1, heads):
        log_steps = jnp.where(row >= h * states, -6.9 + 4.6 * h / (heads - 1), log_steps)
    return jnp.exp(log_steps)


def state_powers(decay, freq, step, stride):
    places = lax.broadcasted_iota(jnp.int32, (1, LANES), 1).astype(f32) * float(stride)
    damping = jnp.exp(-(step * decay) * places)
    phase = (step * freq) * places
    return (damping * jnp.cos(phase), damping * jnp.sin(phase))


def build_bands(decay_ref, freq_ref, re_ref, im_ref, powers, wide, wide_t, length, tick=idle):
    heads, states = decay_ref.shape
    step = head_steps(heads, states)
    decay, freq = (state_column(decay_ref[...]), state_column(freq_ref[...]))
    real, imag = (state_column(re_ref[...]), state_column(im_ref[...]))
    near_re, near_im = state_powers(decay, freq, step, 1)
    far_re, far_im = state_powers(decay, freq, step, LANES)
    powers[0], powers[1], powers[2], powers[3] = (near_re, near_im, far_re, far_im)
    lead_re = real * far_re - imag * far_im
    lead_im = real * far_im + imag * far_re
    blocks = length // LANES
    pieces = []
    for a in range(blocks):
        term = lead_re[:, a : a + 1] * near_re - lead_im[:, a : a + 1] * near_im
        pieces.append(jnp.sum(term.reshape(heads, states, LANES), 1))
    root = jnp.sqrt(step / states)
    factor = jnp.concatenate([root[h * states : h * states + 1, :] for h in range(heads)], 0)
    low = [(piece * factor).astype(bf16) for piece in pieces]
    turn = (
        lax.broadcasted_iota(jnp.int32, (LANES, LANES), 0)
        + lax.broadcasted_iota(jnp.int32, (LANES, LANES), 1)
        == LANES - 1
    ).astype(bf16)
    ring = length + TILE
    zeros = jnp.zeros((heads, TILE), f32)
    forward = jnp.concatenate([piece.astype(f32) for piece in low] + [zeros], 1)
    backward = jnp.concatenate([dot(piece, turn) for piece in low[::-1]] + [zeros], 1)
    backward = pltpu.roll(backward, ring - (TILE - 1), 1)
    tick(9.0)
    for source, band in ((backward, wide), (forward, wide_t)):
        for h in range(heads):
            if h == heads // 2:
                tick(9.0)
            row = jnp.broadcast_to(source[h : h + 1, :], (8, ring))
            base = pltpu.roll(row, 0, 1, stride=1, stride_axis=0)
            for g in range(0, LANES // 8, 2):
                pair = jnp.concatenate(
                    [pltpu.roll(base, 8 * g, 1), pltpu.roll(base, 8 * g + 8, 1)], 0
                )
                for q in range(TILE // LANES):
                    if q == 0:
                        cut = pair[:, :length]
                    else:
                        cut = jnp.concatenate(
                            [pair[:, ring - q * LANES :], pair[:, : length - q * LANES]], 1
                        )
                    place = (h % 2) * TILE + q * LANES + 8 * g
                    band[h // 2, place : place + 16, :] = cut.astype(bf16)
        tick(9.0)


def state_grads(kernel_grad, powers, decay_ref, re_ref, im_ref, out):
    heads, states = decay_ref.shape
    step = head_steps(heads, states)
    real, imag = (state_column(re_ref[...]), state_column(im_ref[...]))
    near_re, near_im, far_re, far_im = (powers[0], powers[1], powers[2], powers[3])
    length = kernel_grad.shape[1]
    zero_re = zero_im = one_re = one_im = None
    for a in range(length // LANES):
        block = kernel_grad[:, a * LANES : (a + 1) * LANES]
        spread = jnp.concatenate(
            [jnp.broadcast_to(block[h : h + 1, :], (states, LANES)) for h in range(heads)], 0
        )
        term_re, term_im = (far_re[:, a : a + 1] * spread, far_im[:, a : a + 1] * spread)
        if a == 0:
            zero_re, zero_im = (term_re, term_im)
            one_re, one_im = (jnp.zeros_like(term_re), jnp.zeros_like(term_im))
        else:
            zero_re, zero_im = (zero_re + term_re, zero_im + term_im)
            one_re, one_im = (one_re + a * LANES * term_re, one_im + a * LANES * term_im)
    places = lax.broadcasted_iota(jnp.int32, (1, LANES), 1).astype(f32)
    one_re, one_im = (one_re + places * zero_re, one_im + places * zero_im)

    def close(left_re, left_im):
        return (
            jnp.sum(near_re * left_re - near_im * left_im, 1, keepdims=True),
            jnp.sum(near_re * left_im + near_im * left_re, 1, keepdims=True),
        )

    plain_re, plain_im = close(zero_re, zero_im)
    place_re, place_im = close(one_re, one_im)
    scale = jnp.sqrt(step / states)
    columns = (
        -step * scale * (real * place_re - imag * place_im),
        -step * scale * (real * place_im + imag * place_re),
        scale * plain_re,
        -scale * plain_im,
    )
    out[...] = jnp.zeros_like(out)
    for number, column in enumerate(columns):
        out[number * heads : (number + 1) * heads, :states] = state_rows(column, heads)


def swish(value):
    sig = jax.nn.sigmoid(value)
    out = value * sig
    return (out, sig + out * (1.0 - sig))


def feed_forward(normal, weight_in, weight_out, table, base, active_ref, slope_ref, rows):
    width = normal.shape[1]
    total = None
    for c in range(weight_in.shape[1] // width):
        part = slice(c * width, (c + 1) * width)
        value = dot(normal, weight_in[:, part]) + table[base + 2 + c : base + 3 + c, :]
        active, slope = swish(value)
        active = active.astype(bf16)
        active_ref[rows, part] = active
        slope_ref[rows, part] = slope.astype(bf16)
        term = dot(active, weight_out[part, :])
        total = term if total is None else total + term
    return total


def ffn1_forward(
    count, frames, table, weight_in, weight_out, hidden, active, slope, tick=idle
):
    length = frames.shape[0] // count
    blocks = weight_in.shape[1] // weight_in.shape[0]

    def step(u):
        rows = at(u, length)
        value = frames[rows, :].astype(f32)
        normed, _ = norm(value)
        normal = (normed * table[F1 : F1 + 1, :] + table[F1 + 1 : F1 + 2, :]).astype(bf16)
        total = feed_forward(normal, weight_in, weight_out, table, F1, active, slope, rows)
        bias = table[F1 + 2 + blocks : F1 + 3 + blocks, :]
        hidden[rows, :] = value + 0.5 * (total + bias)

    steps_of(count, step, tick, 4.0)


def head_lanes():
    return lax.broadcasted_iota(jnp.int32, (1, 2 * LANES), 1) % LANES < LANES // 2


def ssm_forward(
    count, hidden, table, weight_in, weight_out, wide, normed_ref, scale_ref, value_ref, swish_ref,
    side_ref, gated, tick=idle,
):
    total_rows, width = hidden.shape
    length = total_rows // count
    tiles = width // LANES

    def enter(u):
        rows = at(u, length)
        lanes = at(u, LANES)
        normed, scale = norm(hidden[rows, :])
        normed_ref[rows, :] = normed.astype(bf16)
        scale_ref[rows, :] = scale
        normal = (normed * table[SS : SS + 1, :] + table[SS + 1 : SS + 2, :]).astype(bf16)
        value = dot(normal, weight_in[:, :width]).astype(bf16)
        gate = dot(normal, weight_in[:, width:]).astype(bf16)
        for j in range(tiles):
            part = slice(j * LANES, (j + 1) * LANES)
            value_ref[j, :, lanes] = value[:, part]
            side_ref[j, :, lanes] = gate[:, part]

    steps_of(count, enter, tick, 1.5)
    first = head_lanes()
    steps = length // TILE
    for j in range(tiles):
        part = slice(j * LANES, (j + 1) * LANES)
        skip = table[SS + 2 : SS + 3, part]
        skip = jnp.concatenate([skip, skip], 1)
        for i in range(steps):
            rows = slice(i * TILE, (i + 1) * TILE)
            both = dot(wide[j, :, (steps - 1 - i) * TILE :], value_ref[j, : (i + 1) * TILE, :])
            mixed = jnp.where(first, both[:TILE], both[TILE:])
            gate, slope = swish(side_ref[j, rows, :].astype(f32))
            state = mixed + skip * value_ref[j, rows, :].astype(f32)
            swish_ref[j, rows, :] = gate.astype(bf16)
            side_ref[j, rows, :] = (state * slope).astype(bf16)
            out = (state * gate).astype(bf16)
            for u in range(count):
                gated[u * length + i * TILE : u * length + (i + 1) * TILE, part] = out[
                    :, u * LANES : (u + 1) * LANES
                ]
        if j % 2:
            tick(1.2)

    def leave(u):
        rows = at(u, length)
        hidden[rows, :] += dot(gated[rows, :], weight_out[...])

    loop(count, leave)
    tick(1.0)


def clear_edges(padded, length):
    number, _, lanes = padded.shape
    zeros = jnp.zeros((number, EDGE, lanes), f32)
    padded[:, :EDGE, :] = zeros
    padded[:, EDGE + length :, :] = zeros


ROWS, GROUP = (64, 4)


def conv_rows(n, base):
    first = pl.multiple_of(n * (ROWS * GROUP), ROWS * GROUP)
    for g in range(GROUP):
        begin = first + g * ROWS
        yield begin, pl.ds(pl.multiple_of(base + begin, 32), ROWS)


def shifted(padded, index, begin):
    for b in range(8):
        near = padded[index, pl.ds(begin + b + EDGE - 8, ROWS + 8), :]
        yield b - 8, near[:ROWS]
        yield b, near[8:]


def conv_forward(
    count, hidden, lengths, table, weight_in, weight_out, normed_ref, scale_ref, glu_ref, gate_ref,
    side_ref, slope_ref, active, glu, tick=idle,
):
    total_rows, width = hidden.shape
    length = total_rows // count
    tiles = width // LANES
    clear_edges(glu, length)

    def enter(u):
        rows = at(u, length)
        normed, scale = norm(hidden[rows, :])
        normed_ref[rows, :] = normed.astype(bf16)
        scale_ref[rows, :] = scale
        normal = (normed * table[CV : CV + 1, :] + table[CV + 1 : CV + 2, :]).astype(bf16)
        linear = dot(normal, weight_in[:, :width])
        sig = jax.nn.sigmoid(dot(normal, weight_in[:, width:]))
        gate = sig * frame_mask(length, lengths[u])
        value = linear * gate
        glu_ref[rows, :] = value.astype(bf16)
        gate_ref[rows, :] = gate.astype(bf16)
        side_ref[rows, :] = (value * (1.0 - sig)).astype(bf16)
        for j in range(tiles):
            glu[u * tiles + j, EDGE : EDGE + length, :] = value[:, j * LANES : (j + 1) * LANES]

    steps_of(count, enter, tick, 1.7)
    number = CONV_TAPS

    def convolve(index):
        u, j = (index // tiles, index % tiles)
        lanes = at(j, LANES)
        taps = [table[CV + 2 + t : CV + 3 + t, lanes] for t in range(number)]

        def block(n):
            for begin, rows in conv_rows(n, u * length):
                total = None
                for shift, moved in shifted(glu, index, begin):
                    t = number // 2 + shift
                    if 0 <= t < number:
                        term = taps[t] * moved
                        total = term if total is None else total + term
                out, slope = swish(total)
                active[rows, lanes] = out.astype(bf16)
                slope_ref[rows, lanes] = slope.astype(bf16)

        loop(length // (ROWS * GROUP), block)

    steps_of(count, lambda u: loop(tiles, lambda j: convolve(u * tiles + j)), tick, 1.6)

    def leave(u):
        rows = at(u, length)
        hidden[rows, :] += dot(active[rows, :], weight_out[...])

    loop(count, leave)
    tick(1.0)


CONV_TAPS = 15


def half_of(size, q):
    return [slice(b + q * LANES, b + (q + 1) * LANES) for b in range(0, size, 2 * LANES)]


IN_PIECES = ((0, 0, 1), (1, 0, 2), (1, 1, 2))


def ffn_backward(
    count, weight_in, weight_out, active, slope, branch, normal, grad_in, grad_out, vec_grad,
    leave, tick=idle, ready=None,
):
    total_rows, width = branch.shape
    length = total_rows // count
    halves = [half_of(weight_in.shape[1], q) for q in range(2)]
    done = 0
    for q, parts in enumerate(halves):
        mine = jnp.concatenate([active[:, part] for part in parts], 1)
        grad_out[q][...] = dot_tn(mine, branch[...]).astype(bf16)
        if ready:
            ready(done)
        done += 1
        tick(2.1)
    for q, parts in enumerate(halves):

        def step(u):
            rows = at(u, length)
            out = jnp.concatenate([weight_out[part, :] for part in parts], 0)
            grad = dot_nt(branch[rows, :], out)
            slopes = jnp.concatenate([slope[rows, part] for part in parts], 1)
            low = (grad * slopes.astype(f32)).astype(bf16)
            sums = jnp.sum(low.astype(f32), 0, keepdims=True)
            for n, part in enumerate(parts):
                lanes = slice(n * LANES, (n + 1) * LANES)
                slope[rows, part] = low[:, lanes]
                row, begin = (2 + part.start // width, part.start % width)
                vec_grad[row : row + 1, begin : begin + LANES] += sums[:, lanes]

        steps_of(count, step, tick, 1.5)
        for target, (half, first, every) in zip(grad_in, IN_PIECES):
            if half == q:
                mine = [slope[:, part] for part in parts[first::every]]
                target[...] = dot_tn(normal[...], jnp.concatenate(mine, 1)).astype(bf16)
                if ready:
                    ready(done)
                done += 1
                tick(2.1 / every)
    if ready:
        ready(done)

    def finish(u):
        rows = at(u, length)
        leave(rows, dot_nt(slope[rows, :], weight_in[...]))

    if tick is idle:
        loop(count, finish)
    else:
        for u in range(count):
            if u:
                tick(3.0)
            finish(u)


def ffn2_both(
    count, hidden, cotangent, lengths, table, weight_in, weight_out, output, grad, grad_in,
    grad_out, vec_grad, normed_ref, scale_ref, active, slope, normal_ref, branch, tick=idle,
    ready=None, greeted=None,
):
    total_rows, width = hidden.shape
    length = total_rows // count
    blocks = weight_in.shape[1] // width
    vec_grad[...] = jnp.zeros_like(vec_grad)
    last = 3 + blocks

    def forward(u):
        rows = at(u, length)
        value = hidden[rows, :]
        normed, scale = norm(value)
        normed_ref[rows, :] = normed.astype(bf16)
        scale_ref[rows, :] = scale
        normal = (normed * table[F2 : F2 + 1, :] + table[F2 + 1 : F2 + 2, :]).astype(bf16)
        normal_ref[rows, :] = normal
        total = feed_forward(normal, weight_in, weight_out, table, F2, active, slope, rows)
        value = value + 0.5 * (total + table[F2 + 2 + blocks : F2 + 3 + blocks, :])
        normed, scale = norm(value)
        gain = table[F2 + last : F2 + last + 1, :]
        mask = frame_mask(length, lengths[u])
        shift = table[F2 + last + 1 : F2 + last + 2, :]
        grad_in, gain_grad, shift_grad = norm_back(
            cotangent[rows, :].astype(f32) * mask, normed, scale, gain
        )
        output[rows, :] = ((normed * gain + shift) * mask).astype(bf16)
        vec_grad[last : last + 1, :] += gain_grad
        vec_grad[last + 1 : last + 2, :] += shift_grad
        grad[rows, :] = grad_in
        low = (0.5 * grad_in).astype(bf16)
        branch[rows, :] = low
        vec_grad[last - 1 : last, :] += jnp.sum(low.astype(f32), 0, keepdims=True)

    if tick is idle:
        loop(count, forward)
    else:
        forward(0)
        greeted()
        for u in range(1, count):
            forward(u)

    def leave(rows, value):
        grad_in, gain_grad, shift_grad = norm_back(
            value, normed_ref[rows, :].astype(f32), scale_ref[rows, :], table[F2 : F2 + 1, :]
        )
        grad[rows, :] += grad_in
        vec_grad[0:1, :] += gain_grad
        vec_grad[1:2, :] += shift_grad

    ffn_backward(
        count, weight_in, weight_out, active, slope, branch, normal_ref, grad_in, grad_out,
        vec_grad, leave, tick, ready,
    )


def conv_backward(
    count, table, weight_in, weight_out, normed_ref, scale_ref, glu_ref, gate_ref, side_ref,
    slope_ref, active, grad, grad_in, grad_out, vec_grad, normal_ref, branch, depth_grad,
    tap_grads, mixed_grad, tick=idle,
):
    total_rows, width = grad.shape
    length = total_rows // count
    tiles = width // LANES
    number = CONV_TAPS
    vec_grad[...] = jnp.zeros_like(vec_grad)
    clear_edges(depth_grad, length)

    def enter(u):
        rows = at(u, length)
        low = grad[rows, :].astype(bf16)
        branch[rows, :] = low
        normed = normed_ref[rows, :].astype(f32)
        normal = (normed * table[CV : CV + 1, :] + table[CV + 1 : CV + 2, :]).astype(bf16)
        normal_ref[rows, :] = normal
        active_grad = dot_nt(low, weight_out[...])
        slope = active_grad * slope_ref[rows, :].astype(f32)
        for j in range(tiles):
            part = slice(j * LANES, (j + 1) * LANES)
            depth_grad[u * tiles + j, EDGE : EDGE + length, :] = slope[:, part]

    steps_of(count, enter, tick, 1.8)

    def convolve(index):
        u, j = (index // tiles, index % tiles)
        lanes = at(j, LANES)
        second = pl.ds(pl.multiple_of(width + j * LANES, LANES), LANES)
        taps = [table[CV + 2 + t : CV + 3 + t, lanes] for t in range(number)]
        tap_grads[...] = jnp.zeros_like(tap_grads)

        def block(n):
            sums = [None] * number
            for begin, rows in conv_rows(n, u * length):
                glu = glu_ref[rows, lanes].astype(f32)
                total = None
                for shift, moved in shifted(depth_grad, index, begin):
                    t = number // 2 - shift
                    if not 0 <= t < number:
                        continue
                    term = taps[t] * moved
                    total = term if total is None else total + term
                    pairs = jnp.sum((glu * moved).reshape(ROWS // 8, 8, LANES), 0)
                    sums[t] = pairs if sums[t] is None else sums[t] + pairs
                gate = gate_ref[rows, lanes].astype(f32)
                side = side_ref[rows, lanes].astype(f32)
                mixed_grad[rows, lanes] = (total * gate).astype(bf16)
                mixed_grad[rows, second] = (total * side).astype(bf16)
            for t in range(number):
                tap_grads[t] += sums[t]

        loop(length // (ROWS * GROUP), block)
        for t in range(number):
            vec_grad[2 + t : 3 + t, lanes] += jnp.sum(tap_grads[t], 0, keepdims=True)

    steps_of(count, lambda u: loop(tiles, lambda j: convolve(u * tiles + j)), tick, 2.7)
    grad_in[...] = dot_tn(normal_ref[...], mixed_grad[...]).astype(bf16)
    tick(2.1)
    grad_out[...] = dot_tn(active[...], branch[...]).astype(bf16)
    tick(1.3)
    mixer_leave(
        count, table, CV, weight_in, normed_ref, scale_ref, grad, vec_grad, mixed_grad, tick
    )


def mixer_leave(
    count, table, base, weight_in, normed_ref, scale_ref, grad, vec_grad, mixed_grad, tick
):
    length = grad.shape[0] // count

    def leave(u):
        rows = at(u, length)
        back = dot_nt(mixed_grad[rows, :], weight_in[...])
        grad_in, gain_grad, shift_grad = norm_back(
            back, normed_ref[rows, :].astype(f32), scale_ref[rows, :], table[base : base + 1, :]
        )
        grad[rows, :] += grad_in
        vec_grad[0:1, :] += gain_grad
        vec_grad[1:2, :] += shift_grad

    steps_of(count, leave, tick, 1.5)


def diagonal_sums(block):
    size = block.shape[0]
    zeros = jnp.zeros((8, size), f32)
    total = None
    for g in range(size // 8):
        rows = jnp.concatenate([block[8 * g : 8 * g + 8, :], zeros], 1)
        if g:
            rows = pltpu.roll(rows, 2 * size - 8 * g, 1)
        total = rows if total is None else total + rows
    out = total[0:1, :]
    for i in range(1, 8):
        out = out + pltpu.roll(total, 2 * size - i, 1)[i : i + 1, :]
    return out


def mix_grads(value_ref, time_grad, kernel_grad):
    tiles, length, _ = value_ref.shape
    steps = length // TILE
    first = head_lanes()
    kernel_rows = []
    for j in range(tiles):
        sums = [[None] * steps for _ in range(2)]
        for d in range(steps):
            total = None
            for i in range(steps - d):
                value = value_ref[j, i * TILE : (i + 1) * TILE, :]
                split = jnp.concatenate(
                    [jnp.where(first, value, 0), jnp.where(first, 0, value)], 0
                ).astype(bf16)
                term = dot_nt(split, time_grad[j, (i + d) * TILE : (i + d + 1) * TILE, :])
                total = term if total is None else total + term
            for e in range(2):
                sums[e][d] = diagonal_sums(total[e * TILE : (e + 1) * TILE, :])
        for e in range(2):
            pieces = []
            for d in range(steps):
                piece = sums[e][d][:, :TILE]
                if d + 1 < steps:
                    piece = piece + sums[e][d + 1][:, TILE:]
                pieces.append(piece)
            kernel_rows.append(jnp.concatenate(pieces, 1))
    kernel_grad[...] = jnp.concatenate(kernel_rows, 0)


def ssm_backward(
    count, table, weight_in, weight_out, wide_t, normed_ref, scale_ref, value_ref, swish_ref,
    side_ref, gated, grad, grad_in, grad_out, vec_grad, normal_ref, branch, time_grad, mixed_grad,
    tick=idle, start=None, ready=None,
):
    total_rows, width = grad.shape
    length = total_rows // count
    tiles = width // LANES
    steps = length // TILE
    vec_grad[...] = jnp.zeros_like(vec_grad)

    def enter(u):
        rows = at(u, length)
        lanes = at(u, LANES)
        low = grad[rows, :].astype(bf16)
        branch[rows, :] = low
        normed = normed_ref[rows, :].astype(f32)
        normal = (normed * table[SS : SS + 1, :] + table[SS + 1 : SS + 2, :]).astype(bf16)
        normal_ref[rows, :] = normal
        gated_grad = dot_nt(low, weight_out[...])
        for j in range(tiles):
            part = slice(j * LANES, (j + 1) * LANES)
            second = slice(width + j * LANES, width + (j + 1) * LANES)
            here = gated_grad[:, part]
            state_grad = here * swish_ref[j, :, lanes].astype(f32)
            time_grad[j, :, lanes] = state_grad.astype(bf16)
            mixed_grad[rows, second] = (here * side_ref[j, :, lanes].astype(f32)).astype(bf16)
            vec_grad[2:3, part] += jnp.sum(
                state_grad * value_ref[j, :, lanes].astype(f32), 0, keepdims=True
            )

    if tick is idle:
        loop(count, enter)
    else:
        enter(0)
        start()
        for u in range(1, count):
            enter(u)
            tick(1.0)
    grad_out[...] = dot_tn(gated[...], branch[...]).astype(bf16)
    if ready:
        ready(0)
    tick(0.9)
    first = head_lanes()
    for j in range(tiles):
        part = slice(j * LANES, (j + 1) * LANES)
        skip = table[SS + 2 : SS + 3, part]
        skip = jnp.concatenate([skip, skip], 1)
        for i in range(steps):
            rows = slice(i * TILE, (i + 1) * TILE)
            both = dot(wide_t[j, :, : length - i * TILE], time_grad[j, i * TILE :, :])
            back = jnp.where(first, both[:TILE], both[TILE:])
            back = (back + skip * time_grad[j, rows, :].astype(f32)).astype(bf16)
            for u in range(count):
                mixed_grad[u * length + i * TILE : u * length + (i + 1) * TILE, part] = back[
                    :, u * LANES : (u + 1) * LANES
                ]
        tick(0.6)
    grad_in[...] = dot_tn(normal_ref[...], mixed_grad[...]).astype(bf16)
    if ready:
        ready(1)
    tick(1.9)
    mixer_leave(
        count, table, SS, weight_in, normed_ref, scale_ref, grad, vec_grad, mixed_grad, tick
    )


def ffn1_backward(
    count, frames, grad, table, weight_in, weight_out, active, slope, frames_grad, grad_in,
    grad_out, vec_grad, normal_ref, branch, tick=idle, ready=None,
):
    total_rows, width = frames.shape
    length = total_rows // count
    blocks = weight_in.shape[1] // width
    vec_grad[...] = jnp.zeros_like(vec_grad)

    def enter(u):
        rows = at(u, length)
        normed, _ = norm(frames[rows, :].astype(f32))
        normal = (normed * table[F1 : F1 + 1, :] + table[F1 + 1 : F1 + 2, :]).astype(bf16)
        normal_ref[rows, :] = normal
        low = (0.5 * grad[rows, :]).astype(bf16)
        branch[rows, :] = low
        vec_grad[2 + blocks : 3 + blocks, :] += jnp.sum(low.astype(f32), 0, keepdims=True)

    steps_of(count, enter, tick, 1.0)

    def leave(rows, value):
        normed, scale = norm(frames[rows, :].astype(f32))
        grad_in, gain_grad, shift_grad = norm_back(value, normed, scale, table[F1 : F1 + 1, :])
        frames_grad[rows, :] = (grad[rows, :] + grad_in).astype(bf16)
        vec_grad[0:1, :] += gain_grad
        vec_grad[1:2, :] += shift_grad

    ffn_backward(
        count, weight_in, weight_out, active, slope, branch, normal_ref, grad_in, grad_out,
        vec_grad, leave, tick, ready,
    )


def shape(dims, kind):
    return jax.ShapeDtypeStruct(dims, kind)


def call(kernel, outs, scratch, smem, *operands):
    whole = pl.BlockSpec(memory_space=pltpu.VMEM)
    scalars = pl.BlockSpec(memory_space=pltpu.SMEM)
    return pl.pallas_call(
        kernel,
        out_shape=outs,
        in_specs=[scalars if n in smem else whole for n in range(len(operands))],
        out_specs=[whole] * len(outs),
        scratch_shapes=[pltpu.VMEM(s.shape, s.dtype) for s in scratch],
        compiler_params=pltpu.CompilerParams(vmem_limit_bytes=VMEM_BYTES),
    )(*operands)


def bring(weight_in, weight_out):
    first, second = (
        lax.all_gather(weight_in, "fsdp", axis=1, tiled=True),
        lax.all_gather(weight_out, "fsdp", axis=1, tiled=True),
    )
    return (
        lax.all_gather(first, "dp", axis=0, tiled=True),
        lax.all_gather(second, "dp", axis=0, tiled=True),
    )


def send(grad):
    part = lax.psum_scatter(grad, "fsdp", scatter_dimension=1, tiled=True)
    return lax.psum_scatter(part, "dp", scatter_dimension=0, tiled=True).astype(f32)


class Place:
    def __init__(self):
        me, z = (lax.axis_index("dp"), lax.axis_index("fsdp"))
        y, x, core = (me // 4, me // 2 % 2, me % 2)
        self.me, self.z, self.depth, self.layers = (me, z, 8, 4)
        self.chip, self.core = (me // 2, core)
        self.across = me + 2 - 4 * x
        self.along = me + 4 - 8 * y
        self.corner = me + 6 - 4 * x - 8 * y
        self.twin = me + 1 - 2 * core
        self.mates = (me, self.across, self.along, self.corner)
        turn = 1 - 2 * core
        self.twin_mates = tuple(mate + turn for mate in self.mates)

    def above(self, offset):
        return (self.z + offset) % self.layers

    def greet(self, everyone):
        barrier = pltpu.get_barrier_semaphore()
        others = [(self.me, self.above(o)) for o in range(1, self.layers)]
        if everyone:
            others += [((self.me + o) % self.depth, self.z) for o in range(1, self.depth)]
        else:
            others += [(mate, self.z) for mate in (self.across, self.along, self.twin)]
        for other in others:
            pl.semaphore_signal(
                barrier, inc=1, device_id=other, device_id_type=pl.DeviceIdType.MESH
            )
        return lambda: pl.semaphore_wait(barrier, len(others))


def copy_to(source, target, sems, slot, device):
    copy = pltpu.make_async_remote_copy(
        src_ref=source,
        dst_ref=target,
        send_sem=sems.at[0, slot],
        recv_sem=sems.at[1, slot],
        device_id=device,
        device_id_type=pl.DeviceIdType.MESH,
    )
    copy.start()
    return copy


TWIN, LAYER, LINE, LITTLE = range(4)
LATENCY = (1.4, 2.7, 2.7, 3.0)
SLACK = (1.5, 1.0)


class Turns:
    def __init__(self, slack=0.0):
        self.slack = slack
        self.pieces, self.begun, self.due = ([], [], [])
        self.now, self.free, self.open = (0.0, [0.0] * 4, [0.0] * 4)

    def add(self, piece, at_once=False):
        link, micros = piece[0][0][1:]
        self.pieces.append(piece)
        self.begun.append(0)
        self.due.append(max(self.now, self.open[link] - micros))
        self.open[link] = max(self.now, self.open[link]) + micros
        if at_once:
            self.step(len(self.pieces) - 1)
        self.settle()
        return len(self.pieces) - 1

    def step(self, n):
        action, link, micros = self.pieces[n][0][self.begun[n]]
        action()
        self.begun[n] += 1
        self.free[link] = max(self.now, self.free[link]) + micros
        self.due[n] = self.free[link] + LATENCY[link] + self.slack

    def live(self):
        return [n for n in range(len(self.pieces)) if not self.finished(n)]

    def settle(self):
        while True:
            due = [n for n in self.live() if self.due[n] <= self.now]
            if not due:
                return
            self.step(min(due, key=lambda n: (self.due[n], n)))

    def tick(self, micros):
        self.now += micros
        self.settle()

    def finished(self, n):
        return self.begun[n] == len(self.pieces[n][0])

    def run_until(self, *names):
        while not all(self.finished(n) for n in names):
            n = min(self.live(), key=lambda n: (self.due[n], n))
            self.now = max(self.now, self.due[n])
            self.step(n)

    def close(self):
        self.run_until(*range(len(self.pieces)))
        for _, copies in self.pieces:
            for copy in copies.values():
                copy.wait_send()


GATHER_SLOTS = 8
GATHER_RATES = (0.15, 0.09, 0.045, 0.03)


def gather_piece(spot, shard, whole, sems, begin, number):
    columns = shard.shape[1]
    half = number // 2
    copies = {}
    chip, core = (spot.chip, spot.core)
    lanes = at(spot.z, columns)

    def start(name, source, target, device):
        copies[name] = copy_to(source, target, sems, len(copies), device)

    def send_up():
        own = whole.at[chip, core, begin : begin + number, lanes]
        for o in range(1, spot.layers):
            start(("z", o), shard.at[begin : begin + number, :], own, (spot.me, spot.above(o)))
        whole[chip, core, begin : begin + number, lanes] = shard[begin : begin + number, :]

    def send_line():
        for o in range(1, spot.layers):
            copies["z", o].wait_recv()
        mine = whole.at[chip, core, begin : begin + number]
        start("across", mine, mine, (spot.across, spot.z))
        start("along", mine, mine, (spot.along, spot.z))

    def send_on():
        copies["across"].wait_recv()
        part = whole.at[spot.across // 2, core, begin : begin + half]
        start("corner along", part, part, (spot.along, spot.z))
        copies["along"].wait_recv()
        part = whole.at[spot.along // 2, core, begin + half : begin + number]
        start("corner across", part, part, (spot.across, spot.z))

    def send_twin():
        copies["corner along"].wait_recv()
        copies["corner across"].wait_recv()
        mine = whole.at[:, core, begin : begin + number]
        start("twin", mine, mine, (spot.twin, spot.z))

    def finish():
        copies["twin"].wait_recv()

    size = 1e-3 * number * columns * 2
    steps = [
        (send_up, LINE, GATHER_RATES[0] * size),
        (send_line, LAYER, GATHER_RATES[1] * size),
        (send_on, LAYER, GATHER_RATES[2] * size),
        (send_twin, TWIN, GATHER_RATES[3] * size),
        (finish, TWIN, 0.0),
    ]
    return (steps, copies)


def table_piece(spot, shard, whole, sems):
    columns = shard.shape[1]
    copies = {}

    def send_up():
        own = whole.at[:, at(spot.z, columns)]
        for o in range(1, spot.layers):
            copies[o] = copy_to(shard, own, sems, o - 1, (spot.me, spot.above(o)))
        whole[:, at(spot.z, columns)] = shard[...]

    def finish():
        for copy in copies.values():
            copy.wait_recv()

    return ([send_up, finish], copies)


def scatter_buffers(number, columns):
    return [
        shape((4, number, columns), bf16),
        shape((2, number // 2, columns), bf16),
        shape((2, number, columns), bf16),
        shape((3, number, columns // 4), bf16),
    ]


SCATTER_SLOTS = 11
SCATTER_RATES = (0.0008, 0.0013, 0.0026, 0.003)


def scatter_piece(spot, grad, keep, sums, corner, layer, lines, sems):
    number, columns = (grad.shape[0] // spot.depth, grad.shape[1])
    part = columns // spot.layers
    half = number // 2
    copies = {}

    def start(name, source, target, device):
        copies[name] = copy_to(source, target, sems, len(copies), device)

    def block(owner):
        return at(owner, number)

    def send_twin():
        for n in (3, 1, 2, 0):
            theirs = grad.at[block(spot.twin_mates[n]), :]
            start(("twin", n), theirs, sums.at[n], (spot.twin, spot.z))

    def add(target, first, size, one, other):
        sums[target, first : first + size, :] = one + other

    def send_corner():
        for n in (3, 1, 2, 0):
            copies["twin", n].wait_recv()
            add(n, 0, number, grad[block(spot.mates[n]), :], sums[n])
            if n == 3:
                start("along", sums.at[3, :half], corner.at[0], (spot.along, spot.z))
                start("across", sums.at[3, half:], corner.at[1], (spot.across, spot.z))

    def send_layer():
        copies["along"].wait_recv()
        add(1, 0, half, sums[1, :half, :], corner[0])
        start("own across", sums.at[1], layer.at[0], (spot.across, spot.z))
        copies["across"].wait_recv()
        add(2, half, half, sums[2, half:, :], corner[1])
        start("own along", sums.at[2], layer.at[1], (spot.along, spot.z))

    def send_up():
        copies["own across"].wait_recv()
        copies["own along"].wait_recv()
        total = sums[0].astype(f32) + layer[0].astype(f32) + layer[1].astype(f32)
        sums[0] = total.astype(bf16)
        for o in range(1, spot.layers):
            theirs = sums.at[0, :, at(spot.above(o), part)]
            start(("z", o), theirs, lines.at[o - 1], (spot.me, spot.above(o)))

    def finish():
        total = sums[0, :, at(spot.z, part)].astype(f32)
        for o in range(1, spot.layers):
            copies["z", o].wait_recv()
            total = total + lines[o - 1].astype(f32)
        keep(total)

    size = 1e-3 * 8 * number * columns * 2
    steps = [
        (send_twin, TWIN, SCATTER_RATES[0] * size),
        (send_corner, LAYER, SCATTER_RATES[1] * size),
        (send_layer, LAYER, SCATTER_RATES[2] * size),
        (send_up, LINE, SCATTER_RATES[3] * size),
        (finish, TWIN, 0.0),
    ]
    return (steps, copies)


SMALL_SLOTS = 13


def small_piece(spot, vectors, states, keep, lines, layers, sems):
    high = vectors.shape[0]
    columns = vectors.shape[1] // spot.layers
    copies = {}

    def start(source, target, device):
        copies[len(copies)] = copy_to(source, target, sems, len(copies), device)

    def send_up():
        for o in range(1, spot.layers):
            above = spot.above(o)
            start(vectors.at[:, at(above, columns)], lines.at[spot.z, :high], (spot.me, above))
            start(states, lines.at[spot.z, high:], (spot.me, above))
        lines[spot.z, :high, :] = vectors[:, at(spot.z, columns)]
        lines[spot.z, high:, :] = states[...]

    def send_layer():
        for n in range(2 * spot.layers - 2):
            copies[n].wait_recv()
        total = lines[0]
        for n in range(1, spot.layers):
            total = total + lines[n]
        layers[spot.me] = total
        own = layers.at[spot.me]
        for o in range(1, spot.depth):
            start(own, own, ((spot.me + o) % spot.depth, spot.z))

    def finish():
        for n in range(2 * spot.layers - 2, len(copies)):
            copies[n].wait_recv()
        total = layers[0]
        for n in range(1, spot.depth):
            total = total + layers[n]
        keep(total)

    steps = [(send_up, LITTLE, 0.0), (send_layer, LITTLE, 0.5), (finish, TWIN, 0.0)]
    return (steps, copies)


class Whole:
    def __init__(self, ref):
        chips, cores, rows, columns = ref.shape
        self.ref, self.block = (ref, cores * rows)
        self.shape = (chips * cores * rows, columns)

    def __getitem__(self, key):
        rows, columns = key if isinstance(key, tuple) else (slice(None), slice(None))
        if rows != slice(None):
            rows = slice(rows.start // self.block, rows.stop // self.block)
        value = self.ref[rows, :, :, columns]
        return value.reshape(-1, value.shape[-1])


class Refs:
    def __init__(self):
        self.copies, self.spilled = ({}, [])

    def later(self, *refs):
        return [Late(self, ref) for ref in refs]

    def fetch(self, *refs):
        return [late.start() for late in self.later(*refs)]

    def ready(self, *refs):
        for ref in refs:
            self.copies[id(ref)].wait()

    def spill(self, *refs):
        for ref in refs:
            self.copies[id(ref)].start()
            self.spilled.append(ref)


class Late:
    def __init__(self, r, ref):
        self.r, self.ref, self.here = (r, ref, False)
        self.shape, self.dtype = (ref.shape, ref.dtype)

    def start(self):
        self.r.copies[id(self.ref)].start()
        return self

    def land(self):
        if not self.here:
            self.r.ready(self.ref)
            self.here = True
        return self.ref

    def __getitem__(self, key):
        return self.land()[key]

    def __setitem__(self, key, value):
        self.land()[key] = value


NEAR, SCALAR, ANY, FAR = (pltpu.VMEM, pltpu.SMEM, pl.ANY, None)


def launch(body, inputs, outputs, scratch, collective=None, semaphores=None):
    operands = {**inputs, **outputs}
    names = list(operands)
    far = [name for name in names if operands[name][1] is FAR]
    semaphores = semaphores or {}

    def kernel(*refs):
        r = Refs()
        near = dict(zip(names, refs))
        rest = refs[len(names) :]
        buffers = dict(zip(far, rest))
        sems = rest[len(far)]
        rest = rest[len(far) + 1 :]
        for slot, name in enumerate(far):
            pair = (near[name], buffers[name])
            if name in outputs:
                pair = pair[::-1]
            r.copies[id(buffers[name])] = pltpu.make_async_copy(*pair, sems.at[slot])
        near.update(buffers)
        near.update(zip(list(scratch) + list(semaphores), rest))
        r.__dict__.update(near)
        body(r)
        r.ready(*r.spilled)

    def like(value):
        return pltpu.VMEM(value.shape, value.dtype)

    def specs(values):
        return [pl.BlockSpec(memory_space=ANY if p is FAR else p) for _, p in values.values()]

    results = pl.pallas_call(
        kernel,
        out_shape=[value for value, _ in outputs.values()],
        in_specs=specs(inputs),
        out_specs=specs(outputs),
        scratch_shapes=[like(operands[name][0]) for name in far]
        + [pltpu.SemaphoreType.DMA((max(1, len(far)),))]
        + [like(value) for value in scratch.values()]
        + [pltpu.SemaphoreType.DMA(dims) for dims in semaphores.values()],
        compiler_params=pltpu.CompilerParams(
            vmem_limit_bytes=VMEM_BYTES,
            collective_id=collective,
            has_side_effects=collective is not None,
        ),
    )(*[value for value, _ in inputs.values()])
    return dict(zip(outputs, results))


CUTS = (2, 2, 1, 1, 1, 1, 2, 2)
WEIGHTS = ("w1", "w2", "s1", "s2", "c1", "c2", "f1", "f2")


def under(prefix, values):
    return {prefix + str(n): value for n, value in enumerate(values)}


def held(r, prefix, number):
    return [r.__dict__[prefix + str(n)] for n in range(number)]


def scatter(r, spot, slot, name, keep):
    return scatter_piece(
        spot, r.__dict__[name], keep, *held(r, name + "_", 4), r.scatter_sems.at[slot]
    )


def piece_names(first):
    names = [first + "2" + str(q) for q in range(2)]
    return names + [first + "1" + str(half) + str(start) for half, start, _ in IN_PIECES]


def scatter_halves(r, spot, slot, first, turns, after=idle):
    ins, outs = (r.__dict__[first + "1_out"], r.__dict__[first + "2_out"])
    names = piece_names(first)
    plans = {first + "1" + str(half) + str(start): (half, start) for half, start, _ in IN_PIECES}

    def ready(n):
        if n == len(names):
            return after()
        name = names[n]

        def keep_out(total):
            q = int(name[-1])
            outs[q * LANES : (q + 1) * LANES, :] = total

        def keep_in(total):
            half, start = plans[name]
            for part in range(total.shape[1] // LANES):
                begin = (2 * (start + part) + half) * LANES
                ins[:, begin : begin + LANES] = total[:, part * LANES : (part + 1) * LANES]

        turns.add(scatter(r, spot, slot + n, name, keep_in if name in plans else keep_out))

    return ready


def half_pieces(width, hidden_width):
    half = hidden_width // 2
    ins = [shape((width, half // every), bf16) for _, _, every in IN_PIECES]
    return (ins, [shape((half, width), bf16)] * 2)


def half_scratch(first, width, hidden_width):
    ins, outs = half_pieces(width, hidden_width)
    scratch = {}
    for name in piece_names(first):
        grad = ins.pop(0) if name[1] == "1" else outs.pop(0)
        scratch[name] = grad
        scratch.update(under(name + "_", scatter_buffers(grad.shape[0] // 8, grad.shape[1])))
    return scratch


def half_refs(r, first):
    names = piece_names(first)
    ins = [r.__dict__[name] for name in names if name[1] == "1"]
    return (ins, [r.__dict__[name] for name in names if name[1] == "2"])


def fast_layer(frames, lengths, vectors, states_in, weights, cotangent):
    count, length, width = frames.shape
    rows = count * length
    tiles = width // LANES
    hidden_width = weights[0].shape[1] * 4
    heads, states = states_in[0].shape
    flat = frames.reshape(rows, width)
    row = shape((rows, width), bf16)
    row_f = shape((rows, width), f32)
    wide_row = shape((rows, hidden_width), bf16)
    scales = shape((rows, 1), f32)
    mixes = shape((tiles, length, count * LANES), bf16)
    band = shape((tiles, 2 * TILE, length), bf16)
    padded = shape((count * tiles, length + 2 * EDGE, LANES), f32)
    power = shape((4, heads * states, LANES), f32)
    whole_table = shape((TABLE, width), f32)
    bases = (F1, SS, CV, F2)
    decay, freq, real, imag = states_in

    def gathered(w):
        return shape((4, 2, w.shape[0], 4 * w.shape[1]), bf16)

    cuts = CUTS

    def forward(r):
        r.fetch(r.frames)
        spot = Place()
        greeted = spot.greet(False)
        r.shard[...] = jnp.zeros_like(r.shard)
        for ref, base in zip(held(r, "vec", 4), bases):
            r.shard[base : base + ref.shape[0], :] = ref[...].astype(f32)
        greeted()
        turns = Turns()
        place = {}
        for name, cut, shard in zip(WEIGHTS, cuts, held(r, "shard", 8)):
            size = shard.shape[0] // cut
            place[name] = []
            for q in range(cut):
                sems = r.gather_sems.at[len(turns.pieces)]
                piece = gather_piece(spot, shard, r.__dict__[name], sems, q * size, size)
                place[name].append(turns.add(piece))
        vector_steps, vector_copies = table_piece(spot, r.shard, r.table, r.table_sems)
        tick = turns.tick
        vector_steps[0]()
        build_bands(r.decay, r.freq, r.real, r.imag, r.powers, r.wide, r.wide_t, length, tick)
        r.spill(r.powers, r.wide_t)
        vector_steps[1]()

        def need(*wanted):
            for name in wanted:
                turns.run_until(*place[name])
                r.spill(r.__dict__[name])
            return [Whole(r.__dict__[name]) for name in wanted]

        first = need(*WEIGHTS[:2])
        r.ready(r.frames)
        ffn1_forward(
            count, r.frames, r.table, *first, r.hidden, r.w_active, r.w_slope, tick
        )
        r.spill(r.w_active, r.w_slope)
        mixer = need(*WEIGHTS[2:4])
        ssm_forward(
            count, r.hidden, r.table, *mixer, r.wide, r.s_normed, r.s_scale, r.s_value, r.s_swish,
            r.s_side, r.s_gated, tick,
        )
        r.spill(r.s_normed, r.s_scale, r.s_value, r.s_swish, r.s_side, r.s_gated)
        module = need(*WEIGHTS[4:6])
        conv_forward(
            count, r.hidden, r.lengths, r.table, *module, r.c_normed, r.c_scale, r.c_glu,
            r.c_gate, r.c_side, r.c_slope, r.c_active, r.glu, tick,
        )
        r.spill(r.hidden, r.c_normed, r.c_scale, r.c_glu, r.c_gate, r.c_side, r.c_slope, r.c_active)
        need(*WEIGHTS[6:])
        turns.close()
        for copy in vector_copies.values():
            copy.wait_send()

    saved = launch(
        forward,
        dict(
            frames=(flat, FAR), lengths=(lengths, SCALAR), decay=(decay, NEAR), freq=(freq, NEAR),
            real=(real, NEAR), imag=(imag, NEAR), **under("vec", [(v, NEAR) for v in vectors]),
            **under("shard", [(w, NEAR) for w in weights]),
        ),
        dict(
            table=(whole_table, NEAR), hidden=(row_f, FAR), w_active=(wide_row, FAR),
            w_slope=(wide_row, FAR), powers=(power, FAR), wide_t=(band, FAR), s_normed=(row, FAR),
            s_scale=(scales, FAR), s_value=(mixes, FAR), s_swish=(mixes, FAR), s_side=(mixes, FAR),
            s_gated=(row, FAR), c_normed=(row, FAR), c_scale=(scales, FAR), c_glu=(row, FAR),
            c_gate=(row, FAR), c_side=(row, FAR), c_slope=(row, FAR), c_active=(row, FAR),
            **{name: (gathered(w), FAR) for name, w in zip(WEIGHTS, weights)},
        ),
        dict(shard=shape((TABLE, LANES), f32), wide=band, glu=padded),
        0,
        dict(gather_sems=(sum(cuts), 2, GATHER_SLOTS), table_sems=(2, 3)),
    )
    shards = {}
    for name, w in zip(WEIGHTS, weights):
        saved[name] = saved[name].reshape(8 * w.shape[0], 4 * w.shape[1])
        shards[name + "_out"] = (shape(w.shape, f32), NEAR)
    kept = {name: (value, FAR) for name, value in saved.items()}
    table = (saved["table"], NEAR)

    def some(values, *prefixes):
        return {name: value for name, value in values.items() if name.startswith(prefixes)}

    half_width = hidden_width // 2
    square, double = (shape((width, width), bf16), shape((width, 2 * width), bf16))
    half_row = shape((rows, half_width), bf16)

    def later(r):
        spot = Place()
        greeted = spot.greet(False)
        hidden, f1, f2, cot = r.fetch(r.hidden, r.f1, r.f2, r.cot)
        conv_in = r.later(
            r.c2, r.c_normed, r.c_scale, r.c_glu, r.c_gate, r.c_side, r.c_slope, r.c_active, r.c1
        )

        def start():
            greeted()
            for late in conv_in:
                late.start()

        turns = Turns(SLACK[0])
        tick = turns.tick
        ffn2_both(
            count, hidden, cot, r.lengths, r.table, f1, f2, cot, hidden, *half_refs(r, "f"),
            r.f_vec, r.normed, r.scale, r.active, r.slope, r.normal, r.branch, tick,
            scatter_halves(r, spot, 0, "f", turns), start,
        )
        save_output = pltpu.make_async_copy(r.cot, r.output, r.save_sems.at[1])
        save_output.start()
        c2, *kept_in, c1 = [late.land() for late in conv_in]
        conv_backward(
            count, r.table, c1, c2, *kept_in, r.hidden, r.c1_grad, r.c2_grad, r.c_vec, r.normal,
            r.branch, r.depth_grad, r.tap_grads, r.active.at[:, : 2 * width], tick,
        )
        r.spill(r.c1_grad, r.c2_grad)
        save = pltpu.make_async_copy(r.hidden, r.grad, r.save_sems.at[0])
        save.start()
        turns.close()
        save.wait()
        save_output.wait()

    two = launch(
        later,
        dict(
            cot=(cotangent.reshape(rows, width), FAR), lengths=(lengths, SCALAR), table=table,
            **some(kept, "hidden", "f", "c"),
        ),
        dict(
            output=(row, ANY), grad=(row_f, ANY), c1_grad=(double, FAR), c2_grad=(square, FAR),
            f_vec=(shape((TABLE - F2, width), f32), NEAR),
            c_vec=(shape((F2 - CV, width), f32), NEAR), **some(shards, "f"),
        ),
        dict(
            normed=row, scale=scales, active=wide_row, slope=wide_row, normal=row, branch=row,
            depth_grad=padded, tap_grads=shape((CONV_TAPS, 8, LANES), f32),
            **half_scratch("f", width, hidden_width),
        ),
        1,
        dict(scatter_sems=(5, 2, SCATTER_SLOTS), save_sems=(2,)),
    )

    def last(r):
        spot = Place()
        greeted = spot.greet(True)
        grad, s2, *kept_in = r.fetch(
            r.grad, r.s2, r.s_normed, r.s_scale, r.s_value, r.s_swish, r.s_side
        )
        sent = r.fetch(r.c1g, r.c2g)
        wide_t, gated, s1, frames, w2, slope, active, w1, powers = r.later(
            r.wide_t, r.s_gated, r.s1, r.frames, r.w2, r.w_slope, r.w_active, r.w1, r.powers
        )
        r.vectors[...] = jnp.zeros_like(r.vectors)
        r.vectors[CV:F2, :] = r.c_vec[...]
        r.vectors[F2:, :] = r.f_vec[...]
        turns = Turns(SLACK[1])
        tick = turns.tick

        def send(name, slot, out):
            def keep(total):
                out[...] = total

            turns.add(scatter(r, spot, slot, name, keep))

        def start():
            for late in (wide_t, gated, s1, frames, w2, slope, active, w1, powers):
                late.start()
            for late in sent:
                late.land()
            greeted()
            send("c1g", 0, r.c1_out)
            send("c2g", 1, r.c2_out)

        def ready(n):
            send(*(("s1g", 2, r.s1_out) if n else ("s2g", 3, r.s2_out)))

        ssm_backward(
            count, r.table, s1, s2, wide_t, *kept_in, gated, grad, r.s1g, r.s2g,
            r.vectors.at[SS:CV], r.normal, r.branch, r.time_grad, r.mixed, tick, start,
            ready,
        )

        def after():
            mix_grads(r.s_value, r.time_grad, r.kernel_grad)
            tick(4.0)
            state_grads(r.kernel_grad[...], powers, r.decay, r.real, r.imag, r.states)
            tick(2.0)

        ffn1_backward(
            count, frames, r.grad, r.table, w1, w2, active, slope, r.normal, *half_refs(r, "w"),
            r.vectors.at[F1:SS], r.normal, r.branch, tick,
            scatter_halves(r, spot, 4, "w", turns, after),
        )
        save = pltpu.make_async_copy(r.normal, r.frames_grad, r.save_sems.at[0])
        save.start()

        def keep(total):
            r.small[...] = total

        turns.add(
            small_piece(spot, r.vectors, r.states, keep, r.lines, r.layers, r.small_sems), True
        )
        turns.close()
        save.wait()

    small = shape((TABLE + 4 * heads, LANES), f32)
    sent = dict(c1g=double, c2g=square, s1g=double, s2g=square)
    arriving = {}
    for name, grad in sent.items():
        arriving.update(under(name + "_", scatter_buffers(grad.shape[0] // 8, grad.shape[1])))
    three = launch(
        last,
        dict(
            frames=(flat, FAR), grad=(two["grad"], FAR), c1g=(two["c1_grad"], FAR),
            c2g=(two["c2_grad"], FAR), table=table, c_vec=(two["c_vec"], NEAR),
            f_vec=(two["f_vec"], NEAR), decay=(decay, NEAR), real=(real, NEAR), imag=(imag, NEAR),
            **some(kept, "s", "w", "powers"),
        ),
        dict(frames_grad=(row, ANY), small=(small, NEAR), **some(shards, "w", "s", "c")),
        dict(
            s1g=double, s2g=square, states=shape((4 * heads, LANES), f32), normal=row, branch=row,
            mixed=half_row, time_grad=mixes, vectors=whole_table,
            kernel_grad=shape((heads, length), f32), lines=shape((4,) + small.shape, f32),
            layers=shape((8,) + small.shape, f32), **half_scratch("w", width, hidden_width),
            **arriving,
        ),
        2,
        dict(
            scatter_sems=(9, 2, SCATTER_SLOTS), small_sems=(2, SMALL_SLOTS), save_sems=(1,)
        ),
    )

    done = [(two if name[0] == "f" else three)[name + "_out"] for name in WEIGHTS]

    def finish(r):
        for target, value in zip(held(r, "out", 8), held(r, "in", 8)):
            target[...] = value[...]
        for base, target in zip(bases, held(r, "vec", 4)):
            target[...] = r.small[base : base + target.shape[0], :]
        for n, target in enumerate(held(r, "st", 4)):
            begin = TABLE + n * heads
            target[...] = r.small[begin : begin + heads, :states]
        r.frames_end[...] = r.frames_grad[...]

    end = launch(
        finish,
        dict(
            small=(three["small"], NEAR), frames_grad=(three["frames_grad"], NEAR),
            **under("in", [(value, NEAR) for value in done]),
        ),
        dict(
            frames_end=(row, NEAR),
            **under("out", [(shape(value.shape, f32), NEAR) for value in done]),
            **under("vec", [(shape(v.shape, f32), NEAR) for v in vectors]),
            **under("st", [(shape((heads, states), f32), NEAR)] * 4),
        ),
        {},
    )
    frames_end, *outs = end.values()
    vec, state_grads_out = (outs[8:12], outs[12:])
    return (
        (two["output"].reshape(frames.shape), frames_end.reshape(frames.shape))
        + (outs[0], outs[1], vec[0], outs[2], outs[3], vec[1])
        + tuple(state_grads_out)
        + (outs[4], outs[5], vec[2], outs[6], outs[7], vec[3])
    )


def body(
    frames,
    lengths,
    ffn1_in,
    ffn1_out,
    ffn1_vec,
    ssm_in,
    ssm_out,
    ssm_vec,
    decay,
    freq,
    coef_re,
    coef_im,
    conv_in,
    conv_out,
    conv_vec,
    ffn2_in,
    ffn2_out,
    ffn2_vec,
    cotangent,
):
    count, length, width = frames.shape
    rows = count * length
    tiles = width // LANES
    hidden_width = width * (ffn1_vec.shape[0] - 3)
    heads, states = decay.shape
    flat = frames.reshape(rows, width)

    vectors = (ffn1_vec, ssm_vec, conv_vec, ffn2_vec)
    states_in = (decay, freq, coef_re, coef_im)
    weights = (ffn1_in, ffn1_out, ssm_in, ssm_out, conv_in, conv_out, ffn2_in, ffn2_out)
    if (lax.axis_size("dp"), lax.axis_size("fsdp")) == (8, 4):
        return fast_layer(frames, lengths, vectors, states_in, weights, cotangent)

    def pad(vec, to):
        return jnp.pad(vec.astype(f32), ((0, to - vec.shape[0]), (0, 0)))

    table = jnp.concatenate(
        [pad(ffn1_vec, SS - F1), pad(ssm_vec, CV - SS), pad(conv_vec, F2 - CV), pad(ffn2_vec, TABLE - F2)], 0
    )
    table = lax.all_gather(table, "fsdp", axis=1, tiled=True)
    weights = [whole for n in range(0, 8, 2) for whole in bring(weights[n], weights[n + 1])]
    first_in, first_out, mixer_in, mixer_out = weights[:4]
    module_in, module_out, second_in, second_out = weights[4:]

    row = shape((rows, width), bf16)
    row_f = shape((rows, width), f32)
    wide_row = shape((rows, hidden_width), bf16)
    scales = shape((rows, 1), f32)
    mixes = shape((tiles, length, count * LANES), bf16)
    band = shape((tiles, 2 * TILE, length), bf16)
    padded = shape((count * tiles, length + 2 * EDGE, LANES), f32)
    square = shape((width, width), bf16)
    double = shape((width, 2 * width), bf16)
    half_row = shape((rows, hidden_width // 2), bf16)
    power = shape((4, heads * states, LANES), f32)

    hidden, first_active, first_slope = call(
        partial(ffn1_forward, count), [row_f, wide_row, wide_row], [], (), flat, table, first_in,
        first_out,
    )

    def mixer_kernel(
        hidden_in, table, weight_in, weight_out, decay, freq, re, im, hidden, normed, scale, value,
        swish, side, gated, powers, wide_t, wide,
    ):
        hidden[...] = hidden_in[...]
        build_bands(decay, freq, re, im, powers, wide, wide_t, length)
        ssm_forward(
            count, hidden, table, weight_in, weight_out, wide, normed, scale, value, swish, side,
            gated,
        )

    hidden, *mixer_kept, powers, wide_t = call(
        mixer_kernel, [row_f, row, scales, mixes, mixes, mixes, row, power, band], [band],
        (), hidden, table, mixer_in, mixer_out, decay, freq, coef_re, coef_im,
    )

    def module_kernel(hidden_in, lengths, table, weight_in, weight_out, hidden, *rest):
        hidden[...] = hidden_in[...]
        conv_forward(count, hidden, lengths, table, weight_in, weight_out, *rest)

    hidden, *module_kept = call(
        module_kernel, [row_f, row, scales, row, row, row, row, row], [padded], (1,), hidden,
        lengths, table, module_in, module_out,
    )

    ins, outs = half_pieces(width, hidden_width)
    number = len(ins)

    def second_kernel(hidden, cot, lengths, table, w_in, w_out, output, grad, *rest):
        ffn2_both(
            count, hidden, cot, lengths, table, w_in, w_out, output, grad, rest[:number],
            rest[number : number + 2], *rest[number + 2 :],
        )

    output, grad, *second_grads, second_vec = call(
        second_kernel,
        [row, row_f, *ins, *outs, shape((TABLE - F2, width), f32)],
        [row, scales, wide_row, wide_row, row, row],
        (2,), hidden, cotangent.reshape(rows, width), lengths, table, second_in, second_out,
    )

    def module_back(grad_in, table, *rest):
        kept, rest = (rest[: 2 + len(module_kept)], rest[2 + len(module_kept) :])
        rest[0][...] = grad_in[...]
        conv_backward(count, table, *kept, *rest)

    grad, module_in_grad, module_out_grad, module_vec = call(
        module_back,
        [row_f, double, square, shape((F2 - CV, width), f32)],
        [
            row, row, padded, shape((CONV_TAPS, 8, LANES), f32),
            shape((rows, 2 * width), bf16),
        ],
        (), grad, table, module_in, module_out, *module_kept,
    )

    def mixer_back(
        grad_in, table, w_in, w_out, wide_t, powers, decay, re, im, normed, scale, value, swish,
        side, gated, grad, in_grad, out_grad, vec_grad, states, *rest,
    ):
        grad[...] = grad_in[...]
        ssm_backward(
            count, table, w_in, w_out, wide_t, normed, scale, value, swish, side, gated, grad,
            in_grad, out_grad, vec_grad, *rest[1:],
        )
        mix_grads(value, rest[3], rest[0])
        state_grads(rest[0][...], powers, decay, re, im, states)

    grad, mixer_in_grad, mixer_out_grad, mixer_vec, state_grad = call(
        mixer_back,
        [row_f, double, square, shape((CV - SS, width), f32), shape((4 * heads, LANES), f32)],
        [
            shape((heads, length), f32), row, row, mixes, shape((rows, 2 * width), bf16),
        ],
        (), grad, table, mixer_in, mixer_out, wide_t, powers, decay, coef_re, coef_im,
        *mixer_kept,
    )

    def first_back(frames, grad, table, w_in, w_out, active, kept, out, *rest):
        *rest, slope = rest
        slope[...] = kept[...]
        ffn1_backward(
            count, frames, grad, table, w_in, w_out, active, slope, out, rest[:number],
            rest[number : number + 2], *rest[number + 2 :],
        )

    frames_grad, *first_grads, first_vec = call(
        first_back,
        [row, *ins, *outs, shape((SS - F1, width), f32)],
        [row, row, wide_row],
        (), flat, grad, table, first_in, first_out, first_active, first_slope,
    )
    vec_grads = jnp.concatenate([first_vec, mixer_vec, module_vec, second_vec], 0)

    def join(in_a, *parts):
        wide = [part.reshape(width, -1, LANES) for part in (in_a,) + parts[:2]]
        wide = [wide[0], jnp.stack(wide[1:], 2).reshape(width, -1, LANES)]
        tall = [part.reshape(-1, LANES, width) for part in parts[2:]]
        return (
            jnp.stack(wide, 2).reshape(width, hidden_width),
            jnp.stack(tall, 1).reshape(hidden_width, width),
        )

    grads = (
        *join(*first_grads), mixer_in_grad, mixer_out_grad, module_in_grad, module_out_grad,
        *join(*second_grads),
    )
    vec_grads = lax.psum(
        lax.psum_scatter(vec_grads, "fsdp", scatter_dimension=1, tiled=True), "dp"
    )
    state_grad = lax.psum(state_grad, ("dp", "fsdp"))
    grads = [send(grad) for grad in grads]
    state_grad = state_grad[:, :states].reshape(4, heads, states)

    def layer(number, base, like):
        return (grads[number], grads[number + 1], vec_grads[base : base + like.shape[0]])

    return (
        (output.reshape(count, length, width), frames_grad.reshape(count, length, width))
        + layer(0, F1, ffn1_vec)
        + layer(2, SS, ssm_vec)
        + tuple(state_grad[n] for n in range(4))
        + layer(4, CV, conv_vec)
        + layer(6, F2, ffn2_vec)
    )


def solution(mesh):
    split = P(("dp", "fsdp"), None, None)
    weight = P("dp", "fsdp")
    vector = P(None, "fsdp")
    layer = (weight, weight, vector)
    whole = (P(), P(), P(), P())
    in_specs = (split, P(("dp", "fsdp"))) + layer + layer + whole + layer + layer + (split,)
    out_specs = (split, split) + layer + layer + whole + layer + layer
    return jax.shard_map(body, mesh=mesh, in_specs=in_specs, out_specs=out_specs, check_vma=False)
```

```python
from functools import partial

import jax
import jax.numpy as jnp
from jax import lax
from jax.experimental import pallas as pl
from jax.experimental.pallas import tpu as pltpu
from jax.sharding import PartitionSpec as P

EPSILON = 1e-05
VMEM_BYTES = 62 * 2**20
LANES = 128
TILE = 256
EDGE = 8
F1, SS, CV, F2 = (0, 8, 16, 40)
TABLE = 56
f32 = jnp.float32
bf16 = jnp.bfloat16


def dot(left, right):
    return jnp.dot(left, right, preferred_element_type=f32)


def dot_nt(left, right):
    return lax.dot_general(left, right, (((1,), (1,)), ((), ())), preferred_element_type=f32)


def dot_tn(left, right):
    return lax.dot_general(left, right, (((0,), (0,)), ((), ())), preferred_element_type=f32)


def loop(number, step):
    def turn(index, carry):
        step(index)
        return carry

    lax.fori_loop(0, number, turn, 0)


def at(index, size):
    if isinstance(index, int):
        return slice(index * size, (index + 1) * size)
    return pl.ds(pl.multiple_of(index * size, size), size)


def idle(micros=0.0):
    pass


def steps_of(number, step, tick, micros):
    if tick is idle:
        loop(number, step)
    else:
        for index in range(number):
            step(index)
            tick(micros)


def norm(hidden):
    center = hidden - jnp.mean(hidden, -1, keepdims=True)
    scale = lax.rsqrt(jnp.mean(center * center, -1, keepdims=True) + EPSILON)
    return (center * scale, scale)


def norm_back(grad, normed, scale, gain):
    scaled = grad * gain
    centered = (
        scaled
        - jnp.mean(scaled, -1, keepdims=True)
        - normed * jnp.mean(scaled * normed, -1, keepdims=True)
    )
    return (
        scale * centered,
        jnp.sum(grad * normed, 0, keepdims=True),
        jnp.sum(grad, 0, keepdims=True),
    )


def frame_mask(length, valid):
    return (lax.broadcasted_iota(jnp.int32, (length, 1), 0) < valid).astype(f32)


def identity(size):
    return lax.broadcasted_iota(jnp.int32, (size, size), 0) == lax.broadcasted_iota(
        jnp.int32, (size, size), 1
    )


def state_column(values):
    heads, states = values.shape
    eye = identity(states)
    columns = [
        jnp.sum(
            jnp.where(eye, jnp.broadcast_to(values[h : h + 1, :], (states, states)), 0.0),
            1,
            keepdims=True,
        )
        for h in range(heads)
    ]
    return jnp.concatenate(columns, 0)


def state_rows(column, heads):
    states = column.shape[0] // heads
    eye = identity(states)
    rows = [
        jnp.sum(
            jnp.where(
                eye,
                jnp.broadcast_to(column[h * states : (h + 1) * states, :], (states, states)),
                0.0,
            ),
            0,
            keepdims=True,
        )
        for h in range(heads)
    ]
    return jnp.concatenate(rows, 0)


def head_steps(heads, states):
    row = lax.broadcasted_iota(jnp.int32, (heads * states, 1), 0)
    log_steps = jnp.full((heads * states, 1), -6.9, f32)
    for h in range(1, heads):
        log_steps = jnp.where(row >= h * states, -6.9 + 4.6 * h / (heads - 1), log_steps)
    return jnp.exp(log_steps)


def state_powers(decay, freq, step, stride):
    places = lax.broadcasted_iota(jnp.int32, (1, LANES), 1).astype(f32) * float(stride)
    damping = jnp.exp(-(step * decay) * places)
    phase = (step * freq) * places
    return (damping * jnp.cos(phase), damping * jnp.sin(phase))


def build_bands(decay_ref, freq_ref, re_ref, im_ref, powers, wide, wide_t, length, tick=idle):
    heads, states = decay_ref.shape
    step = head_steps(heads, states)
    decay, freq = (state_column(decay_ref[...]), state_column(freq_ref[...]))
    real, imag = (state_column(re_ref[...]), state_column(im_ref[...]))
    near_re, near_im = state_powers(decay, freq, step, 1)
    far_re, far_im = state_powers(decay, freq, step, LANES)
    powers[0], powers[1], powers[2], powers[3] = (near_re, near_im, far_re, far_im)
    lead_re = real * far_re - imag * far_im
    lead_im = real * far_im + imag * far_re
    blocks = length // LANES
    pieces = []
    for a in range(blocks):
        term = lead_re[:, a : a + 1] * near_re - lead_im[:, a : a + 1] * near_im
        pieces.append(jnp.sum(term.reshape(heads, states, LANES), 1))
    root = jnp.sqrt(step / states)
    factor = jnp.concatenate([root[h * states : h * states + 1, :] for h in range(heads)], 0)
    low = [(piece * factor).astype(bf16) for piece in pieces]
    turn = (
        lax.broadcasted_iota(jnp.int32, (LANES, LANES), 0)
        + lax.broadcasted_iota(jnp.int32, (LANES, LANES), 1)
        == LANES - 1
    ).astype(bf16)
    ring = length + TILE
    zeros = jnp.zeros((heads, TILE), f32)
    forward = jnp.concatenate([piece.astype(f32) for piece in low] + [zeros], 1)
    backward = jnp.concatenate([dot(piece, turn) for piece in low[::-1]] + [zeros], 1)
    backward = pltpu.roll(backward, ring - (TILE - 1), 1)
    tick(9.0)
    for source, band in ((backward, wide), (forward, wide_t)):
        for h in range(heads):
            if h == heads // 2:
                tick(9.0)
            row = jnp.broadcast_to(source[h : h + 1, :], (8, ring))
            base = pltpu.roll(row, 0, 1, stride=1, stride_axis=0)
            for g in range(0, LANES // 8, 2):
                pair = jnp.concatenate(
                    [pltpu.roll(base, 8 * g, 1), pltpu.roll(base, 8 * g + 8, 1)], 0
                )
                for q in range(TILE // LANES):
                    if q == 0:
                        cut = pair[:, :length]
                    else:
                        cut = jnp.concatenate(
                            [pair[:, ring - q * LANES :], pair[:, : length - q * LANES]], 1
                        )
                    place = (h % 2) * TILE + q * LANES + 8 * g
                    band[h // 2, place : place + 16, :] = cut.astype(bf16)
        tick(9.0)


def state_grads(kernel_grad, powers, decay_ref, re_ref, im_ref, out):
    heads, states = decay_ref.shape
    step = head_steps(heads, states)
    real, imag = (state_column(re_ref[...]), state_column(im_ref[...]))
    near_re, near_im, far_re, far_im = (powers[0], powers[1], powers[2], powers[3])
    length = kernel_grad.shape[1]
    zero_re = zero_im = one_re = one_im = None
    for a in range(length // LANES):
        block = kernel_grad[:, a * LANES : (a + 1) * LANES]
        spread = jnp.concatenate(
            [jnp.broadcast_to(block[h : h + 1, :], (states, LANES)) for h in range(heads)], 0
        )
        term_re, term_im = (far_re[:, a : a + 1] * spread, far_im[:, a : a + 1] * spread)
        if a == 0:
            zero_re, zero_im = (term_re, term_im)
            one_re, one_im = (jnp.zeros_like(term_re), jnp.zeros_like(term_im))
        else:
            zero_re, zero_im = (zero_re + term_re, zero_im + term_im)
            one_re, one_im = (one_re + a * LANES * term_re, one_im + a * LANES * term_im)
    places = lax.broadcasted_iota(jnp.int32, (1, LANES), 1).astype(f32)
    one_re, one_im = (one_re + places * zero_re, one_im + places * zero_im)

    def close(left_re, left_im):
        return (
            jnp.sum(near_re * left_re - near_im * left_im, 1, keepdims=True),
            jnp.sum(near_re * left_im + near_im * left_re, 1, keepdims=True),
        )

    plain_re, plain_im = close(zero_re, zero_im)
    place_re, place_im = close(one_re, one_im)
    scale = jnp.sqrt(step / states)
    columns = (
        -step * scale * (real * place_re - imag * place_im),
        -step * scale * (real * place_im + imag * place_re),
        scale * plain_re,
        -scale * plain_im,
    )
    out[...] = jnp.zeros_like(out)
    for number, column in enumerate(columns):
        out[number * heads : (number + 1) * heads, :states] = state_rows(column, heads)


def swish(value):
    sig = jax.nn.sigmoid(value)
    out = value * sig
    return (out, sig + out * (1.0 - sig))


def feed_forward(normal, weight_in, weight_out, table, base, active_ref, slope_ref, rows):
    width = normal.shape[1]
    total = None
    for c in range(weight_in.shape[1] // width):
        part = slice(c * width, (c + 1) * width)
        value = dot(normal, weight_in[:, part]) + table[base + 2 + c : base + 3 + c, :]
        active, slope = swish(value)
        active = active.astype(bf16)
        active_ref[rows, part] = active
        slope_ref[rows, part] = slope.astype(bf16)
        term = dot(active, weight_out[part, :])
        total = term if total is None else total + term
    return total


def ffn1_forward(
    count, frames, table, weight_in, weight_out, hidden, active, slope, tick=idle
):
    length = frames.shape[0] // count
    blocks = weight_in.shape[1] // weight_in.shape[0]

    def step(u):
        rows = at(u, length)
        value = frames[rows, :].astype(f32)
        normed, _ = norm(value)
        normal = (normed * table[F1 : F1 + 1, :] + table[F1 + 1 : F1 + 2, :]).astype(bf16)
        total = feed_forward(normal, weight_in, weight_out, table, F1, active, slope, rows)
        bias = table[F1 + 2 + blocks : F1 + 3 + blocks, :]
        hidden[rows, :] = value + 0.5 * (total + bias)

    steps_of(count, step, tick, 4.0)


def head_lanes():
    return lax.broadcasted_iota(jnp.int32, (1, 2 * LANES), 1) % LANES < LANES // 2


def ssm_forward(
    count, hidden, table, weight_in, weight_out, wide, normed_ref, scale_ref, value_ref, swish_ref,
    side_ref, gated, tick=idle,
):
    total_rows, width = hidden.shape
    length = total_rows // count
    tiles = width // LANES

    def enter(u):
        rows = at(u, length)
        lanes = at(u, LANES)
        normed, scale = norm(hidden[rows, :])
        normed_ref[rows, :] = normed.astype(bf16)
        scale_ref[rows, :] = scale
        normal = (normed * table[SS : SS + 1, :] + table[SS + 1 : SS + 2, :]).astype(bf16)
        value = dot(normal, weight_in[:, :width]).astype(bf16)
        gate = dot(normal, weight_in[:, width:]).astype(bf16)
        for j in range(tiles):
            part = slice(j * LANES, (j + 1) * LANES)
            value_ref[j, :, lanes] = value[:, part]
            side_ref[j, :, lanes] = gate[:, part]

    steps_of(count, enter, tick, 1.5)
    first = head_lanes()
    steps = length // TILE
    for j in range(tiles):
        part = slice(j * LANES, (j + 1) * LANES)
        skip = table[SS + 2 : SS + 3, part]
        skip = jnp.concatenate([skip, skip], 1)
        for i in range(steps):
            rows = slice(i * TILE, (i + 1) * TILE)
            both = dot(wide[j, :, (steps - 1 - i) * TILE :], value_ref[j, : (i + 1) * TILE, :])
            mixed = jnp.where(first, both[:TILE], both[TILE:])
            gate, slope = swish(side_ref[j, rows, :].astype(f32))
            state = mixed + skip * value_ref[j, rows, :].astype(f32)
            swish_ref[j, rows, :] = gate.astype(bf16)
            side_ref[j, rows, :] = (state * slope).astype(bf16)
            out = (state * gate).astype(bf16)
            for u in range(count):
                gated[u * length + i * TILE : u * length + (i + 1) * TILE, part] = out[
                    :, u * LANES : (u + 1) * LANES
                ]
        if j % 2:
            tick(1.2)

    def leave(u):
        rows = at(u, length)
        hidden[rows, :] += dot(gated[rows, :], weight_out[...])

    loop(count, leave)
    tick(1.0)


def clear_edges(padded, length):
    number, _, lanes = padded.shape
    zeros = jnp.zeros((number, EDGE, lanes), f32)
    padded[:, :EDGE, :] = zeros
    padded[:, EDGE + length :, :] = zeros


ROWS, GROUP = (64, 4)


def conv_rows(n, base):
    first = pl.multiple_of(n * (ROWS * GROUP), ROWS * GROUP)
    for g in range(GROUP):
        begin = first + g * ROWS
        yield begin, pl.ds(pl.multiple_of(base + begin, 32), ROWS)


def shifted(padded, index, begin):
    for b in range(8):
        near = padded[index, pl.ds(begin + b + EDGE - 8, ROWS + 8), :]
        yield b - 8, near[:ROWS]
        yield b, near[8:]


def conv_forward(
    count, hidden, lengths, table, weight_in, weight_out, normed_ref, scale_ref, glu_ref, gate_ref,
    side_ref, slope_ref, active, glu, tick=idle,
):
    total_rows, width = hidden.shape
    length = total_rows // count
    tiles = width // LANES
    clear_edges(glu, length)

    def enter(u):
        rows = at(u, length)
        normed, scale = norm(hidden[rows, :])
        normed_ref[rows, :] = normed.astype(bf16)
        scale_ref[rows, :] = scale
        normal = (normed * table[CV : CV + 1, :] + table[CV + 1 : CV + 2, :]).astype(bf16)
        linear = dot(normal, weight_in[:, :width])
        sig = jax.nn.sigmoid(dot(normal, weight_in[:, width:]))
        gate = sig * frame_mask(length, lengths[u])
        value = linear * gate
        glu_ref[rows, :] = value.astype(bf16)
        gate_ref[rows, :] = gate.astype(bf16)
        side_ref[rows, :] = (value * (1.0 - sig)).astype(bf16)
        for j in range(tiles):
            glu[u * tiles + j, EDGE : EDGE + length, :] = value[:, j * LANES : (j + 1) * LANES]

    steps_of(count, enter, tick, 1.7)
    number = CONV_TAPS

    def convolve(index):
        u, j = (index // tiles, index % tiles)
        lanes = at(j, LANES)
        taps = [table[CV + 2 + t : CV + 3 + t, lanes] for t in range(number)]

        def block(n):
            for begin, rows in conv_rows(n, u * length):
                total = None
                for shift, moved in shifted(glu, index, begin):
                    t = number // 2 + shift
                    if 0 <= t < number:
                        term = taps[t] * moved
                        total = term if total is None else total + term
                out, slope = swish(total)
                active[rows, lanes] = out.astype(bf16)
                slope_ref[rows, lanes] = slope.astype(bf16)

        loop(length // (ROWS * GROUP), block)

    steps_of(count, lambda u: loop(tiles, lambda j: convolve(u * tiles + j)), tick, 1.6)

    def leave(u):
        rows = at(u, length)
        hidden[rows, :] += dot(active[rows, :], weight_out[...])

    loop(count, leave)
    tick(1.0)


CONV_TAPS = 15


def half_of(size, q):
    return [slice(b + q * LANES, b + (q + 1) * LANES) for b in range(0, size, 2 * LANES)]


IN_PIECES = ((0, 0, 1), (1, 0, 2), (1, 1, 2))


def ffn_backward(
    count, weight_in, weight_out, active, slope, branch, normal, grad_in, grad_out, vec_grad,
    leave, tick=idle, ready=None,
):
    total_rows, width = branch.shape
    length = total_rows // count
    halves = [half_of(weight_in.shape[1], q) for q in range(2)]
    done = 0
    for q, parts in enumerate(halves):
        mine = jnp.concatenate([active[:, part] for part in parts], 1)
        grad_out[q][...] = dot_tn(mine, branch[...]).astype(bf16)
        if ready:
            ready(done)
        done += 1
        tick(2.1)
    for q, parts in enumerate(halves):

        def step(u):
            rows = at(u, length)
            out = jnp.concatenate([weight_out[part, :] for part in parts], 0)
            grad = dot_nt(branch[rows, :], out)
            slopes = jnp.concatenate([slope[rows, part] for part in parts], 1)
            low = (grad * slopes.astype(f32)).astype(bf16)
            sums = jnp.sum(low.astype(f32), 0, keepdims=True)
            for n, part in enumerate(parts):
                lanes = slice(n * LANES, (n + 1) * LANES)
                slope[rows, part] = low[:, lanes]
                row, begin = (2 + part.start // width, part.start % width)
                vec_grad[row : row + 1, begin : begin + LANES] += sums[:, lanes]

        steps_of(count, step, tick, 1.5)
        for target, (half, first, every) in zip(grad_in, IN_PIECES):
            if half == q:
                mine = [slope[:, part] for part in parts[first::every]]
                target[...] = dot_tn(normal[...], jnp.concatenate(mine, 1)).astype(bf16)
                if ready:
                    ready(done)
                done += 1
                tick(2.1 / every)
    if ready:
        ready(done)

    def finish(u):
        rows = at(u, length)
        leave(rows, dot_nt(slope[rows, :], weight_in[...]))

    if tick is idle:
        loop(count, finish)
    else:
        for u in range(count):
            if u:
                tick(3.0)
            finish(u)


def ffn2_both(
    count, hidden, cotangent, lengths, table, weight_in, weight_out, output, grad, grad_in,
    grad_out, vec_grad, normed_ref, scale_ref, active, slope, normal_ref, branch, tick=idle,
    ready=None, greeted=None,
):
    total_rows, width = hidden.shape
    length = total_rows // count
    blocks = weight_in.shape[1] // width
    vec_grad[...] = jnp.zeros_like(vec_grad)
    last = 3 + blocks

    def forward(u):
        rows = at(u, length)
        value = hidden[rows, :]
        normed, scale = norm(value)
        normed_ref[rows, :] = normed.astype(bf16)
        scale_ref[rows, :] = scale
        normal = (normed * table[F2 : F2 + 1, :] + table[F2 + 1 : F2 + 2, :]).astype(bf16)
        normal_ref[rows, :] = normal
        total = feed_forward(normal, weight_in, weight_out, table, F2, active, slope, rows)
        value = value + 0.5 * (total + table[F2 + 2 + blocks : F2 + 3 + blocks, :])
        normed, scale = norm(value)
        gain = table[F2 + last : F2 + last + 1, :]
        mask = frame_mask(length, lengths[u])
        shift = table[F2 + last + 1 : F2 + last + 2, :]
        grad_in, gain_grad, shift_grad = norm_back(
            cotangent[rows, :].astype(f32) * mask, normed, scale, gain
        )
        output[rows, :] = ((normed * gain + shift) * mask).astype(bf16)
        vec_grad[last : last + 1, :] += gain_grad
        vec_grad[last + 1 : last + 2, :] += shift_grad
        grad[rows, :] = grad_in
        low = (0.5 * grad_in).astype(bf16)
        branch[rows, :] = low
        vec_grad[last - 1 : last, :] += jnp.sum(low.astype(f32), 0, keepdims=True)

    if tick is idle:
        loop(count, forward)
    else:
        forward(0)
        greeted()
        for u in range(1, count):
            forward(u)

    def leave(rows, value):
        grad_in, gain_grad, shift_grad = norm_back(
            value, normed_ref[rows, :].astype(f32), scale_ref[rows, :], table[F2 : F2 + 1, :]
        )
        grad[rows, :] += grad_in
        vec_grad[0:1, :] += gain_grad
        vec_grad[1:2, :] += shift_grad

    ffn_backward(
        count, weight_in, weight_out, active, slope, branch, normal_ref, grad_in, grad_out,
        vec_grad, leave, tick, ready,
    )


def conv_backward(
    count, table, weight_in, weight_out, normed_ref, scale_ref, glu_ref, gate_ref, side_ref,
    slope_ref, active, grad, grad_in, grad_out, vec_grad, normal_ref, branch, depth_grad,
    tap_grads, mixed_grad, tick=idle,
):
    total_rows, width = grad.shape
    length = total_rows // count
    tiles = width // LANES
    number = CONV_TAPS
    vec_grad[...] = jnp.zeros_like(vec_grad)
    clear_edges(depth_grad, length)

    def enter(u):
        rows = at(u, length)
        low = grad[rows, :].astype(bf16)
        branch[rows, :] = low
        normed = normed_ref[rows, :].astype(f32)
        normal = (normed * table[CV : CV + 1, :] + table[CV + 1 : CV + 2, :]).astype(bf16)
        normal_ref[rows, :] = normal
        active_grad = dot_nt(low, weight_out[...])
        slope = active_grad * slope_ref[rows, :].astype(f32)
        for j in range(tiles):
            part = slice(j * LANES, (j + 1) * LANES)
            depth_grad[u * tiles + j, EDGE : EDGE + length, :] = slope[:, part]

    steps_of(count, enter, tick, 1.8)

    def convolve(index):
        u, j = (index // tiles, index % tiles)
        lanes = at(j, LANES)
        second = pl.ds(pl.multiple_of(width + j * LANES, LANES), LANES)
        taps = [table[CV + 2 + t : CV + 3 + t, lanes] for t in range(number)]
        tap_grads[...] = jnp.zeros_like(tap_grads)

        def block(n):
            sums = [None] * number
            for begin, rows in conv_rows(n, u * length):
                glu = glu_ref[rows, lanes].astype(f32)
                total = None
                for shift, moved in shifted(depth_grad, index, begin):
                    t = number // 2 - shift
                    if not 0 <= t < number:
                        continue
                    term = taps[t] * moved
                    total = term if total is None else total + term
                    pairs = jnp.sum((glu * moved).reshape(ROWS // 8, 8, LANES), 0)
                    sums[t] = pairs if sums[t] is None else sums[t] + pairs
                gate = gate_ref[rows, lanes].astype(f32)
                side = side_ref[rows, lanes].astype(f32)
                mixed_grad[rows, lanes] = (total * gate).astype(bf16)
                mixed_grad[rows, second] = (total * side).astype(bf16)
            for t in range(number):
                tap_grads[t] += sums[t]

        loop(length // (ROWS * GROUP), block)
        for t in range(number):
            vec_grad[2 + t : 3 + t, lanes] += jnp.sum(tap_grads[t], 0, keepdims=True)

    steps_of(count, lambda u: loop(tiles, lambda j: convolve(u * tiles + j)), tick, 2.7)
    grad_in[...] = dot_tn(normal_ref[...], mixed_grad[...]).astype(bf16)
    tick(2.1)
    grad_out[...] = dot_tn(active[...], branch[...]).astype(bf16)
    tick(1.3)
    mixer_leave(
        count, table, CV, weight_in, normed_ref, scale_ref, grad, vec_grad, mixed_grad, tick
    )


def mixer_leave(
    count, table, base, weight_in, normed_ref, scale_ref, grad, vec_grad, mixed_grad, tick
):
    length = grad.shape[0] // count

    def leave(u):
        rows = at(u, length)
        back = dot_nt(mixed_grad[rows, :], weight_in[...])
        grad_in, gain_grad, shift_grad = norm_back(
            back, normed_ref[rows, :].astype(f32), scale_ref[rows, :], table[base : base + 1, :]
        )
        grad[rows, :] += grad_in
        vec_grad[0:1, :] += gain_grad
        vec_grad[1:2, :] += shift_grad

    steps_of(count, leave, tick, 1.5)


def diagonal_sums(block):
    size = block.shape[0]
    zeros = jnp.zeros((8, size), f32)
    total = None
    for g in range(size // 8):
        rows = jnp.concatenate([block[8 * g : 8 * g + 8, :], zeros], 1)
        if g:
            rows = pltpu.roll(rows, 2 * size - 8 * g, 1)
        total = rows if total is None else total + rows
    out = total[0:1, :]
    for i in range(1, 8):
        out = out + pltpu.roll(total, 2 * size - i, 1)[i : i + 1, :]
    return out


def mix_grads(value_ref, time_grad, kernel_grad, tick=idle):
    tiles, length, _ = value_ref.shape
    steps = length // TILE
    first = head_lanes()
    kernel_rows = []
    for j in range(tiles):
        sums = [[None] * steps for _ in range(2)]
        for d in range(steps):
            total = None
            for i in range(steps - d):
                value = value_ref[j, i * TILE : (i + 1) * TILE, :]
                split = jnp.concatenate(
                    [jnp.where(first, value, 0), jnp.where(first, 0, value)], 0
                ).astype(bf16)
                term = dot_nt(split, time_grad[j, (i + d) * TILE : (i + d + 1) * TILE, :])
                total = term if total is None else total + term
            for e in range(2):
                sums[e][d] = diagonal_sums(total[e * TILE : (e + 1) * TILE, :])
        for e in range(2):
            pieces = []
            for d in range(steps):
                piece = sums[e][d][:, :TILE]
                if d + 1 < steps:
                    piece = piece + sums[e][d + 1][:, TILE:]
                pieces.append(piece)
            kernel_rows.append(jnp.concatenate(pieces, 1))
        tick(1.0)
    kernel_grad[...] = jnp.concatenate(kernel_rows, 0)


def ssm_backward(
    count, table, weight_in, weight_out, wide_t, normed_ref, scale_ref, value_ref, swish_ref,
    side_ref, gated, grad, grad_in, grad_out, vec_grad, normal_ref, branch, time_grad, mixed_grad,
    tick=idle, start=None, ready=None,
):
    total_rows, width = grad.shape
    length = total_rows // count
    tiles = width // LANES
    steps = length // TILE
    vec_grad[...] = jnp.zeros_like(vec_grad)

    def enter(u):
        rows = at(u, length)
        lanes = at(u, LANES)
        low = grad[rows, :].astype(bf16)
        branch[rows, :] = low
        normed = normed_ref[rows, :].astype(f32)
        normal = (normed * table[SS : SS + 1, :] + table[SS + 1 : SS + 2, :]).astype(bf16)
        normal_ref[rows, :] = normal
        gated_grad = dot_nt(low, weight_out[...])
        for j in range(tiles):
            part = slice(j * LANES, (j + 1) * LANES)
            second = slice(width + j * LANES, width + (j + 1) * LANES)
            here = gated_grad[:, part]
            state_grad = here * swish_ref[j, :, lanes].astype(f32)
            time_grad[j, :, lanes] = state_grad.astype(bf16)
            mixed_grad[rows, second] = (here * side_ref[j, :, lanes].astype(f32)).astype(bf16)
            vec_grad[2:3, part] += jnp.sum(
                state_grad * value_ref[j, :, lanes].astype(f32), 0, keepdims=True
            )

    if tick is idle:
        loop(count, enter)
    else:
        enter(0)
        start()
        for u in range(1, count):
            enter(u)
            tick(1.0)
    grad_out[...] = dot_tn(gated[...], branch[...]).astype(bf16)
    if ready:
        ready(0)
    tick(0.9)
    first = head_lanes()
    for j in range(tiles):
        part = slice(j * LANES, (j + 1) * LANES)
        skip = table[SS + 2 : SS + 3, part]
        skip = jnp.concatenate([skip, skip], 1)
        for i in range(steps):
            rows = slice(i * TILE, (i + 1) * TILE)
            both = dot(wide_t[j, :, : length - i * TILE], time_grad[j, i * TILE :, :])
            back = jnp.where(first, both[:TILE], both[TILE:])
            back = (back + skip * time_grad[j, rows, :].astype(f32)).astype(bf16)
            for u in range(count):
                mixed_grad[u * length + i * TILE : u * length + (i + 1) * TILE, part] = back[
                    :, u * LANES : (u + 1) * LANES
                ]
        tick(0.6)
    grad_in[...] = dot_tn(normal_ref[...], mixed_grad[...]).astype(bf16)
    if ready:
        ready(1)
    tick(1.9)
    mixer_leave(
        count, table, SS, weight_in, normed_ref, scale_ref, grad, vec_grad, mixed_grad, tick
    )


def ffn1_backward(
    count, frames, grad, table, weight_in, weight_out, active, slope, frames_grad, grad_in,
    grad_out, vec_grad, normal_ref, branch, tick=idle, ready=None,
):
    total_rows, width = frames.shape
    length = total_rows // count
    blocks = weight_in.shape[1] // width
    vec_grad[...] = jnp.zeros_like(vec_grad)

    def enter(u):
        rows = at(u, length)
        normed, _ = norm(frames[rows, :].astype(f32))
        normal = (normed * table[F1 : F1 + 1, :] + table[F1 + 1 : F1 + 2, :]).astype(bf16)
        normal_ref[rows, :] = normal
        low = (0.5 * grad[rows, :]).astype(bf16)
        branch[rows, :] = low
        vec_grad[2 + blocks : 3 + blocks, :] += jnp.sum(low.astype(f32), 0, keepdims=True)

    steps_of(count, enter, tick, 1.0)

    def leave(rows, value):
        normed, scale = norm(frames[rows, :].astype(f32))
        grad_in, gain_grad, shift_grad = norm_back(value, normed, scale, table[F1 : F1 + 1, :])
        frames_grad[rows, :] = (grad[rows, :] + grad_in).astype(bf16)
        vec_grad[0:1, :] += gain_grad
        vec_grad[1:2, :] += shift_grad

    ffn_backward(
        count, weight_in, weight_out, active, slope, branch, normal_ref, grad_in, grad_out,
        vec_grad, leave, tick, ready,
    )


def shape(dims, kind):
    return jax.ShapeDtypeStruct(dims, kind)


def call(kernel, outs, scratch, smem, *operands):
    whole = pl.BlockSpec(memory_space=pltpu.VMEM)
    scalars = pl.BlockSpec(memory_space=pltpu.SMEM)
    return pl.pallas_call(
        kernel,
        out_shape=outs,
        in_specs=[scalars if n in smem else whole for n in range(len(operands))],
        out_specs=[whole] * len(outs),
        scratch_shapes=[pltpu.VMEM(s.shape, s.dtype) for s in scratch],
        compiler_params=pltpu.CompilerParams(vmem_limit_bytes=VMEM_BYTES),
    )(*operands)


def bring(weight_in, weight_out):
    first, second = (
        lax.all_gather(weight_in, "fsdp", axis=1, tiled=True),
        lax.all_gather(weight_out, "fsdp", axis=1, tiled=True),
    )
    return (
        lax.all_gather(first, "dp", axis=0, tiled=True),
        lax.all_gather(second, "dp", axis=0, tiled=True),
    )


def send(grad):
    part = lax.psum_scatter(grad, "fsdp", scatter_dimension=1, tiled=True)
    return lax.psum_scatter(part, "dp", scatter_dimension=0, tiled=True).astype(f32)


class Place:
    def __init__(self):
        me, z = (lax.axis_index("dp"), lax.axis_index("fsdp"))
        y, x, core = (me // 4, me // 2 % 2, me % 2)
        self.me, self.z, self.depth, self.layers = (me, z, 8, 4)
        self.chip, self.core = (me // 2, core)
        self.across = me + 2 - 4 * x
        self.along = me + 4 - 8 * y
        self.corner = me + 6 - 4 * x - 8 * y
        self.twin = me + 1 - 2 * core
        self.mates = (me, self.across, self.along, self.corner)
        turn = 1 - 2 * core
        self.twin_mates = tuple(mate + turn for mate in self.mates)

    def above(self, offset):
        return (self.z + offset) % self.layers

    def greet(self, everyone):
        barrier = pltpu.get_barrier_semaphore()
        others = [(self.me, self.above(o)) for o in range(1, self.layers)]
        if everyone:
            others += [((self.me + o) % self.depth, self.z) for o in range(1, self.depth)]
        else:
            others += [(mate, self.z) for mate in (self.across, self.along, self.twin)]
        for other in others:
            pl.semaphore_signal(
                barrier, inc=1, device_id=other, device_id_type=pl.DeviceIdType.MESH
            )
        return lambda: pl.semaphore_wait(barrier, len(others))


def copy_to(source, target, sems, slot, device):
    copy = pltpu.make_async_remote_copy(
        src_ref=source,
        dst_ref=target,
        send_sem=sems.at[0, slot],
        recv_sem=sems.at[1, slot],
        device_id=device,
        device_id_type=pl.DeviceIdType.MESH,
    )
    copy.start()
    return copy


TWIN, LAYER, LINE, LITTLE = range(4)
LATENCY = (1.4, 2.7, 2.7, 3.0)
SLACK = (1.5, 1.0)


class Turns:
    def __init__(self, slack=0.0):
        self.slack = slack
        self.pieces, self.begun, self.due = ([], [], [])
        self.now, self.free, self.open = (0.0, [0.0] * 4, [0.0] * 4)

    def add(self, piece, at_once=False):
        link, micros = piece[0][0][1:]
        self.pieces.append(piece)
        self.begun.append(0)
        self.due.append(max(self.now, self.open[link] - micros))
        self.open[link] = max(self.now, self.open[link]) + micros
        if at_once:
            self.step(len(self.pieces) - 1)
        self.settle()
        return len(self.pieces) - 1

    def step(self, n):
        action, link, micros = self.pieces[n][0][self.begun[n]]
        action()
        self.begun[n] += 1
        self.free[link] = max(self.now, self.free[link]) + micros
        self.due[n] = self.free[link] + LATENCY[link] + self.slack

    def live(self):
        return [n for n in range(len(self.pieces)) if not self.finished(n)]

    def settle(self):
        while True:
            due = [n for n in self.live() if self.due[n] <= self.now]
            if not due:
                return
            self.step(min(due, key=lambda n: (self.due[n], n)))

    def tick(self, micros):
        self.now += micros
        self.settle()

    def finished(self, n):
        return self.begun[n] == len(self.pieces[n][0])

    def run_until(self, *names):
        while not all(self.finished(n) for n in names):
            n = min(self.live(), key=lambda n: (self.due[n], n))
            self.now = max(self.now, self.due[n])
            self.step(n)

    def close(self):
        self.run_until(*range(len(self.pieces)))
        for _, copies in self.pieces:
            for copy in copies.values():
                copy.wait_send()


GATHER_SLOTS = 8
GATHER_RATES = (0.15, 0.07, 0.035, 0.03)


def gather_piece(spot, shard, whole, sems, begin, number):
    columns = shard.shape[1]
    half = number // 2
    copies = {}
    chip, core = (spot.chip, spot.core)
    lanes = at(spot.z, columns)

    def start(name, source, target, device):
        copies[name] = copy_to(source, target, sems, len(copies), device)

    def send_up():
        own = whole.at[chip, core, begin : begin + number, lanes]
        for o in range(1, spot.layers):
            start(("z", o), shard.at[begin : begin + number, :], own, (spot.me, spot.above(o)))
        whole[chip, core, begin : begin + number, lanes] = shard[begin : begin + number, :]

    def send_line():
        for o in range(1, spot.layers):
            copies["z", o].wait_recv()
        mine = whole.at[chip, core, begin : begin + number]
        start("across", mine, mine, (spot.across, spot.z))
        start("along", mine, mine, (spot.along, spot.z))

    def send_on():
        copies["across"].wait_recv()
        part = whole.at[spot.across // 2, core, begin : begin + half]
        start("corner along", part, part, (spot.along, spot.z))
        copies["along"].wait_recv()
        part = whole.at[spot.along // 2, core, begin + half : begin + number]
        start("corner across", part, part, (spot.across, spot.z))

    def send_twin():
        copies["corner along"].wait_recv()
        copies["corner across"].wait_recv()
        mine = whole.at[:, core, begin : begin + number]
        start("twin", mine, mine, (spot.twin, spot.z))

    def finish():
        copies["twin"].wait_recv()

    size = 1e-3 * number * columns * 2
    steps = [
        (send_up, LINE, GATHER_RATES[0] * size),
        (send_line, LAYER, GATHER_RATES[1] * size),
        (send_on, LAYER, GATHER_RATES[2] * size),
        (send_twin, TWIN, GATHER_RATES[3] * size),
        (finish, TWIN, 0.0),
    ]
    return (steps, copies)


def table_piece(spot, shard, whole, sems):
    columns = shard.shape[1]
    copies = {}

    def send_up():
        own = whole.at[:, at(spot.z, columns)]
        for o in range(1, spot.layers):
            copies[o] = copy_to(shard, own, sems, o - 1, (spot.me, spot.above(o)))
        whole[:, at(spot.z, columns)] = shard[...]

    def finish():
        for copy in copies.values():
            copy.wait_recv()

    return ([send_up, finish], copies)


def scatter_buffers(number, columns):
    return [
        shape((4, number, columns), bf16),
        shape((2, number // 2, columns), bf16),
        shape((2, number, columns), bf16),
        shape((3, number, columns // 4), bf16),
    ]


SCATTER_SLOTS = 11
SCATTER_RATES = (0.0008, 0.0013, 0.0026, 0.003)


def scatter_piece(spot, grad, keep, sums, corner, layer, lines, sems):
    number, columns = (grad.shape[0] // spot.depth, grad.shape[1])
    part = columns // spot.layers
    half = number // 2
    copies = {}

    def start(name, source, target, device):
        copies[name] = copy_to(source, target, sems, len(copies), device)

    def block(owner):
        return at(owner, number)

    def send_twin():
        for n in (3, 1, 2, 0):
            theirs = grad.at[block(spot.twin_mates[n]), :]
            start(("twin", n), theirs, sums.at[n], (spot.twin, spot.z))

    def add(target, first, size, one, other):
        sums[target, first : first + size, :] = one + other

    def send_corner():
        for n in (3, 1, 2, 0):
            copies["twin", n].wait_recv()
            add(n, 0, number, grad[block(spot.mates[n]), :], sums[n])
            if n == 3:
                start("along", sums.at[3, :half], corner.at[0], (spot.along, spot.z))
                start("across", sums.at[3, half:], corner.at[1], (spot.across, spot.z))

    def send_layer():
        copies["along"].wait_recv()
        add(1, 0, half, sums[1, :half, :], corner[0])
        start("own across", sums.at[1], layer.at[0], (spot.across, spot.z))
        copies["across"].wait_recv()
        add(2, half, half, sums[2, half:, :], corner[1])
        start("own along", sums.at[2], layer.at[1], (spot.along, spot.z))

    def send_up():
        copies["own across"].wait_recv()
        copies["own along"].wait_recv()
        total = sums[0].astype(f32) + layer[0].astype(f32) + layer[1].astype(f32)
        sums[0] = total.astype(bf16)
        for o in range(1, spot.layers):
            theirs = sums.at[0, :, at(spot.above(o), part)]
            start(("z", o), theirs, lines.at[o - 1], (spot.me, spot.above(o)))

    def finish():
        total = sums[0, :, at(spot.z, part)].astype(f32)
        for o in range(1, spot.layers):
            copies["z", o].wait_recv()
            total = total + lines[o - 1].astype(f32)
        keep(total)

    size = 1e-3 * 8 * number * columns * 2
    steps = [
        (send_twin, TWIN, SCATTER_RATES[0] * size),
        (send_corner, LAYER, SCATTER_RATES[1] * size),
        (send_layer, LAYER, SCATTER_RATES[2] * size),
        (send_up, LINE, SCATTER_RATES[3] * size),
        (finish, TWIN, 0.0),
    ]
    return (steps, copies)


SMALL_SLOTS = 13


def small_piece(spot, vectors, states, keep, lines, layers, sems):
    high = vectors.shape[0]
    columns = vectors.shape[1] // spot.layers
    copies = {}

    def start(source, target, device):
        copies[len(copies)] = copy_to(source, target, sems, len(copies), device)

    def send_up():
        for o in range(1, spot.layers):
            above = spot.above(o)
            start(vectors.at[:, at(above, columns)], lines.at[spot.z, :high], (spot.me, above))
            start(states, lines.at[spot.z, high:], (spot.me, above))
        lines[spot.z, :high, :] = vectors[:, at(spot.z, columns)]
        lines[spot.z, high:, :] = states[...]

    def send_layer():
        for n in range(2 * spot.layers - 2):
            copies[n].wait_recv()
        total = lines[0]
        for n in range(1, spot.layers):
            total = total + lines[n]
        layers[spot.me] = total
        own = layers.at[spot.me]
        for o in range(1, spot.depth):
            start(own, own, ((spot.me + o) % spot.depth, spot.z))

    def finish():
        for n in range(2 * spot.layers - 2, len(copies)):
            copies[n].wait_recv()
        total = layers[0]
        for n in range(1, spot.depth):
            total = total + layers[n]
        keep(total)

    steps = [(send_up, LITTLE, 0.0), (send_layer, LITTLE, 0.5), (finish, TWIN, 0.0)]
    return (steps, copies)


class Whole:
    def __init__(self, ref):
        chips, cores, rows, columns = ref.shape
        self.ref, self.block = (ref, cores * rows)
        self.shape = (chips * cores * rows, columns)

    def __getitem__(self, key):
        rows, columns = key if isinstance(key, tuple) else (slice(None), slice(None))
        if rows != slice(None):
            rows = slice(rows.start // self.block, rows.stop // self.block)
        value = self.ref[rows, :, :, columns]
        return value.reshape(-1, value.shape[-1])


class Refs:
    def __init__(self):
        self.copies, self.spilled = ({}, [])

    def later(self, *refs):
        return [Late(self, ref) for ref in refs]

    def fetch(self, *refs):
        return [late.start() for late in self.later(*refs)]

    def ready(self, *refs):
        for ref in refs:
            self.copies[id(ref)].wait()

    def spill(self, *refs):
        for ref in refs:
            self.copies[id(ref)].start()
            self.spilled.append(ref)


class Late:
    def __init__(self, r, ref):
        self.r, self.ref, self.here = (r, ref, False)
        self.shape, self.dtype = (ref.shape, ref.dtype)

    def start(self):
        self.r.copies[id(self.ref)].start()
        return self

    def land(self):
        if not self.here:
            self.r.ready(self.ref)
            self.here = True
        return self.ref

    def __getitem__(self, key):
        return self.land()[key]

    def __setitem__(self, key, value):
        self.land()[key] = value


NEAR, SCALAR, ANY, FAR = (pltpu.VMEM, pltpu.SMEM, pl.ANY, None)


def launch(body, inputs, outputs, scratch, collective=None, semaphores=None):
    operands = {**inputs, **outputs}
    names = list(operands)
    far = [name for name in names if operands[name][1] is FAR]
    semaphores = semaphores or {}

    def kernel(*refs):
        r = Refs()
        near = dict(zip(names, refs))
        rest = refs[len(names) :]
        buffers = dict(zip(far, rest))
        sems = rest[len(far)]
        rest = rest[len(far) + 1 :]
        for slot, name in enumerate(far):
            pair = (near[name], buffers[name])
            if name in outputs:
                pair = pair[::-1]
            r.copies[id(buffers[name])] = pltpu.make_async_copy(*pair, sems.at[slot])
        near.update(buffers)
        near.update(zip(list(scratch) + list(semaphores), rest))
        r.__dict__.update(near)
        body(r)
        r.ready(*r.spilled)

    def like(value):
        return pltpu.VMEM(value.shape, value.dtype)

    def specs(values):
        return [pl.BlockSpec(memory_space=ANY if p is FAR else p) for _, p in values.values()]

    results = pl.pallas_call(
        kernel,
        out_shape=[value for value, _ in outputs.values()],
        in_specs=specs(inputs),
        out_specs=specs(outputs),
        scratch_shapes=[like(operands[name][0]) for name in far]
        + [pltpu.SemaphoreType.DMA((max(1, len(far)),))]
        + [like(value) for value in scratch.values()]
        + [pltpu.SemaphoreType.DMA(dims) for dims in semaphores.values()],
        compiler_params=pltpu.CompilerParams(
            vmem_limit_bytes=VMEM_BYTES,
            collective_id=collective,
            has_side_effects=collective is not None,
        ),
    )(*[value for value, _ in inputs.values()])
    return dict(zip(outputs, results))


CUTS = (2, 2, 1, 1, 1, 1, 2, 2)
WEIGHTS = ("w1", "w2", "s1", "s2", "c1", "c2", "f1", "f2")


def under(prefix, values):
    return {prefix + str(n): value for n, value in enumerate(values)}


def held(r, prefix, number):
    return [r.__dict__[prefix + str(n)] for n in range(number)]


def scatter(r, spot, slot, name, keep):
    return scatter_piece(
        spot, r.__dict__[name], keep, *held(r, name + "_", 4), r.scatter_sems.at[slot]
    )


def piece_names(first):
    names = [first + "2" + str(q) for q in range(2)]
    return names + [first + "1" + str(half) + str(start) for half, start, _ in IN_PIECES]


def scatter_halves(r, spot, slot, first, turns, after=idle):
    ins, outs = (r.__dict__[first + "1_out"], r.__dict__[first + "2_out"])
    names = piece_names(first)
    plans = {first + "1" + str(half) + str(start): (half, start) for half, start, _ in IN_PIECES}

    def ready(n):
        if n == len(names):
            return after()
        name = names[n]

        def keep_out(total):
            q = int(name[-1])
            outs[q * LANES : (q + 1) * LANES, :] = total

        def keep_in(total):
            half, start = plans[name]
            for part in range(total.shape[1] // LANES):
                begin = (2 * (start + part) + half) * LANES
                ins[:, begin : begin + LANES] = total[:, part * LANES : (part + 1) * LANES]

        turns.add(scatter(r, spot, slot + n, name, keep_in if name in plans else keep_out))

    return ready


def half_pieces(width, hidden_width):
    half = hidden_width // 2
    ins = [shape((width, half // every), bf16) for _, _, every in IN_PIECES]
    return (ins, [shape((half, width), bf16)] * 2)


def half_scratch(first, width, hidden_width):
    ins, outs = half_pieces(width, hidden_width)
    scratch = {}
    for name in piece_names(first):
        grad = ins.pop(0) if name[1] == "1" else outs.pop(0)
        scratch[name] = grad
        scratch.update(under(name + "_", scatter_buffers(grad.shape[0] // 8, grad.shape[1])))
    return scratch


def half_refs(r, first):
    names = piece_names(first)
    ins = [r.__dict__[name] for name in names if name[1] == "1"]
    return (ins, [r.__dict__[name] for name in names if name[1] == "2"])


def fast_layer(frames, lengths, vectors, states_in, weights, cotangent):
    count, length, width = frames.shape
    rows = count * length
    tiles = width // LANES
    hidden_width = weights[0].shape[1] * 4
    heads, states = states_in[0].shape
    flat = frames.reshape(rows, width)
    row = shape((rows, width), bf16)
    row_f = shape((rows, width), f32)
    wide_row = shape((rows, hidden_width), bf16)
    scales = shape((rows, 1), f32)
    mixes = shape((tiles, length, count * LANES), bf16)
    band = shape((tiles, 2 * TILE, length), bf16)
    padded = shape((count * tiles, length + 2 * EDGE, LANES), f32)
    power = shape((4, heads * states, LANES), f32)
    whole_table = shape((TABLE, width), f32)
    bases = (F1, SS, CV, F2)
    decay, freq, real, imag = states_in

    def gathered(w):
        return shape((4, 2, w.shape[0], 4 * w.shape[1]), bf16)

    cuts = CUTS

    def forward(r):
        r.fetch(r.frames)
        spot = Place()
        greeted = spot.greet(False)
        r.shard[...] = jnp.zeros_like(r.shard)
        for ref, base in zip(held(r, "vec", 4), bases):
            r.shard[base : base + ref.shape[0], :] = ref[...].astype(f32)
        greeted()
        turns = Turns()
        place = {}
        for name, cut, shard in zip(WEIGHTS, cuts, held(r, "shard", 8)):
            size = shard.shape[0] // cut
            place[name] = []
            for q in range(cut):
                sems = r.gather_sems.at[len(turns.pieces)]
                piece = gather_piece(spot, shard, r.__dict__[name], sems, q * size, size)
                place[name].append(turns.add(piece))
        vector_steps, vector_copies = table_piece(spot, r.shard, r.table, r.table_sems)
        tick = turns.tick
        vector_steps[0]()
        build_bands(r.decay, r.freq, r.real, r.imag, r.powers, r.wide, r.wide_t, length, tick)
        r.spill(r.powers, r.wide_t)
        vector_steps[1]()

        def need(*wanted):
            for name in wanted:
                turns.run_until(*place[name])
                r.spill(r.__dict__[name])
            return [Whole(r.__dict__[name]) for name in wanted]

        first = need(*WEIGHTS[:2])
        r.ready(r.frames)
        ffn1_forward(
            count, r.frames, r.table, *first, r.hidden, r.w_active, r.w_slope, tick
        )
        r.spill(r.w_active, r.w_slope)
        mixer = need(*WEIGHTS[2:4])
        ssm_forward(
            count, r.hidden, r.table, *mixer, r.wide, r.s_normed, r.s_scale, r.s_value, r.s_swish,
            r.s_side, r.s_gated, tick,
        )
        r.spill(r.s_normed, r.s_scale, r.s_value, r.s_swish, r.s_side, r.s_gated)
        module = need(*WEIGHTS[4:6])
        conv_forward(
            count, r.hidden, r.lengths, r.table, *module, r.c_normed, r.c_scale, r.c_glu,
            r.c_gate, r.c_side, r.c_slope, r.c_active, r.glu, tick,
        )
        r.spill(r.hidden, r.c_normed, r.c_scale, r.c_glu, r.c_gate, r.c_side, r.c_slope, r.c_active)
        need(*WEIGHTS[6:])
        turns.close()
        for copy in vector_copies.values():
            copy.wait_send()

    saved = launch(
        forward,
        dict(
            frames=(flat, FAR), lengths=(lengths, SCALAR), decay=(decay, NEAR), freq=(freq, NEAR),
            real=(real, NEAR), imag=(imag, NEAR), **under("vec", [(v, NEAR) for v in vectors]),
            **under("shard", [(w, NEAR) for w in weights]),
        ),
        dict(
            table=(whole_table, NEAR), hidden=(row_f, FAR), w_active=(wide_row, FAR),
            w_slope=(wide_row, FAR), powers=(power, FAR), wide_t=(band, FAR), s_normed=(row, FAR),
            s_scale=(scales, FAR), s_value=(mixes, FAR), s_swish=(mixes, FAR), s_side=(mixes, FAR),
            s_gated=(row, FAR), c_normed=(row, FAR), c_scale=(scales, FAR), c_glu=(row, FAR),
            c_gate=(row, FAR), c_side=(row, FAR), c_slope=(row, FAR), c_active=(row, FAR),
            **{name: (gathered(w), FAR) for name, w in zip(WEIGHTS, weights)},
        ),
        dict(shard=shape((TABLE, LANES), f32), wide=band, glu=padded),
        0,
        dict(gather_sems=(sum(cuts), 2, GATHER_SLOTS), table_sems=(2, 3)),
    )
    shards = {}
    for name, w in zip(WEIGHTS, weights):
        saved[name] = saved[name].reshape(8 * w.shape[0], 4 * w.shape[1])
        shards[name + "_out"] = (shape(w.shape, f32), NEAR)
    kept = {name: (value, FAR) for name, value in saved.items()}
    table = (saved["table"], NEAR)

    def some(values, *prefixes):
        return {name: value for name, value in values.items() if name.startswith(prefixes)}

    half_width = hidden_width // 2
    square, double = (shape((width, width), bf16), shape((width, 2 * width), bf16))
    half_row = shape((rows, half_width), bf16)

    def later(r):
        spot = Place()
        greeted = spot.greet(False)
        hidden, f1, f2, cot = r.fetch(r.hidden, r.f1, r.f2, r.cot)
        conv_in = r.later(
            r.c2, r.c_normed, r.c_scale, r.c_glu, r.c_gate, r.c_side, r.c_slope, r.c_active, r.c1
        )

        def start():
            greeted()
            for late in conv_in:
                late.start()

        turns = Turns(SLACK[0])
        tick = turns.tick
        ffn2_both(
            count, hidden, cot, r.lengths, r.table, f1, f2, cot, hidden, *half_refs(r, "f"),
            r.f_vec, r.normed, r.scale, r.active, r.slope, r.normal, r.branch, tick,
            scatter_halves(r, spot, 0, "f", turns), start,
        )
        save_output = pltpu.make_async_copy(r.cot, r.output, r.save_sems.at[1])
        save_output.start()
        c2, *kept_in, c1 = [late.land() for late in conv_in]
        conv_backward(
            count, r.table, c1, c2, *kept_in, r.hidden, r.c1_grad, r.c2_grad, r.c_vec, r.normal,
            r.branch, r.depth_grad, r.tap_grads, r.active.at[:, : 2 * width], tick,
        )
        r.spill(r.c1_grad, r.c2_grad)
        save = pltpu.make_async_copy(r.hidden, r.grad, r.save_sems.at[0])
        save.start()
        turns.close()
        save.wait()
        save_output.wait()

    two = launch(
        later,
        dict(
            cot=(cotangent.reshape(rows, width), FAR), lengths=(lengths, SCALAR), table=table,
            **some(kept, "hidden", "f", "c"),
        ),
        dict(
            output=(row, ANY), grad=(row_f, ANY), c1_grad=(double, FAR), c2_grad=(square, FAR),
            f_vec=(shape((TABLE - F2, width), f32), NEAR),
            c_vec=(shape((F2 - CV, width), f32), NEAR), **some(shards, "f"),
        ),
        dict(
            normed=row, scale=scales, active=wide_row, slope=wide_row, normal=row, branch=row,
            depth_grad=padded, tap_grads=shape((CONV_TAPS, 8, LANES), f32),
            **half_scratch("f", width, hidden_width),
        ),
        1,
        dict(scatter_sems=(5, 2, SCATTER_SLOTS), save_sems=(2,)),
    )

    def last(r):
        spot = Place()
        greeted = spot.greet(True)
        grad, s2, *kept_in = r.fetch(
            r.grad, r.s2, r.s_normed, r.s_scale, r.s_value, r.s_swish, r.s_side
        )
        sent = r.fetch(r.c1g, r.c2g)
        wide_t, gated, s1, frames, w2, slope, active, w1, powers = r.later(
            r.wide_t, r.s_gated, r.s1, r.frames, r.w2, r.w_slope, r.w_active, r.w1, r.powers
        )
        r.vectors[...] = jnp.zeros_like(r.vectors)
        r.vectors[CV:F2, :] = r.c_vec[...]
        r.vectors[F2:, :] = r.f_vec[...]
        turns = Turns(SLACK[1])
        tick = turns.tick

        def send(name, slot, out):
            def keep(total):
                out[...] = total

            turns.add(scatter(r, spot, slot, name, keep))

        def start():
            for late in (wide_t, gated, s1, frames, w2, slope, active, w1, powers):
                late.start()
            for late in sent:
                late.land()
            greeted()
            send("c1g", 0, r.c1_out)
            send("c2g", 1, r.c2_out)

        def ready(n):
            send(*(("s1g", 2, r.s1_out) if n else ("s2g", 3, r.s2_out)))

        ssm_backward(
            count, r.table, s1, s2, wide_t, *kept_in, gated, grad, r.s1g, r.s2g,
            r.vectors.at[SS:CV], r.normal, r.branch, r.time_grad, r.mixed, tick, start,
            ready,
        )

        def after():
            mix_grads(r.s_value, r.time_grad, r.kernel_grad, tick)
            state_grads(r.kernel_grad[...], powers, r.decay, r.real, r.imag, r.states)
            tick(2.0)

        ffn1_backward(
            count, frames, r.grad, r.table, w1, w2, active, slope, r.normal, *half_refs(r, "w"),
            r.vectors.at[F1:SS], r.normal, r.branch, tick,
            scatter_halves(r, spot, 4, "w", turns, after),
        )
        save = pltpu.make_async_copy(r.normal, r.frames_grad, r.save_sems.at[0])
        save.start()

        def keep(total):
            r.small[...] = total

        turns.add(
            small_piece(spot, r.vectors, r.states, keep, r.lines, r.layers, r.small_sems), True
        )
        turns.close()
        save.wait()

    small = shape((TABLE + 4 * heads, LANES), f32)
    sent = dict(c1g=double, c2g=square, s1g=double, s2g=square)
    arriving = {}
    for name, grad in sent.items():
        arriving.update(under(name + "_", scatter_buffers(grad.shape[0] // 8, grad.shape[1])))
    three = launch(
        last,
        dict(
            frames=(flat, FAR), grad=(two["grad"], FAR), c1g=(two["c1_grad"], FAR),
            c2g=(two["c2_grad"], FAR), table=table, c_vec=(two["c_vec"], NEAR),
            f_vec=(two["f_vec"], NEAR), decay=(decay, NEAR), real=(real, NEAR), imag=(imag, NEAR),
            **some(kept, "s", "w", "powers"),
        ),
        dict(frames_grad=(row, ANY), small=(small, NEAR), **some(shards, "w", "s", "c")),
        dict(
            s1g=double, s2g=square, states=shape((4 * heads, LANES), f32), normal=row, branch=row,
            mixed=half_row, time_grad=mixes, vectors=whole_table,
            kernel_grad=shape((heads, length), f32), lines=shape((4,) + small.shape, f32),
            layers=shape((8,) + small.shape, f32), **half_scratch("w", width, hidden_width),
            **arriving,
        ),
        2,
        dict(
            scatter_sems=(9, 2, SCATTER_SLOTS), small_sems=(2, SMALL_SLOTS), save_sems=(1,)
        ),
    )

    done = [(two if name[0] == "f" else three)[name + "_out"] for name in WEIGHTS]

    def finish(r):
        for target, value in zip(held(r, "out", 8), held(r, "in", 8)):
            target[...] = value[...]
        for base, target in zip(bases, held(r, "vec", 4)):
            target[...] = r.small[base : base + target.shape[0], :]
        for n, target in enumerate(held(r, "st", 4)):
            begin = TABLE + n * heads
            target[...] = r.small[begin : begin + heads, :states]
        r.frames_end[...] = r.frames_grad[...]

    end = launch(
        finish,
        dict(
            small=(three["small"], NEAR), frames_grad=(three["frames_grad"], NEAR),
            **under("in", [(value, NEAR) for value in done]),
        ),
        dict(
            frames_end=(row, NEAR),
            **under("out", [(shape(value.shape, f32), NEAR) for value in done]),
            **under("vec", [(shape(v.shape, f32), NEAR) for v in vectors]),
            **under("st", [(shape((heads, states), f32), NEAR)] * 4),
        ),
        {},
    )
    frames_end, *outs = end.values()
    vec, state_grads_out = (outs[8:12], outs[12:])
    return (
        (two["output"].reshape(frames.shape), frames_end.reshape(frames.shape))
        + (outs[0], outs[1], vec[0], outs[2], outs[3], vec[1])
        + tuple(state_grads_out)
        + (outs[4], outs[5], vec[2], outs[6], outs[7], vec[3])
    )


def body(
    frames,
    lengths,
    ffn1_in,
    ffn1_out,
    ffn1_vec,
    ssm_in,
    ssm_out,
    ssm_vec,
    decay,
    freq,
    coef_re,
    coef_im,
    conv_in,
    conv_out,
    conv_vec,
    ffn2_in,
    ffn2_out,
    ffn2_vec,
    cotangent,
):
    count, length, width = frames.shape
    rows = count * length
    tiles = width // LANES
    hidden_width = width * (ffn1_vec.shape[0] - 3)
    heads, states = decay.shape
    flat = frames.reshape(rows, width)

    vectors = (ffn1_vec, ssm_vec, conv_vec, ffn2_vec)
    states_in = (decay, freq, coef_re, coef_im)
    weights = (ffn1_in, ffn1_out, ssm_in, ssm_out, conv_in, conv_out, ffn2_in, ffn2_out)
    if (lax.axis_size("dp"), lax.axis_size("fsdp")) == (8, 4):
        return fast_layer(frames, lengths, vectors, states_in, weights, cotangent)

    def pad(vec, to):
        return jnp.pad(vec.astype(f32), ((0, to - vec.shape[0]), (0, 0)))

    table = jnp.concatenate(
        [pad(ffn1_vec, SS - F1), pad(ssm_vec, CV - SS), pad(conv_vec, F2 - CV), pad(ffn2_vec, TABLE - F2)], 0
    )
    table = lax.all_gather(table, "fsdp", axis=1, tiled=True)
    weights = [whole for n in range(0, 8, 2) for whole in bring(weights[n], weights[n + 1])]
    first_in, first_out, mixer_in, mixer_out = weights[:4]
    module_in, module_out, second_in, second_out = weights[4:]

    row = shape((rows, width), bf16)
    row_f = shape((rows, width), f32)
    wide_row = shape((rows, hidden_width), bf16)
    scales = shape((rows, 1), f32)
    mixes = shape((tiles, length, count * LANES), bf16)
    band = shape((tiles, 2 * TILE, length), bf16)
    padded = shape((count * tiles, length + 2 * EDGE, LANES), f32)
    square = shape((width, width), bf16)
    double = shape((width, 2 * width), bf16)
    half_row = shape((rows, hidden_width // 2), bf16)
    power = shape((4, heads * states, LANES), f32)

    hidden, first_active, first_slope = call(
        partial(ffn1_forward, count), [row_f, wide_row, wide_row], [], (), flat, table, first_in,
        first_out,
    )

    def mixer_kernel(
        hidden_in, table, weight_in, weight_out, decay, freq, re, im, hidden, normed, scale, value,
        swish, side, gated, powers, wide_t, wide,
    ):
        hidden[...] = hidden_in[...]
        build_bands(decay, freq, re, im, powers, wide, wide_t, length)
        ssm_forward(
            count, hidden, table, weight_in, weight_out, wide, normed, scale, value, swish, side,
            gated,
        )

    hidden, *mixer_kept, powers, wide_t = call(
        mixer_kernel, [row_f, row, scales, mixes, mixes, mixes, row, power, band], [band],
        (), hidden, table, mixer_in, mixer_out, decay, freq, coef_re, coef_im,
    )

    def module_kernel(hidden_in, lengths, table, weight_in, weight_out, hidden, *rest):
        hidden[...] = hidden_in[...]
        conv_forward(count, hidden, lengths, table, weight_in, weight_out, *rest)

    hidden, *module_kept = call(
        module_kernel, [row_f, row, scales, row, row, row, row, row], [padded], (1,), hidden,
        lengths, table, module_in, module_out,
    )

    ins, outs = half_pieces(width, hidden_width)
    number = len(ins)

    def second_kernel(hidden, cot, lengths, table, w_in, w_out, output, grad, *rest):
        ffn2_both(
            count, hidden, cot, lengths, table, w_in, w_out, output, grad, rest[:number],
            rest[number : number + 2], *rest[number + 2 :],
        )

    output, grad, *second_grads, second_vec = call(
        second_kernel,
        [row, row_f, *ins, *outs, shape((TABLE - F2, width), f32)],
        [row, scales, wide_row, wide_row, row, row],
        (2,), hidden, cotangent.reshape(rows, width), lengths, table, second_in, second_out,
    )

    def module_back(grad_in, table, *rest):
        kept, rest = (rest[: 2 + len(module_kept)], rest[2 + len(module_kept) :])
        rest[0][...] = grad_in[...]
        conv_backward(count, table, *kept, *rest)

    grad, module_in_grad, module_out_grad, module_vec = call(
        module_back,
        [row_f, double, square, shape((F2 - CV, width), f32)],
        [
            row, row, padded, shape((CONV_TAPS, 8, LANES), f32),
            shape((rows, 2 * width), bf16),
        ],
        (), grad, table, module_in, module_out, *module_kept,
    )

    def mixer_back(
        grad_in, table, w_in, w_out, wide_t, powers, decay, re, im, normed, scale, value, swish,
        side, gated, grad, in_grad, out_grad, vec_grad, states, *rest,
    ):
        grad[...] = grad_in[...]
        ssm_backward(
            count, table, w_in, w_out, wide_t, normed, scale, value, swish, side, gated, grad,
            in_grad, out_grad, vec_grad, *rest[1:],
        )
        mix_grads(value, rest[3], rest[0])
        state_grads(rest[0][...], powers, decay, re, im, states)

    grad, mixer_in_grad, mixer_out_grad, mixer_vec, state_grad = call(
        mixer_back,
        [row_f, double, square, shape((CV - SS, width), f32), shape((4 * heads, LANES), f32)],
        [
            shape((heads, length), f32), row, row, mixes, shape((rows, 2 * width), bf16),
        ],
        (), grad, table, mixer_in, mixer_out, wide_t, powers, decay, coef_re, coef_im,
        *mixer_kept,
    )

    def first_back(frames, grad, table, w_in, w_out, active, kept, out, *rest):
        *rest, slope = rest
        slope[...] = kept[...]
        ffn1_backward(
            count, frames, grad, table, w_in, w_out, active, slope, out, rest[:number],
            rest[number : number + 2], *rest[number + 2 :],
        )

    frames_grad, *first_grads, first_vec = call(
        first_back,
        [row, *ins, *outs, shape((SS - F1, width), f32)],
        [row, row, wide_row],
        (), flat, grad, table, first_in, first_out, first_active, first_slope,
    )
    vec_grads = jnp.concatenate([first_vec, mixer_vec, module_vec, second_vec], 0)

    def join(in_a, *parts):
        wide = [part.reshape(width, -1, LANES) for part in (in_a,) + parts[:2]]
        wide = [wide[0], jnp.stack(wide[1:], 2).reshape(width, -1, LANES)]
        tall = [part.reshape(-1, LANES, width) for part in parts[2:]]
        return (
            jnp.stack(wide, 2).reshape(width, hidden_width),
            jnp.stack(tall, 1).reshape(hidden_width, width),
        )

    grads = (
        *join(*first_grads), mixer_in_grad, mixer_out_grad, module_in_grad, module_out_grad,
        *join(*second_grads),
    )
    vec_grads = lax.psum(
        lax.psum_scatter(vec_grads, "fsdp", scatter_dimension=1, tiled=True), "dp"
    )
    state_grad = lax.psum(state_grad, ("dp", "fsdp"))
    grads = [send(grad) for grad in grads]
    state_grad = state_grad[:, :states].reshape(4, heads, states)

    def layer(number, base, like):
        return (grads[number], grads[number + 1], vec_grads[base : base + like.shape[0]])

    return (
        (output.reshape(count, length, width), frames_grad.reshape(count, length, width))
        + layer(0, F1, ffn1_vec)
        + layer(2, SS, ssm_vec)
        + tuple(state_grad[n] for n in range(4))
        + layer(4, CV, conv_vec)
        + layer(6, F2, ffn2_vec)
    )


def solution(mesh):
    split = P(("dp", "fsdp"), None, None)
    weight = P("dp", "fsdp")
    vector = P(None, "fsdp")
    layer = (weight, weight, vector)
    whole = (P(), P(), P(), P())
    in_specs = (split, P(("dp", "fsdp"))) + layer + layer + whole + layer + layer + (split,)
    out_specs = (split, split) + layer + layer + whole + layer + layer
    return jax.shard_map(body, mesh=mesh, in_specs=in_specs, out_specs=out_specs, check_vma=False)
```
